32 devices in a mesh: frames: 8 (over y, x, core), space: 4 (over z).
Axes of the slice: x: 2, y: 2, z: 4, core: 2. Of those that a mesh axis runs over, the one named last changes fastest.
Arguments:
- latents: bfloat16 [8, 1792, 1152], P('frames', 'space'), may hold values from -6 to 6
- merge_slot: int32 [8, 1792], P('frames', 'space'), may hold values from 0 to 895, as said below
- modulation: float32 [6, 1152], replicated, may hold values from -3 to 3
- spatial_qkv: bfloat16 [1152, 1728], replicated, may hold values from -0.41247896 to 0.41247896
- spatial_proj: bfloat16 [576, 1152], replicated, may hold values from -0.25 to 0.25
- temporal_qkv: bfloat16 [1152, 1728], replicated, may hold values from -0.41247896 to 0.41247896
- temporal_proj: bfloat16 [576, 1152], replicated, may hold values from -0.25 to 0.25
Outputs:
- block_out: bfloat16 [8, 1792, 1152], P('frames', 'space')
The draws below stay inside these ranges and needn't reach their ends.
Inputs may be any that keep to these rules, and one draw needn't show every extreme that they name: `merge_slot`: within each frame, the tokens of the k-th aligned block of 448 tokens join merged tokens k * 224 to (k + 1) * 224 - 1 only, and every merged token is joined by at least one token.
All inputs are finite; a program needn't handle non-finite values.
Results may differ from the reference program's by a relative error of at most 0.0062.
Values may be sent and summed in bfloat16 or wider, within the bound.
No kernel may reach another device: no remote copies, remote signals or barrier semaphores. Data moves between devices by JAX's collectives and lax.ppermute only.
A program may use at most 128 MiB of HBM per device.

```python
import math
import jax
import jax.numpy as jnp
from jax import lax

D = 1152
HEADS = 8
HD = 72
ROWS = 448
INNER = 576
FRAMES = 8
TOK = 1792
HALF = 896
MROWS = 224


def draw_projection(key, fan_rows, inner):
    base_key = jax.random.fold_in(key, 0)
    return jnp.clip(jax.random.normal(base_key, (fan_rows, 3 * inner), jnp.float32), -4.0, 4.0) / math.sqrt(fan_rows)


def draw_spatial_qkv(key, part):
    return draw_projection(jax.random.fold_in(key, 11), D, INNER).astype(jnp.bfloat16)


def draw_temporal_qkv(key, part):
    return draw_projection(jax.random.fold_in(key, 23), D, INNER).astype(jnp.bfloat16)


def draw_merge_slot(key, part):
    block_count = FRAMES * (TOK // ROWS)
    keys_all = jax.random.split(key, block_count)

    def one_block(block_key):
        order_key, extra_key = jax.random.split(block_key)
        order = jax.random.permutation(order_key, ROWS)
        extra = jax.random.randint(extra_key, (ROWS,), 0, MROWS)
        ranks = jnp.arange(ROWS, dtype=jnp.int32)
        slot_of_rank = jnp.where(ranks < MROWS, ranks, extra).astype(jnp.int32)
        return jnp.zeros((ROWS,), jnp.int32).at[order].set(slot_of_rank)
    local = jax.vmap(one_block)(keys_all).reshape(FRAMES, TOK // ROWS, ROWS)
    offsets = (jnp.arange(TOK // ROWS, dtype=jnp.int32) * MROWS)[None, :, None]
    return (local + offsets).reshape(FRAMES, TOK).astype(jnp.int32)


def steps_of(stream_key, extent, cuts, low, high):
    level = 1.0
    for axis_at, shards_of in cuts:
        heights = jax.random.uniform(jax.random.fold_in(jax.random.fold_in(stream_key, 6), axis_at), (shards_of,), jnp.float32, low / len(cuts), high / len(cuts))
        level = level * jnp.repeat(jnp.exp(heights), extent[axis_at] // shards_of).reshape((-1,) + (1,) * (len(extent) - 1 - axis_at))
    return level


def gaussian(own_key, extent, deviation, bound, cuts=(), kind=jnp.bfloat16):
    drawn = jax.random.normal(own_key, extent, jnp.float32) * deviation
    if len(cuts) > 0:
        drawn = steps_of(own_key, extent, cuts, -0.22, 0.18) * drawn
    return jnp.clip(drawn, min=-bound, max=bound).astype(kind)


def setup_inputs(seed: int = 0) -> dict:
    key_of = jax.random.split(jax.random.key(seed), 8)
    return {
        "latents": gaussian(key_of[0], (FRAMES, TOK, D), 1.0, 6.0, ((0, 8), (1, 4))),
        "merge_slot": draw_merge_slot(jax.random.fold_in(key_of[7], 71), 0),
        "modulation": gaussian(key_of[2], (6, D), 0.5, 3.0, (), jnp.float32),
        "spatial_qkv": draw_spatial_qkv(jax.random.fold_in(key_of[7], 71), 0),
        "spatial_proj": gaussian(key_of[4], (INNER, D), INNER ** -0.5, 0.25),
        "temporal_qkv": draw_temporal_qkv(jax.random.fold_in(key_of[7], 71), 0),
        "temporal_proj": gaussian(key_of[6], (INNER, D), INNER ** -0.5, 0.25),
    }


def layer_norm(values):
    values = values.astype(jnp.float32)
    center = values - lax.optimization_barrier(jnp.mean(values, -1, keepdims=True))
    spread = lax.optimization_barrier(jnp.mean(center * center, -1, keepdims=True))
    return center * lax.rsqrt(spread + 1e-06)

def modulate(values, modulation, which):
    return (layer_norm(values) * (1.0 + modulation[which + 1]) + modulation[which]).astype(jnp.bfloat16)

def head_attention(operands):
    query_rows, key_rows, value_rows = operands
    scores = jnp.dot(query_rows, key_rows.T, preferred_element_type=jnp.float32) / math.sqrt(HD)
    weights = jnp.exp(scores - lax.optimization_barrier(jnp.max(scores, -1, keepdims=True)))
    row_total = lax.optimization_barrier(jnp.sum(weights, -1, keepdims=True))
    mixture = jnp.dot(weights.astype(jnp.bfloat16), value_rows, preferred_element_type=jnp.float32)
    return (mixture / row_total).astype(jnp.bfloat16)

def by_heads(block):
    return block.reshape(block.shape[0], HEADS, HD).transpose(1, 0, 2)

def reference(latents, merge_slot, modulation, spatial_qkv, spatial_proj, temporal_qkv, temporal_proj):

    def spatial_frame(operands):
        frame_rows, frame_slots = operands
        normed = modulate(frame_rows, modulation, 0)
        one_hot = (frame_slots[:, None] == jnp.arange(HALF, dtype=jnp.int32)[None, :]).astype(jnp.bfloat16)
        counts = lax.optimization_barrier(jnp.sum(one_hot.astype(jnp.float32), 0))
        summed = jnp.dot(one_hot.T, normed, preferred_element_type=jnp.float32)
        merged = (summed / counts[:, None]).astype(jnp.bfloat16)
        projected = jnp.dot(merged, spatial_qkv, preferred_element_type=jnp.float32).astype(jnp.bfloat16)
        heads_out = lax.map(head_attention, (by_heads(projected[:, :INNER]), by_heads(projected[:, INNER:2 * INNER]), by_heads(projected[:, 2 * INNER:])))
        attended = heads_out.transpose(1, 0, 2).reshape(HALF, INNER)
        spatial_out = jnp.dot(attended, spatial_proj, preferred_element_type=jnp.float32).astype(jnp.bfloat16)
        spread_back = jnp.dot(one_hot, spatial_out, preferred_element_type=jnp.float32)
        return (frame_rows.astype(jnp.float32) + modulation[2] * spread_back).astype(jnp.bfloat16)
    after_spatial = lax.map(spatial_frame, (latents, merge_slot))
    by_place = after_spatial.transpose(1, 0, 2).reshape(TOK // ROWS, ROWS, FRAMES, D)

    def temporal_block(block):
        flat = block.reshape(ROWS * FRAMES, D)
        normed = modulate(flat, modulation, 3)
        projected = jnp.dot(normed, temporal_qkv, preferred_element_type=jnp.float32).astype(jnp.bfloat16)
        split = projected.reshape(ROWS, FRAMES, 3, HEADS, HD).astype(jnp.float32)
        scores = jnp.einsum('pfhd,pghd->phfg', split[:, :, 0], split[:, :, 1]) / math.sqrt(HD)
        weights = jnp.exp(scores - lax.optimization_barrier(jnp.max(scores, -1, keepdims=True)))
        row_total = lax.optimization_barrier(jnp.sum(weights, -1))
        rounded = lax.optimization_barrier(weights.astype(jnp.bfloat16)).astype(jnp.float32)
        mixture = jnp.einsum('phfg,pghd->pfhd', rounded, split[:, :, 2]) / row_total.transpose(0, 2, 1)[..., None]
        attended = mixture.astype(jnp.bfloat16).reshape(ROWS * FRAMES, INNER)
        branch = jnp.dot(attended, temporal_proj, preferred_element_type=jnp.float32)
        return (flat.astype(jnp.float32) + modulation[5] * branch).astype(jnp.bfloat16).reshape(ROWS, FRAMES, D)
    finished = lax.map(temporal_block, by_place)
    return finished.reshape(TOK, FRAMES, D).transpose(1, 0, 2)
```

```python
import functools
import math

import jax
import jax.numpy as jnp
from jax import lax
from jax.experimental import pallas as pl
from jax.experimental.pallas import tpu as pltpu
from jax.sharding import PartitionSpec as P

HD = 72
LANES = 128
SUB = 16
F32 = jnp.float32
BF16 = jnp.bfloat16
VMEM = pl.BlockSpec(memory_space=pltpu.VMEM)
ANY = pl.BlockSpec(memory_space=pl.ANY)
MIB = 1 << 20


def struct(*shape):
    return jax.ShapeDtypeStruct(shape, BF16)


def params(mib):
    return pltpu.CompilerParams(vmem_limit_bytes=mib * MIB)


def layer_norm(values):
    center = values - jnp.mean(values, -1, keepdims=True)
    spread = jnp.mean(center * center, -1, keepdims=True)
    return center * lax.rsqrt(spread + 1e-06)


def dot(left, right):
    return jnp.dot(left, right, preferred_element_type=F32)


def packing(rows, width):
    full, rest = divmod(width, LANES)
    groups = 1
    if rest:
        units = rows // SUB
        groups = max([g for g in range(1, units + 1) if units % g == 0 and g * rest <= LANES and rows % SUB == 0] or [1])
    return full, rest, groups


def packed_rows(rows, width):
    full, rest, groups = packing(rows, width)
    return full * rows + (rows // groups if rest else 0)


def pack(block):
    rows, width = block.shape
    full, rest, groups = packing(rows, width)
    parts = [block[:, j * LANES : (j + 1) * LANES] for j in range(full)]
    if rest:
        high = rows // groups
        tail = block[:, full * LANES :]
        pieces = [tail[i * high : (i + 1) * high] for i in range(groups)]
        if groups * rest < LANES:
            pieces.append(jnp.zeros((high, LANES - groups * rest), block.dtype))
        parts.append(jnp.concatenate(pieces, 1))
    return jnp.concatenate(parts, 0)


def unpack(packed, rows, width):
    full, rest, groups = packing(rows, width)
    parts = [packed[j * rows : (j + 1) * rows] for j in range(full)]
    if rest:
        high = rows // groups
        tail = packed[full * rows : full * rows + high]
        pieces = [tail[:, i * rest : (i + 1) * rest] for i in range(groups)]
        parts.append(jnp.concatenate(pieces, 0))
    return jnp.concatenate(parts, 1)


def merge_kernel(n_space, latents, slot, modulation, weights, *refs):
    outs, (held, arrived, sem) = refs[:n_space], refs[n_space:]
    copy = pltpu.make_async_copy(weights, arrived, sem)
    copy.start()
    me = lax.axis_index("space")
    rows, slots = latents.shape[0], latents.shape[0] // 2
    inner = weights.shape[1] // 3
    wide = inner // n_space
    values = layer_norm(latents[...].astype(F32))
    normed = (values * (1.0 + modulation[1:2]) + modulation[0:1]).astype(BF16)
    local = slot[...] - me * slots
    chosen = lax.broadcasted_iota(jnp.int32, (slots, rows), 0) == local
    counts = jnp.sum(chosen.astype(F32), 1, keepdims=True)
    merged = (dot(chosen.astype(BF16), normed) / counts).astype(BF16)
    copy.wait()
    projected = dot(merged, arrived[...]).astype(BF16)
    for d in range(n_space):
        held[d] = pack(
            jnp.concatenate([projected[:, j * inner + d * wide : j * inner + (d + 1) * wide] for j in range(3)], 1)
        )
    for s in range(n_space):
        outs[s][...] = held[me ^ s]


def attention_kernel(n_space, slots, wide, *refs):
    ins, outs = refs[:n_space], refs[n_space:]
    blocks = [unpack(r[...], slots, 3 * wide) for r in ins]
    results = [[] for _ in range(n_space)]
    for h in range(wide // HD):
        keys = jnp.concatenate([b[:, wide + h * HD : wide + (h + 1) * HD] for b in blocks], 0)
        vals = jnp.concatenate([b[:, 2 * wide + h * HD : 2 * wide + (h + 1) * HD] for b in blocks], 0)
        vals = jnp.concatenate([vals, jnp.ones((vals.shape[0], LANES - HD), BF16)], 1)
        for s in range(n_space):
            query = blocks[s][:, h * HD : (h + 1) * HD]
            scores = lax.dot_general(query, keys, (((1,), (1,)), ((), ())), preferred_element_type=F32)
            top = jnp.max(scores, -1, keepdims=True)
            weights = jnp.exp((scores - top) * (1.0 / math.sqrt(HD)))
            mixed = dot(weights.astype(BF16), vals)
            results[s].append((mixed[:, :HD] / mixed[:, HD : HD + 1]).astype(BF16))
    for s in range(n_space):
        outs[s][...] = pack(jnp.concatenate(results[s], 1))


def expand_kernel(n_space, n_pair, slots, wide, slot, *refs):
    ins, (keep, give, attended, held, spread) = refs[:n_space], refs[n_space:]
    me, frame = lax.axis_index("space"), lax.axis_index("frames")
    for s in range(n_space):
        held[me ^ s] = unpack(ins[s][...], slots, wide)
    whole = jnp.concatenate([held[d] for d in range(n_space)], 1)
    attended[...] = whole
    local = slot[...] - me * slots
    rows = slot.shape[0]
    chosen = (lax.broadcasted_iota(jnp.int32, (rows, slots), 1) == local).astype(BF16)
    wanted = dot(chosen, whole)
    places = keep.shape[1]
    for f in range(2 * n_pair):
        spread[f] = wanted[f * places : (f + 1) * places].astype(BF16)
    for s in range(n_pair):
        keep[s] = spread[frame ^ (2 * s)]
        give[s] = spread[frame ^ (2 * s + 1)]


def share_kernel(n_pair, latents, keep, give):
    frame = lax.axis_index("frames")
    for s in range(n_pair):
        keep[s] = latents[frame ^ (2 * s)]
        give[s] = latents[frame ^ (2 * s + 1)]


def residual_kernel(attended, slot, latents, modulation, proj, after):
    me = lax.axis_index("space")
    slots, rows = attended.shape[0], slot.shape[0]
    places = latents.shape[1]
    out = dot(attended[...], proj[...]).astype(BF16)
    local = slot[...] - me * slots
    chosen = (lax.broadcasted_iota(jnp.int32, (rows, slots), 1) == local).astype(BF16)
    spread = modulation[2:3] * dot(chosen, out)
    for f in range(latents.shape[0]):
        after[f] = (latents[f].astype(F32) + spread[f * places : (f + 1) * places]).astype(BF16)


def gather_blocks(parts, places):
    groups = -(-places // SUB)
    blocks = []
    for ref in parts:
        for t in range(ref.shape[0]):
            value = ref[t].astype(F32)
            if groups * SUB > places:
                value = jnp.concatenate([value, jnp.zeros((groups * SUB - places, value.shape[1]), F32)], 0)
            blocks.append(value)
    return jnp.concatenate([b[g * SUB : (g + 1) * SUB] for g in range(groups) for b in blocks], 0)


def temporal_kernel(n_pair, places, modulation, proj, weights, *refs):
    tokens, results = refs[:n_pair], refs[n_pair : 2 * n_pair]
    keep, give, held = refs[2 * n_pair :]
    n_frames = 2 * n_pair
    groups = -(-places // SUB)
    inner = proj.shape[0]
    attended = gather_blocks(results, places).astype(BF16)
    spatial = dot(attended, proj[...]).astype(BF16)
    after = (gather_blocks(tokens, places) + modulation[2:3] * spatial.astype(F32)).astype(BF16)
    normed = (layer_norm(after.astype(F32)) * (1.0 + modulation[4:5]) + modulation[3:4]).astype(BF16)
    projected = dot(normed, weights[...]).astype(BF16)
    size = n_frames * SUB
    row = lax.broadcasted_iota(jnp.int32, (size, size), 0)
    col = lax.broadcasted_iota(jnp.int32, (size, size), 1)
    same = (row & (SUB - 1)) == (col & (SUB - 1))
    ones = jnp.ones((size, LANES - HD), BF16)
    for g in range(groups):
        block = projected[g * size : (g + 1) * size]
        mixtures = []
        for h in range(inner // HD):
            query, key, val = (block[:, j * inner + h * HD : j * inner + (h + 1) * HD] for j in range(3))
            scores = lax.dot_general(query, key, (((1,), (1,)), ((), ())), preferred_element_type=F32)
            scores = jnp.where(same, scores, -jnp.inf)
            top = jnp.max(scores, -1, keepdims=True)
            mix = jnp.exp((scores - top) * (1.0 / math.sqrt(HD)))
            mixed = dot(mix.astype(BF16), jnp.concatenate([val, ones], 1))
            mixtures.append((mixed[:, :HD] / mixed[:, HD : HD + 1]).astype(BF16))
        whole = jnp.concatenate(mixtures, 1)
        for f in range(n_frames):
            held[f, g * SUB : (g + 1) * SUB] = whole[f * SUB : (f + 1) * SUB]
    for s in range(n_pair):
        keep[s] = held[2 * s][:places]
        give[s] = held[2 * s + 1][:places]


def finish_kernel(n_pair, places, modulation, proj, after, *refs):
    parts, out = refs[:n_pair], refs[n_pair]
    frame = lax.axis_index("frames")
    pad = -(-places // SUB) * SUB
    blocks = []
    for ref in parts:
        for t in range(ref.shape[0]):
            value = ref[t].astype(F32)
            if pad > places:
                value = jnp.concatenate([value, jnp.zeros((pad - places, value.shape[1]), F32)], 0)
            blocks.append(value.astype(BF16))
    branch = modulation[5:6] * dot(jnp.concatenate(blocks, 0), proj[...])
    for k in range(2 * n_pair):
        at = frame ^ k
        out[at] = (after[at].astype(F32) + branch[k * pad : k * pad + places]).astype(BF16)


def swap(block, axis, size, mask):
    return lax.ppermute(block, axis, [(i, i ^ mask) for i in range(size)])


def exchange(keep, give, size):
    got = swap(give, "frames", size, 1)
    both = jnp.stack([keep, got], 1)
    others = [swap(both[s], "frames", size, 2 * s) for s in range(1, size // 2)]
    return [both[0]] + others


def shards(n_frames, n_space, latents, merge_slot, modulation, spatial_qkv, spatial_proj, temporal_qkv, temporal_proj):
    rows, width = latents.shape[1:]
    slots, places = rows // 2, rows // n_frames
    inner = spatial_proj.shape[0]
    wide = inner // n_space
    n_pair = n_frames // 2
    own = latents[0]
    blocks = latents.reshape(n_frames, places, width)
    slot_column = merge_slot.reshape(rows, 1)
    sent = packed_rows(slots, 3 * wide)
    queries = pl.pallas_call(
        functools.partial(merge_kernel, n_space),
        out_shape=[struct(sent, LANES)] * n_space,
        in_specs=[VMEM, VMEM, VMEM, ANY],
        out_specs=[VMEM] * n_space,
        scratch_shapes=[
            pltpu.VMEM((n_space, sent, LANES), BF16),
            pltpu.VMEM(spatial_qkv.shape, BF16),
            pltpu.SemaphoreType.DMA,
        ],
        compiler_params=params(32),
        name="merge",
    )(own, merge_slot, modulation, spatial_qkv)
    held = [queries[0]] + [swap(queries[s], "space", n_space, s) for s in range(1, n_space)]
    returned = packed_rows(slots, wide)
    results = pl.pallas_call(
        functools.partial(attention_kernel, n_space, slots, wide),
        out_shape=[struct(returned, LANES)] * n_space,
        in_specs=[VMEM] * n_space,
        out_specs=[VMEM] * n_space,
        compiler_params=params(32),
        name="attend",
    )(*held)
    mine = [results[0]] + [swap(results[s], "space", n_space, s) for s in range(1, n_space)]
    keep, give, attended = pl.pallas_call(
        functools.partial(expand_kernel, n_space, n_pair, slots, wide),
        out_shape=[struct(n_pair, places, inner), struct(n_pair, places, inner), struct(slots, inner)],
        in_specs=[VMEM] * (n_space + 1),
        out_specs=[VMEM] * 3,
        scratch_shapes=[pltpu.VMEM((n_space, slots, wide), BF16), pltpu.VMEM((n_frames, places, inner), BF16)],
        compiler_params=params(32),
        name="expand",
    )(slot_column, *mine)
    blocks_late, _ = lax.optimization_barrier((blocks, queries[0]))
    token_keep, token_give = pl.pallas_call(
        functools.partial(share_kernel, n_pair),
        out_shape=[struct(n_pair, places, width)] * 2,
        in_specs=[VMEM],
        out_specs=[VMEM] * 2,
        compiler_params=params(32),
        name="share",
    )(blocks_late)
    tokens = exchange(token_keep, token_give, n_frames)
    attended_parts = exchange(keep, give, n_frames)
    after = pl.pallas_call(
        residual_kernel,
        out_shape=struct(n_frames, places, width),
        in_specs=[VMEM] * 5,
        out_specs=VMEM,
        compiler_params=params(32),
        name="residual",
    )(attended, slot_column, blocks, modulation, spatial_proj)
    pad = -(-places // SUB) * SUB
    mixed_keep, mixed_give = pl.pallas_call(
        functools.partial(temporal_kernel, n_pair, places),
        out_shape=[struct(n_pair, places, inner)] * 2,
        in_specs=[VMEM] * (3 + 2 * n_pair),
        out_specs=[VMEM] * 2,
        scratch_shapes=[pltpu.VMEM((n_frames, pad, inner), BF16)],
        compiler_params=params(48),
        name="temporal",
    )(modulation, spatial_proj, temporal_qkv, *tokens, *attended_parts)
    parts = exchange(mixed_keep, mixed_give, n_frames)
    out = pl.pallas_call(
        functools.partial(finish_kernel, n_pair, places),
        out_shape=struct(n_frames, places, width),
        in_specs=[VMEM] * (3 + n_pair),
        out_specs=VMEM,
        compiler_params=params(32),
        name="finish",
    )(modulation, temporal_proj, after, *parts)
    return out.reshape(1, rows, width)


def plain_modulate(values, modulation, which):
    normed = layer_norm(values.astype(F32))
    return (normed * (1.0 + modulation[which + 1]) + modulation[which]).astype(BF16)


def plain_shards(latents, merge_slot, modulation, spatial_qkv, spatial_proj, temporal_qkv, temporal_proj):
    row_count = latents.shape[1]
    slot_count = row_count // 2
    width = latents.shape[2]
    inner = spatial_proj.shape[0]
    root_size = math.sqrt(HD)
    own_rows = latents[0]
    normed = plain_modulate(own_rows, modulation, 0)
    local_slot = merge_slot[0] - lax.axis_index("space") * slot_count
    one_hot = (local_slot[:, None] == jnp.arange(slot_count, dtype=jnp.int32)[None, :]).astype(
        jnp.bfloat16
    )
    counts = jnp.sum(one_hot.astype(jnp.float32), 0)
    summed = lax.dot_general(
        one_hot, normed, (((0,), (0,)), ((), ())), preferred_element_type=jnp.float32
    )
    merged = (summed / counts[:, None]).astype(jnp.bfloat16)
    projected = jnp.dot(merged, spatial_qkv, preferred_element_type=jnp.float32).astype(
        jnp.bfloat16
    )
    query_rows = projected[:, :inner]
    key_rows = projected[:, inner : 2 * inner]
    value_rows = projected[:, 2 * inner :]
    head_query, head_key, head_value = (
        lax.all_to_all(query_rows, "space", split_axis=1, concat_axis=0, tiled=True),
        lax.all_to_all(key_rows, "space", split_axis=1, concat_axis=0, tiled=True),
        lax.all_to_all(value_rows, "space", split_axis=1, concat_axis=0, tiled=True),
    )
    local_heads = head_query.shape[1] // HD
    all_slots = head_query.shape[0]
    scores = (
        jnp.einsum(
            "qhd,khd->hqk",
            head_query.reshape(all_slots, local_heads, HD),
            head_key.reshape(all_slots, local_heads, HD),
            preferred_element_type=jnp.float32,
        )
        / root_size
    )
    weights = jnp.exp(scores - jnp.max(scores, -1, keepdims=True))
    row_total = jnp.sum(weights, -1)
    mixture = jnp.einsum(
        "hqk,khd->qhd",
        weights.astype(jnp.bfloat16),
        head_value.reshape(all_slots, local_heads, HD),
        preferred_element_type=jnp.float32,
    )
    head_result = (
        (mixture / row_total.T[..., None]).astype(jnp.bfloat16).reshape(all_slots, local_heads * HD)
    )
    attended = lax.all_to_all(head_result, "space", split_axis=0, concat_axis=1, tiled=True)
    spatial_out = jnp.dot(attended, spatial_proj, preferred_element_type=jnp.float32).astype(
        jnp.bfloat16
    )
    spread_back = jnp.dot(one_hot, spatial_out, preferred_element_type=jnp.float32)
    after_spatial = (own_rows.astype(jnp.float32) + modulation[2] * spread_back).astype(
        jnp.bfloat16
    )
    by_place = lax.all_to_all(
        after_spatial[None], "frames", split_axis=1, concat_axis=0, tiled=True
    )
    frame_count = by_place.shape[0]
    place_count = by_place.shape[1]
    flat = by_place.reshape(frame_count * place_count, width)
    normed_time = plain_modulate(flat, modulation, 3)
    projected_time = jnp.dot(normed_time, temporal_qkv, preferred_element_type=jnp.float32).astype(
        jnp.bfloat16
    )
    split = projected_time.reshape(frame_count, place_count, 3, inner // HD, HD)
    scores_time = (
        jnp.einsum(
            "flhd,glhd->lhfg", split[:, :, 0], split[:, :, 1], preferred_element_type=jnp.float32
        )
        / root_size
    )
    weights_time = jnp.exp(scores_time - jnp.max(scores_time, -1, keepdims=True))
    total_time = jnp.sum(weights_time, -1)
    mixture_time = (
        jnp.einsum(
            "lhfg,glhd->flhd",
            weights_time.astype(jnp.bfloat16),
            split[:, :, 2],
            preferred_element_type=jnp.float32,
        )
        / total_time.transpose(2, 0, 1)[..., None]
    )
    attended_time = mixture_time.astype(jnp.bfloat16).reshape(frame_count * place_count, inner)
    branch = jnp.dot(attended_time, temporal_proj, preferred_element_type=jnp.float32)
    finished = (
        (flat.astype(jnp.float32) + modulation[5] * branch)
        .astype(jnp.bfloat16)
        .reshape(frame_count, place_count, width)
    )
    return lax.all_to_all(finished, "frames", split_axis=0, concat_axis=1, tiled=True)


def solution(mesh):
    n_frames, n_space = mesh.shape["frames"], mesh.shape["space"]
    placed = (P("frames", "space", None), P("frames", "space"), P(), P(), P(), P(), P())

    def local(latents, *rest):
        fits = latents.shape[1] % (8 * n_frames) == 0 and n_frames & (n_frames - 1) == 0 and n_space & (n_space - 1) == 0
        body = functools.partial(shards, n_frames, n_space) if fits else plain_shards
        return body(latents, *rest)

    return jax.shard_map(local, mesh=mesh, in_specs=placed, out_specs=P("frames", "space", None), check_vma=False)
```

```python
import functools
import math

import jax
import jax.numpy as jnp
from jax import lax
from jax.experimental import pallas as pl
from jax.experimental.pallas import tpu as pltpu
from jax.sharding import PartitionSpec as P

HD = 72
LANES = 128
SUB = 16
F32 = jnp.float32
BF16 = jnp.bfloat16
VMEM = pl.BlockSpec(memory_space=pltpu.VMEM)
HBM = pl.BlockSpec(memory_space=pltpu.HBM)
MIB = 1 << 20
SCALE = math.log2(math.e) / math.sqrt(HD)


def struct(*shape):
    return jax.ShapeDtypeStruct(shape, BF16)


def params(mib):
    return pltpu.CompilerParams(vmem_limit_bytes=mib * MIB)


def layer_norm(values):
    center = values - jnp.mean(values, -1, keepdims=True)
    spread = jnp.mean(center * center, -1, keepdims=True)
    return center * lax.rsqrt(spread + 1e-06)


def dot(left, right):
    return jnp.dot(left, right, preferred_element_type=F32)


def dot_t(left, right):
    return lax.dot_general(left, right, (((1,), (1,)), ((), ())), preferred_element_type=F32)


def packing(rows, width):
    full, rest = divmod(width, LANES)
    groups = 1
    if rest:
        units = rows // SUB
        groups = max([g for g in range(1, units + 1) if units % g == 0 and g * rest <= LANES and rows % SUB == 0] or [1])
    return full, rest, groups


def packed_rows(rows, width):
    full, rest, groups = packing(rows, width)
    return full * rows + (rows // groups if rest else 0)


def pack(block):
    rows, width = block.shape
    full, rest, groups = packing(rows, width)
    parts = [block[:, j * LANES : (j + 1) * LANES] for j in range(full)]
    if rest:
        high = rows // groups
        tail = block[:, full * LANES :]
        pieces = [tail[i * high : (i + 1) * high] for i in range(groups)]
        if groups * rest < LANES:
            pieces.append(jnp.zeros((high, LANES - groups * rest), block.dtype))
        parts.append(jnp.concatenate(pieces, 1))
    return jnp.concatenate(parts, 0)


def unpack(packed, rows, width):
    full, rest, groups = packing(rows, width)
    parts = [packed[j * rows : (j + 1) * rows] for j in range(full)]
    if rest:
        high = rows // groups
        tail = packed[full * rows : full * rows + high]
        pieces = [tail[:, i * rest : (i + 1) * rest] for i in range(groups)]
        parts.append(jnp.concatenate(pieces, 0))
    return jnp.concatenate(parts, 1)


def merge_kernel(n_space, n_pair, latents, slot, modulation, weights, *refs):
    outs, (keep, give, held, tokens, slots_in, mods, arrived, sems) = refs[:n_space], refs[n_space:]
    pairs = ((latents, tokens), (slot, slots_in), (modulation, mods), (weights, arrived))
    copies = [pltpu.make_async_copy(there, here, sems.at[i]) for i, (there, here) in enumerate(pairs)]
    for copy in copies:
        copy.start()
    me, frame = lax.axis_index("space"), lax.axis_index("frames")
    places, width = latents.shape[1:]
    rows = 2 * n_pair * places
    slots = rows // 2
    inner = weights.shape[0] // 3
    wide = inner // n_space
    for copy in copies[:3]:
        copy.wait()
    shift, scale = mods[0:1], 1.0 + mods[1:2]
    normed = jnp.concatenate(
        [layer_norm(tokens[f].astype(F32)) * scale + shift for f in range(2 * n_pair)], 0
    ).astype(BF16)
    local = slots_in[...] - me * slots
    chosen = lax.broadcasted_iota(jnp.int32, (slots, rows), 0) == local
    counts = jnp.sum(chosen.astype(F32), 1, keepdims=True)
    merged = (dot(chosen.astype(BF16), normed) / counts).astype(BF16)
    for s in range(n_pair):
        keep[s] = tokens[frame ^ (2 * s)]
        give[s] = tokens[frame ^ (2 * s + 1)]
    copies[3].wait()
    projected = dot_t(merged, arrived[...])
    queries = (projected[:, :inner] * SCALE).astype(BF16)
    others = projected[:, inner:].astype(BF16)
    for d in range(n_space):
        at = d * wide
        held[d] = pack(
            jnp.concatenate(
                [queries[:, at : at + wide], others[:, at : at + wide], others[:, inner + at : inner + at + wide]], 1
            )
        )
    for s in range(n_space):
        outs[s][...] = held[me ^ s]


def attention_kernel(n_space, slots, wide, asked, *refs):
    ins, outs = refs[:n_space], refs[n_space:]
    blocks = [unpack(r[...], slots, 3 * wide) for r in reversed(ins)]
    results = [[] for _ in range(n_space)]
    for h in range(wide // HD):
        keys = jnp.concatenate([b[:, wide + h * HD : wide + (h + 1) * HD] for b in blocks], 0)
        vals = jnp.concatenate([b[:, 2 * wide + h * HD : 2 * wide + (h + 1) * HD] for b in blocks], 0)
        vals = jnp.concatenate([vals, jnp.ones((vals.shape[0], LANES - HD), BF16)], 1)
        for s in asked:
            query = blocks[s][:, h * HD : (h + 1) * HD]
            scores = dot_t(query, keys)
            top = jnp.max(scores, -1, keepdims=True)
            mixed = dot(jnp.exp2(scores - top).astype(BF16), vals)
            results[s].append((mixed[:, :HD] / mixed[:, HD : HD + 1]).astype(BF16))
    for out, s in zip(outs, asked):
        out[...] = pack(jnp.concatenate(results[s], 1))


def expand_kernel(n_space, n_pair, slots, wide, slot, *refs):
    ins, (keep, give, attended, held, spread) = refs[:n_space], refs[n_space:]
    me, frame = lax.axis_index("space"), lax.axis_index("frames")
    for s in range(n_space):
        held[me ^ s] = unpack(ins[n_space - 1 - s][...], slots, wide)
    whole = jnp.concatenate([held[d] for d in range(n_space)], 1)
    attended[...] = whole
    local = slot[...] - me * slots
    rows = slot.shape[0]
    chosen = (lax.broadcasted_iota(jnp.int32, (rows, slots), 1) == local).astype(BF16)
    wanted = dot(chosen, whole)
    places = keep.shape[1]
    for f in range(2 * n_pair):
        spread[f] = wanted[f * places : (f + 1) * places].astype(BF16)
    for s in range(n_pair):
        keep[s] = spread[frame ^ (2 * s)]
        give[s] = spread[frame ^ (2 * s + 1)]


def cost(flops):
    return pl.CostEstimate(flops=flops, bytes_accessed=flops // 100, transcendentals=0)


def residual_kernel(attended, slot, latents, modulation, proj, after):
    me = lax.axis_index("space")
    slots, rows = attended.shape[0], slot.shape[0]
    places = latents.shape[1]
    out = dot(attended[...], proj[...]).astype(BF16)
    local = slot[...] - me * slots
    chosen = (lax.broadcasted_iota(jnp.int32, (rows, slots), 1) == local).astype(BF16)
    spread = modulation[2:3] * dot(chosen, out)
    for f in range(latents.shape[0]):
        after[f] = (latents[f].astype(F32) + spread[f * places : (f + 1) * places]).astype(BF16)


def project_blocks(places, modulation, proj, weights, tokens, results, normed):
    frames = [(s, t) for s in range(len(tokens)) for t in range(2)]
    attended = jnp.concatenate([results[s][t].astype(F32) for s, t in frames], 0).astype(BF16)
    spatial = dot(attended, proj[...])
    gate, shift, scale = modulation[2:3], modulation[3:4], 1.0 + modulation[4:5]
    for f, (s, t) in enumerate(frames):
        at = slice(f * places, (f + 1) * places)
        normed[at] = layer_norm(tokens[s][t].astype(F32) + gate * spatial[at]) * scale + shift
    projected = dot_t(normed[...].astype(BF16), weights[...])
    space = jnp.zeros((-places % SUB, projected.shape[1]), F32)
    return [
        jnp.concatenate([projected[f * places : (f + 1) * places], space], 0).astype(BF16)
        for f in range(len(frames))
    ]


def project_kernel(places, n_parts, modulation, proj, weights, *refs):
    out, normed = refs[2 * n_parts :]
    blocks = project_blocks(places, modulation, proj, weights, refs[:n_parts], refs[n_parts : 2 * n_parts], normed)
    for f, block in enumerate(blocks):
        out[f] = block


def temporal_kernel(n_pair, places, n_parts, order, modulation, proj, weights, *refs):
    tokens, results, before = refs[:n_parts], refs[n_parts : 2 * n_parts], refs[2 * n_parts : n_pair + n_parts]
    keep, give, normed, held = refs[n_pair + n_parts :]
    n_frames = 2 * n_pair
    groups = -(-places // SUB)
    inner = proj.shape[0]
    heads = inner // HD
    by_frame = [ref[t] for ref in before for t in range(2)]
    by_frame += project_blocks(places, modulation, proj, weights, tokens, results, normed)
    size = n_frames * SUB
    row = lax.broadcasted_iota(jnp.int32, (size, size), 0)
    col = lax.broadcasted_iota(jnp.int32, (size, size), 1)
    same = ((row & (SUB - 1)) == (col & (SUB - 1)))[None]
    ones = jnp.ones((size, LANES - HD), BF16)
    for g in range(groups):
        block = jnp.concatenate([b[g * SUB : (g + 1) * SUB] for b in by_frame], 0)

        def part(j, h):
            return block[:, j * inner + h * HD : j * inner + (h + 1) * HD]

        scores = jnp.concatenate([dot_t(part(0, h), part(1, h)) for h in range(heads)], 0)
        scores = jnp.where(same, scores.reshape(heads, size, size), -jnp.inf)
        mix = jnp.exp2((scores - jnp.max(scores, -1, keepdims=True)) * SCALE).astype(BF16)
        mixed = [dot(mix[h], jnp.concatenate([part(2, h), ones], 1)) for h in range(heads)]
        whole = jnp.concatenate([(m[:, :HD] / m[:, HD : HD + 1]).astype(BF16) for m in mixed], 1)
        for f in range(n_frames):
            held[f, g * SUB : (g + 1) * SUB] = whole[f * SUB : (f + 1) * SUB]
    for i, s in enumerate(order):
        keep[s] = held[2 * i][:places]
        give[s] = held[2 * i + 1][:places]


def finish_kernel(n_pair, places, modulation, proj, after, *refs):
    parts, out = refs[:n_pair], refs[n_pair]
    frame = lax.axis_index("frames")
    frames = [(s, t) for s in range(n_pair) for t in range(2)]
    mixed = jnp.concatenate([parts[s][t].astype(F32) for s, t in frames], 0).astype(BF16)
    branch = dot(mixed, proj[...])
    gate = modulation[5:6]
    for k in range(2 * n_pair):
        at = frame ^ k
        out[at] = (after[at].astype(F32) + gate * branch[k * places : (k + 1) * places]).astype(BF16)


def swap(block, axis, size, mask):
    return lax.ppermute(block, axis, [(i, i ^ mask) for i in range(size)])


def swaps(blocks, axis, size, step=1):
    moved = {s: swap(blocks[s], axis, size, s * step) for s in range(len(blocks) - 1, 0, -1)}
    return [blocks[0]] + [moved[s] for s in range(1, len(blocks))]


def exchange(keep, give, size):
    got = swap(give, "frames", size, 1)
    both = jnp.stack([keep, got], 1)
    return swaps([both[s] for s in range(size // 2)], "frames", size, 2)


def shards(n_frames, n_space, latents, merge_slot, modulation, spatial_qkv, spatial_proj, temporal_qkv, temporal_proj):
    rows, width = latents.shape[1:]
    slots, places = rows // 2, rows // n_frames
    inner = spatial_proj.shape[0]
    wide = inner // n_space
    n_pair = n_frames // 2
    spatial_qkv, temporal_qkv = spatial_qkv.T, temporal_qkv.T
    blocks = latents.reshape(n_frames, places, width)
    slot_column = merge_slot.reshape(rows, 1)
    sent = packed_rows(slots, 3 * wide)
    *queries, token_keep, token_give = pl.pallas_call(
        functools.partial(merge_kernel, n_space, n_pair),
        out_shape=[struct(sent, LANES)] * n_space + [struct(n_pair, places, width)] * 2,
        in_specs=[HBM] * 4,
        out_specs=[VMEM] * (n_space + 2),
        scratch_shapes=[
            pltpu.VMEM((n_space, sent, LANES), BF16),
            pltpu.VMEM(blocks.shape, BF16),
            pltpu.VMEM(merge_slot.shape, jnp.int32),
            pltpu.VMEM(modulation.shape, F32),
            pltpu.VMEM(spatial_qkv.shape, BF16),
            pltpu.SemaphoreType.DMA((4,)),
        ],
        compiler_params=params(57),
        name="merge",
    )(blocks, merge_slot, modulation, spatial_qkv)
    held = swaps(queries, "space", n_space)
    tokens = exchange(token_keep, token_give, n_frames)
    held = lax.optimization_barrier(held[::-1])
    returned = packed_rows(slots, wide)
    results = {}
    for name, asked in (("others", range(1, n_space)), ("own", range(1))):
        if name == "own":
            held, tokens = lax.optimization_barrier((held, tokens))
        done = pl.pallas_call(
            functools.partial(attention_kernel, n_space, slots, wide, asked),
            out_shape=[struct(returned, LANES)] * len(asked),
            in_specs=[VMEM] * n_space,
            out_specs=[VMEM] * len(asked),
            compiler_params=params(20),
            cost_estimate=cost(4 * slots * slots * n_space * n_space * wide),
            name="attend_" + name,
        )(*held)
        results.update(zip(asked, done))
    mine = swaps(results, "space", n_space)
    keep, give, attended = pl.pallas_call(
        functools.partial(expand_kernel, n_space, n_pair, slots, wide),
        out_shape=[struct(n_pair, places, inner), struct(n_pair, places, inner), struct(slots, inner)],
        in_specs=[VMEM] * (n_space + 1),
        out_specs=[VMEM] * 3,
        scratch_shapes=[pltpu.VMEM((n_space, slots, wide), BF16), pltpu.VMEM((n_frames, places, inner), BF16)],
        compiler_params=params(20),
        name="expand",
    )(slot_column, *reversed(mine))
    attended_parts = exchange(keep, give, n_frames)
    after = pl.pallas_call(
        residual_kernel,
        out_shape=struct(n_frames, places, width),
        in_specs=[VMEM] * 5,
        out_specs=VMEM,
        compiler_params=params(20),
        cost_estimate=cost(4 * slots * inner * width),
        name="residual",
    )(attended, slot_column, blocks, modulation, spatial_proj)
    pad = -(-places // SUB) * SUB
    order = [0] + list(range(n_pair - 1, 0, -1))
    steps = [order[:1], order[1:2]] if n_pair > 2 else [order[:1]]
    last = order[len(steps) :]
    before = []
    for i, step in enumerate(steps):
        before += [
            pl.pallas_call(
                functools.partial(project_kernel, places, len(step)),
                out_shape=struct(2 * len(step), pad, 3 * inner),
                in_specs=[VMEM] * (3 + 2 * len(step)),
                out_specs=VMEM,
                scratch_shapes=[pltpu.VMEM((2 * len(step) * places, width), F32)],
                compiler_params=params(16),
                cost_estimate=cost(2 * 2 * places * len(step) * 3 * inner * width),
                name="project_%d" % i,
            )(
                modulation,
                spatial_proj,
                temporal_qkv,
                *[tokens[s] for s in step],
                *[attended_parts[s] for s in step],
            )
        ]
    mixed = pl.pallas_call(
        functools.partial(temporal_kernel, n_pair, places, len(last), order),
        out_shape=[struct(n_pair, places, inner)] * 2,
        in_specs=[VMEM] * (3 + len(last) + n_pair),
        out_specs=[VMEM] * 2,
        scratch_shapes=[
            pltpu.VMEM((2 * len(last) * places, width), F32),
            pltpu.VMEM((n_frames, pad, inner), BF16),
        ],
        compiler_params=params(20),
        name="temporal",
    )(
        modulation,
        spatial_proj,
        temporal_qkv,
        *[tokens[s] for s in last],
        *[attended_parts[s] for s in last],
        *before,
    )
    mixed_keep, mixed_give = mixed
    parts = exchange(mixed_keep, mixed_give, n_frames)
    out = pl.pallas_call(
        functools.partial(finish_kernel, n_pair, places),
        out_shape=struct(n_frames, places, width),
        in_specs=[VMEM] * (3 + n_pair),
        out_specs=VMEM,
        compiler_params=params(20),
        name="finish",
    )(modulation, temporal_proj, after, *parts)
    return out.reshape(1, rows, width)


def plain_modulate(values, modulation, which):
    normed = layer_norm(values.astype(F32))
    return (normed * (1.0 + modulation[which + 1]) + modulation[which]).astype(BF16)


def plain_shards(latents, merge_slot, modulation, spatial_qkv, spatial_proj, temporal_qkv, temporal_proj):
    row_count = latents.shape[1]
    slot_count = row_count // 2
    width = latents.shape[2]
    inner = spatial_proj.shape[0]
    root_size = math.sqrt(HD)
    own_rows = latents[0]
    normed = plain_modulate(own_rows, modulation, 0)
    local_slot = merge_slot[0] - lax.axis_index("space") * slot_count
    one_hot = (local_slot[:, None] == jnp.arange(slot_count, dtype=jnp.int32)[None, :]).astype(
        jnp.bfloat16
    )
    counts = jnp.sum(one_hot.astype(jnp.float32), 0)
    summed = lax.dot_general(
        one_hot, normed, (((0,), (0,)), ((), ())), preferred_element_type=jnp.float32
    )
    merged = (summed / counts[:, None]).astype(jnp.bfloat16)
    projected = jnp.dot(merged, spatial_qkv, preferred_element_type=jnp.float32).astype(
        jnp.bfloat16
    )
    query_rows = projected[:, :inner]
    key_rows = projected[:, inner : 2 * inner]
    value_rows = projected[:, 2 * inner :]
    head_query, head_key, head_value = (
        lax.all_to_all(query_rows, "space", split_axis=1, concat_axis=0, tiled=True),
        lax.all_to_all(key_rows, "space", split_axis=1, concat_axis=0, tiled=True),
        lax.all_to_all(value_rows, "space", split_axis=1, concat_axis=0, tiled=True),
    )
    local_heads = head_query.shape[1] // HD
    all_slots = head_query.shape[0]
    scores = (
        jnp.einsum(
            "qhd,khd->hqk",
            head_query.reshape(all_slots, local_heads, HD),
            head_key.reshape(all_slots, local_heads, HD),
            preferred_element_type=jnp.float32,
        )
        / root_size
    )
    weights = jnp.exp(scores - jnp.max(scores, -1, keepdims=True))
    row_total = jnp.sum(weights, -1)
    mixture = jnp.einsum(
        "hqk,khd->qhd",
        weights.astype(jnp.bfloat16),
        head_value.reshape(all_slots, local_heads, HD),
        preferred_element_type=jnp.float32,
    )
    head_result = (
        (mixture / row_total.T[..., None]).astype(jnp.bfloat16).reshape(all_slots, local_heads * HD)
    )
    attended = lax.all_to_all(head_result, "space", split_axis=0, concat_axis=1, tiled=True)
    spatial_out = jnp.dot(attended, spatial_proj, preferred_element_type=jnp.float32).astype(
        jnp.bfloat16
    )
    spread_back = jnp.dot(one_hot, spatial_out, preferred_element_type=jnp.float32)
    after_spatial = (own_rows.astype(jnp.float32) + modulation[2] * spread_back).astype(
        jnp.bfloat16
    )
    by_place = lax.all_to_all(
        after_spatial[None], "frames", split_axis=1, concat_axis=0, tiled=True
    )
    frame_count = by_place.shape[0]
    place_count = by_place.shape[1]
    flat = by_place.reshape(frame_count * place_count, width)
    normed_time = plain_modulate(flat, modulation, 3)
    projected_time = jnp.dot(normed_time, temporal_qkv, preferred_element_type=jnp.float32).astype(
        jnp.bfloat16
    )
    split = projected_time.reshape(frame_count, place_count, 3, inner // HD, HD)
    scores_time = (
        jnp.einsum(
            "flhd,glhd->lhfg", split[:, :, 0], split[:, :, 1], preferred_element_type=jnp.float32
        )
        / root_size
    )
    weights_time = jnp.exp(scores_time - jnp.max(scores_time, -1, keepdims=True))
    total_time = jnp.sum(weights_time, -1)
    mixture_time = (
        jnp.einsum(
            "lhfg,glhd->flhd",
            weights_time.astype(jnp.bfloat16),
            split[:, :, 2],
            preferred_element_type=jnp.float32,
        )
        / total_time.transpose(2, 0, 1)[..., None]
    )
    attended_time = mixture_time.astype(jnp.bfloat16).reshape(frame_count * place_count, inner)
    branch = jnp.dot(attended_time, temporal_proj, preferred_element_type=jnp.float32)
    finished = (
        (flat.astype(jnp.float32) + modulation[5] * branch)
        .astype(jnp.bfloat16)
        .reshape(frame_count, place_count, width)
    )
    return lax.all_to_all(finished, "frames", split_axis=0, concat_axis=1, tiled=True)


def solution(mesh):
    n_frames, n_space = mesh.shape["frames"], mesh.shape["space"]
    placed = (P("frames", "space", None), P("frames", "space"), P(), P(), P(), P(), P())

    def local(latents, *rest):
        fits = latents.shape[1] % (8 * n_frames) == 0 and n_frames & (n_frames - 1) == 0 and n_space & (n_space - 1) == 0
        body = functools.partial(shards, n_frames, n_space) if fits else plain_shards
        return body(latents, *rest)

    return jax.shard_map(local, mesh=mesh, in_specs=placed, out_specs=P("frames", "space", None), check_vma=False)
```

```python
import functools
import math

import jax
import jax.numpy as jnp
from jax import lax
from jax.experimental import pallas as pl
from jax.experimental.pallas import tpu as pltpu
from jax.sharding import PartitionSpec as P

HD = 72
LANES = 128
SUB = 16
F32 = jnp.float32
BF16 = jnp.bfloat16
VMEM = pl.BlockSpec(memory_space=pltpu.VMEM)
HBM = pl.BlockSpec(memory_space=pltpu.HBM)
MIB = 1 << 20
SCALE = math.log2(math.e) / math.sqrt(HD)


def struct(*shape):
    return jax.ShapeDtypeStruct(shape, BF16)


def params(mib):
    return pltpu.CompilerParams(vmem_limit_bytes=mib * MIB)


def layer_norm(values):
    center = values - jnp.mean(values, -1, keepdims=True)
    spread = jnp.mean(center * center, -1, keepdims=True)
    return center * lax.rsqrt(spread + 1e-06)


def dot(left, right):
    return jnp.dot(left, right, preferred_element_type=F32)


def dot_t(left, right):
    return lax.dot_general(left, right, (((1,), (1,)), ((), ())), preferred_element_type=F32)


def packing(rows, width):
    full, rest = divmod(width, LANES)
    free = LANES - rest
    parts = rest // free + 1 if rest and rest % free == 0 else 1
    high = -(-rows // (8 * parts)) * 8
    if rows - high * (parts - 1) <= 0 or parts == 1:
        parts, high = 1, rows
    return full, rest, parts, high


def packed_rows(rows, width):
    full, rest, parts, high = packing(rows, width)
    return -(-(full * rows + (max(parts - 1, 1) * high if rest else 0)) // SUB) * SUB


def pack(block):
    rows, width = block.shape
    full, rest, parts, high = packing(rows, width)
    pieces = [block[:, j * LANES : (j + 1) * LANES] for j in range(full)]
    if rest:
        tail, free = block[:, full * LANES :], LANES - rest
        if parts == 1:
            pieces.append(jnp.concatenate([tail, jnp.zeros((rows, free), block.dtype)], 1))
        else:
            last = tail[(parts - 1) * high :]
            if last.shape[0] < high:
                last = jnp.concatenate([last, jnp.zeros((high - last.shape[0], rest), block.dtype)], 0)
            for i in range(parts - 1):
                side = last[:, i * free : (i + 1) * free]
                pieces.append(jnp.concatenate([tail[i * high : (i + 1) * high], side], 1))
    here = sum(p.shape[0] for p in pieces)
    if here % SUB:
        pieces.append(jnp.zeros((-here % SUB, LANES), block.dtype))
    return jnp.concatenate(pieces, 0)


def unpack(packed, rows, width):
    full, rest, parts, high = packing(rows, width)
    pieces = [packed[j * rows : (j + 1) * rows] for j in range(full)]
    if rest:
        tail = packed[full * rows :]
        if parts == 1:
            pieces.append(tail[:rows, :rest])
        else:
            tiles = [tail[i * high : (i + 1) * high] for i in range(parts - 1)]
            last = jnp.concatenate([t[:, rest:] for t in tiles], 1)[: rows - (parts - 1) * high]
            pieces.append(jnp.concatenate([t[:, :rest] for t in tiles] + [last], 0))
    return jnp.concatenate(pieces, 1)


def merge_kernel(n_space, latents, slot, modulation, weights, out, merged, tokens, slots_in, mods, arrived, sems):
    me = lax.axis_index("space")
    inner = weights.shape[0] // 3
    wide = inner // n_space
    theirs = pl.multiple_of((me ^ (n_space - 1)) * wide, SUB)
    pairs = [(latents, tokens), (slot, slots_in), (modulation, mods)]
    pairs += [(weights.at[pl.ds(j * inner + theirs, wide)], arrived.at[pl.ds(j * wide, wide)]) for j in range(3)]
    copies = [pltpu.make_async_copy(there, here, sems.at[i]) for i, (there, here) in enumerate(pairs)]
    for copy in copies:
        copy.start()
    n_frames, places = latents.shape[:2]
    rows = n_frames * places
    slots = rows // 2
    for copy in copies[:3]:
        copy.wait()
    shift, scale = mods[0:1], 1.0 + mods[1:2]
    normed = jnp.concatenate(
        [layer_norm(tokens[f].astype(F32)) * scale + shift for f in range(n_frames)], 0
    ).astype(BF16)
    local = slots_in[...] - me * slots
    chosen = lax.broadcasted_iota(jnp.int32, (slots, rows), 0) == local
    counts = jnp.sum(chosen.astype(F32), 1, keepdims=True)
    held = (dot(chosen.astype(BF16), normed) / counts).astype(BF16)
    merged[...] = held
    for copy in copies[3:]:
        copy.wait()
    projected = dot_t(arrived[...], held)
    out[...] = pack(jnp.concatenate([projected[:wide] * SCALE, projected[wide:]], 0)).astype(BF16)


def spread_kernel(n_space, merged, weights, *refs):
    outs, (held, arrived, sem) = refs[: n_space - 1], refs[n_space - 1 :]
    copy = pltpu.make_async_copy(weights, arrived, sem)
    copy.start()
    me = lax.axis_index("space")
    inner = weights.shape[0] // 3
    wide = inner // n_space
    copy.wait()
    projected = dot_t(arrived[...], merged[...])
    for j in range(3):
        for d in range(n_space):
            part = projected[j * inner + d * wide : j * inner + (d + 1) * wide]
            held[d, j * wide : (j + 1) * wide] = part * SCALE if j == 0 else part
    for s in range(n_space - 1):
        outs[s][...] = pack(held[me ^ s]).astype(BF16)


def share_kernel(n_pair, latents, keep, give):
    frame = lax.axis_index("frames")
    for s in range(n_pair):
        keep[s] = latents[frame ^ (2 * s)]
        give[s] = latents[frame ^ (2 * s + 1)]


def prepare_kernel(wide, packed, slot, keys, others, chosen):
    slots, rows = keys.shape[0], slot.shape[1]
    local = slot[...] - lax.axis_index("space") * slots
    joined = (lax.broadcasted_iota(jnp.int32, (slots, rows), 0) == local).astype(F32)
    chosen[...] = joined.T.astype(BF16)
    block = unpack(packed[...].astype(F32), 3 * wide, slots)
    keys[...] = block[wide : 2 * wide].T.astype(BF16)
    others[...] = jnp.concatenate([block[:wide], block[2 * wide :]], 0).astype(BF16)


def attend(queries, keys, vals):
    ones = jnp.ones((8, vals.shape[1]), F32)
    results = []
    for h in range(vals.shape[0] // HD):
        at = slice(h * HD, (h + 1) * HD)
        scores = dot(keys[:, at], queries[at].astype(BF16))
        weights = jnp.exp2(scores - jnp.max(scores, 0, keepdims=True)).astype(BF16)
        mixed = dot(jnp.concatenate([vals[at], ones], 0).astype(BF16), weights)
        results.append(mixed[:HD] / mixed[HD : HD + 1])
    return jnp.concatenate(results, 0)


def others_kernel(n_space, slots, wide, far_keys, far_others, *refs):
    ins, outs, (own_queries, all_keys, all_vals) = refs[: n_space - 1], refs[n_space - 1 : -3], refs[-3:]
    blocks = [unpack(r[...].astype(F32), 3 * wide, slots) for r in reversed(ins)]
    others = far_others[...].astype(F32)
    queries = jnp.concatenate([b[:wide] for b in blocks[1:]] + [others[:wide]], 1)
    vals = jnp.concatenate([b[2 * wide :] for b in blocks] + [others[wide:]], 1)
    keys = jnp.concatenate([b[wide : 2 * wide].T.astype(BF16) for b in blocks] + [far_keys[...]], 0)
    own_queries[...] = blocks[0][:wide].astype(BF16)
    all_keys[...] = keys
    all_vals[...] = vals.astype(BF16)
    whole = attend(queries, keys, vals)
    for i, out in enumerate(outs):
        out[...] = pack(whole[:, i * slots : (i + 1) * slots]).astype(BF16)


def own_kernel(queries, keys, vals, out):
    out[...] = attend(queries[...].astype(F32), keys[...], vals[...].astype(F32)).astype(BF16)


def expand_kernel(n_space, n_pair, slots, wide, chosen, *refs):
    ins, (keep, give, attended, held, spread) = refs[:n_space], refs[n_space:]
    me, frame = lax.axis_index("space"), lax.axis_index("frames")
    held[me] = ins[n_space - 1][...].astype(F32)
    for s in range(1, n_space):
        held[me ^ s] = unpack(ins[n_space - 1 - s][...].astype(F32), wide, slots)
    whole = jnp.concatenate([held[d] for d in range(n_space)], 0).astype(BF16)
    attended[...] = whole
    wanted = dot_t(chosen[...], whole)
    places = keep.shape[1]
    for f in range(2 * n_pair):
        spread[f] = wanted[f * places : (f + 1) * places].astype(BF16)
    for s in range(n_pair):
        keep[s] = spread[frame ^ (2 * s)]
        give[s] = spread[frame ^ (2 * s + 1)]


def cost(flops):
    return pl.CostEstimate(flops=flops, bytes_accessed=flops // 100, transcendentals=0)


def residual_kernel(attended, chosen, latents, modulation, proj, after):
    places = latents.shape[1]
    out = dot(attended[...].astype(F32).T.astype(BF16), proj[...]).astype(BF16)
    spread = modulation[2:3] * dot(chosen[...], out)
    for f in range(latents.shape[0]):
        after[f] = (latents[f].astype(F32) + spread[f * places : (f + 1) * places]).astype(BF16)


def pair_kernel(keep, got, *outs):
    for s, out in enumerate(outs):
        out[0] = keep[s]
        out[1] = got[s]


def project_blocks(places, modulation, proj, weights, tokens, results, normed):
    frames = [(s, t) for s in range(len(tokens)) for t in range(2)]
    attended = jnp.concatenate([results[s][t].astype(F32) for s, t in frames], 0).astype(BF16)
    spatial = dot(attended, proj[...])
    gate, shift, scale = modulation[2:3], modulation[3:4], 1.0 + modulation[4:5]
    for f, (s, t) in enumerate(frames):
        at = slice(f * places, (f + 1) * places)
        normed[at] = layer_norm(tokens[s][t].astype(F32) + gate * spatial[at]) * scale + shift
    projected = dot_t(normed[...].astype(BF16), weights[...])
    space = jnp.zeros((-places % SUB, projected.shape[1]), F32)
    return [
        jnp.concatenate([projected[f * places : (f + 1) * places], space], 0).astype(BF16)
        for f in range(len(frames))
    ]


def project_kernel(places, n_parts, modulation, proj, weights, *refs):
    out, normed = refs[2 * n_parts :]
    blocks = project_blocks(places, modulation, proj, weights, refs[:n_parts], refs[n_parts : 2 * n_parts], normed)
    for f, block in enumerate(blocks):
        out[f] = block


def temporal_kernel(n_pair, places, n_parts, order, modulation, proj, weights, *refs):
    tokens, results, before = refs[:n_parts], refs[n_parts : 2 * n_parts], refs[2 * n_parts : n_pair + n_parts]
    keep, give, normed, held = refs[n_pair + n_parts :]
    n_frames = 2 * n_pair
    groups = -(-places // SUB)
    inner = proj.shape[0]
    heads = inner // HD
    by_frame = [ref[t] for ref in before for t in range(2)]
    by_frame += project_blocks(places, modulation, proj, weights, tokens, results, normed)
    size = n_frames * SUB
    row = lax.broadcasted_iota(jnp.int32, (size, size), 0)
    col = lax.broadcasted_iota(jnp.int32, (size, size), 1)
    same = jnp.concatenate([(row & (SUB - 1)) == (col & (SUB - 1))] * heads, 1)
    for g in range(groups):
        block = jnp.concatenate([b[g * SUB : (g + 1) * SUB] for b in by_frame], 0)

        def part(j, h):
            return block[:, j * inner + h * HD : j * inner + (h + 1) * HD]

        scores = jnp.concatenate([dot_t(part(1, h), part(0, h)) for h in range(heads)], 1)
        scores = jnp.where(same, scores, -jnp.inf)
        mix = jnp.exp2((scores - jnp.max(scores, 0, keepdims=True)) * SCALE)
        total = jnp.sum(mix, 0, keepdims=True)
        mix = mix.astype(BF16)
        vals = block[:, 2 * inner :].astype(F32).T
        mixed = [
            dot(vals[h * HD : (h + 1) * HD].astype(BF16), mix[:, h * size : (h + 1) * size])
            / total[:, h * size : (h + 1) * size]
            for h in range(heads)
        ]
        whole = jnp.concatenate(mixed, 0).T.astype(BF16)
        for f in range(n_frames):
            held[f, g * SUB : (g + 1) * SUB] = whole[f * SUB : (f + 1) * SUB]
    for i, s in enumerate(order):
        keep[s] = held[2 * i][:places]
        give[s] = held[2 * i + 1][:places]


def finish_kernel(taken, places, modulation, proj, after, *refs):
    parts, out = refs[: len(taken)], refs[-1]
    frame = lax.axis_index("frames")
    frames = [(s, t) for s in range(len(taken)) for t in range(2)]
    mixed = jnp.concatenate([parts[s][t].astype(F32) for s, t in frames], 0).astype(BF16)
    branch = dot(mixed, proj[...])
    gate = modulation[5:6]
    for k, (s, t) in enumerate(frames):
        at = frame ^ (2 * taken[s] + t)
        out[at] = (after[at].astype(F32) + gate * branch[k * places : (k + 1) * places]).astype(BF16)


def swap(block, axis, size, mask):
    return lax.ppermute(block, axis, [(i, i ^ mask) for i in range(size)])


def swaps(blocks, axis, size, step=1):
    moved = {s: swap(blocks[s], axis, size, s * step) for s in range(len(blocks) - 1, 0, -1)}
    return [blocks[0]] + [moved[s] for s in range(1, len(blocks))]


def exchange(keep, give, size):
    got = swap(give, "frames", size, 1)
    both = pl.pallas_call(
        pair_kernel,
        out_shape=[struct(2, *keep.shape[1:])] * (size // 2),
        in_specs=[VMEM] * 2,
        out_specs=[VMEM] * (size // 2),
        compiler_params=params(4),
        name="pair",
    )(keep, got)
    return swaps(both, "frames", size, 2)


def shards(n_frames, n_space, latents, merge_slot, modulation, spatial_qkv, spatial_proj, temporal_qkv, temporal_proj):
    rows, width = latents.shape[1:]
    slots, places = rows // 2, rows // n_frames
    inner = spatial_proj.shape[0]
    wide = inner // n_space
    n_pair = n_frames // 2
    spatial_qkv, temporal_qkv = spatial_qkv.T, temporal_qkv.T
    blocks = latents.reshape(n_frames, places, width)
    sent = packed_rows(3 * wide, slots)
    far, merged = pl.pallas_call(
        functools.partial(merge_kernel, n_space),
        out_shape=[struct(sent, LANES), struct(slots, width)],
        in_specs=[HBM] * 4,
        out_specs=[VMEM] * 2,
        scratch_shapes=[
            pltpu.VMEM(blocks.shape, BF16),
            pltpu.VMEM(merge_slot.shape, jnp.int32),
            pltpu.VMEM(modulation.shape, F32),
            pltpu.VMEM((3 * wide, width), BF16),
            pltpu.SemaphoreType.DMA((6,)),
        ],
        compiler_params=params(57),
        name="merge",
    )(blocks, merge_slot, modulation, spatial_qkv)
    queries = pl.pallas_call(
        functools.partial(spread_kernel, n_space),
        out_shape=[struct(sent, LANES)] * (n_space - 1),
        in_specs=[VMEM, HBM],
        out_specs=[VMEM] * (n_space - 1),
        scratch_shapes=[
            pltpu.VMEM((n_space, 3 * wide, slots), F32),
            pltpu.VMEM(spatial_qkv.shape, BF16),
            pltpu.SemaphoreType.DMA,
        ],
        compiler_params=params(20),
        cost_estimate=cost(2 * slots * 3 * inner * width),
        name="spread",
    )(merged, spatial_qkv)
    shared, merged = lax.optimization_barrier((blocks, merged))
    token_keep, token_give = pl.pallas_call(
        functools.partial(share_kernel, n_pair),
        out_shape=[struct(n_pair, places, width)] * 2,
        in_specs=[VMEM],
        out_specs=[VMEM] * 2,
        compiler_params=params(6),
        name="share",
    )(shared)
    queries = list(queries)
    queries.append(far)
    held = swaps(queries, "space", n_space)
    tokens = exchange(token_keep, token_give, n_frames)
    far_keys, far_others, chosen = pl.pallas_call(
        functools.partial(prepare_kernel, wide),
        out_shape=[struct(slots, wide), struct(2 * wide, slots), struct(rows, slots)],
        in_specs=[VMEM] * 2,
        out_specs=[VMEM] * 3,
        compiler_params=params(4),
        cost_estimate=cost(4 * slots * slots * n_space * n_space * wide),
        name="prepare",
    )(held[-1], merge_slot)
    held = lax.optimization_barrier([far_keys, far_others] + held[-2::-1])
    returned = packed_rows(wide, slots)
    *results, own_queries, all_keys, all_vals = pl.pallas_call(
        functools.partial(others_kernel, n_space, slots, wide),
        out_shape=[struct(returned, LANES)] * (n_space - 1)
        + [struct(wide, slots), struct(n_space * slots, wide), struct(wide, n_space * slots)],
        in_specs=[VMEM] * (n_space + 1),
        out_specs=[VMEM] * (n_space + 2),
        compiler_params=params(12),
        cost_estimate=cost(4 * slots * slots * n_space * (n_space - 1) * wide),
        name="attend_others",
    )(*held)
    own_queries, tokens = lax.optimization_barrier((own_queries, tokens))
    own = pl.pallas_call(
        own_kernel,
        out_shape=struct(wide, slots),
        in_specs=[VMEM] * 3,
        out_specs=VMEM,
        compiler_params=params(8),
        cost_estimate=cost(4 * slots * slots * n_space * wide),
        name="attend_own",
    )(own_queries, all_keys, all_vals)
    mine = swaps([own] + results, "space", n_space)
    keep, give, attended = pl.pallas_call(
        functools.partial(expand_kernel, n_space, n_pair, slots, wide),
        out_shape=[struct(n_pair, places, inner), struct(n_pair, places, inner), struct(inner, slots)],
        in_specs=[VMEM] * (n_space + 1),
        out_specs=[VMEM] * 3,
        scratch_shapes=[pltpu.VMEM((n_space, wide, slots), F32), pltpu.VMEM((n_frames, places, inner), BF16)],
        compiler_params=params(8),
        name="expand",
    )(chosen, *reversed(mine))
    attended_parts = exchange(keep, give, n_frames)
    after = pl.pallas_call(
        residual_kernel,
        out_shape=struct(n_frames, places, width),
        in_specs=[VMEM] * 5,
        out_specs=VMEM,
        compiler_params=params(10),
        cost_estimate=cost(4 * slots * inner * width),
        name="residual",
    )(attended, chosen, blocks, modulation, spatial_proj)
    pad = -(-places // SUB) * SUB
    order = [0] + list(range(n_pair - 1, 0, -1))
    steps = [order[:1], order[1:2]] if n_pair > 2 else [order[:1]]
    last = order[len(steps) :]
    before = []
    for i, step in enumerate(steps):
        before += [
            pl.pallas_call(
                functools.partial(project_kernel, places, len(step)),
                out_shape=struct(2 * len(step), pad, 3 * inner),
                in_specs=[VMEM] * (3 + 2 * len(step)),
                out_specs=VMEM,
                scratch_shapes=[pltpu.VMEM((2 * len(step) * places, width), F32)],
                compiler_params=params(10),
                cost_estimate=cost(2 * 2 * places * len(step) * 3 * inner * width),
                name="project_%d" % i,
            )(
                modulation,
                spatial_proj,
                temporal_qkv,
                *[tokens[s] for s in step],
                *[attended_parts[s] for s in step],
            )
        ]
    mixed = pl.pallas_call(
        functools.partial(temporal_kernel, n_pair, places, len(last), order),
        out_shape=[struct(n_pair, places, inner)] * 2,
        in_specs=[VMEM] * (3 + len(last) + n_pair),
        out_specs=[VMEM] * 2,
        scratch_shapes=[
            pltpu.VMEM((2 * len(last) * places, width), F32),
            pltpu.VMEM((n_frames, pad, inner), BF16),
        ],
        compiler_params=params(16),
        name="temporal",
    )(
        modulation,
        spatial_proj,
        temporal_qkv,
        *[tokens[s] for s in last],
        *[attended_parts[s] for s in last],
        *before,
    )
    mixed_keep, mixed_give = mixed
    parts = exchange(mixed_keep, mixed_give, n_frames)
    out = pl.pallas_call(
        functools.partial(finish_kernel, list(range(n_pair)), places),
        out_shape=struct(n_frames, places, width),
        in_specs=[VMEM] * (3 + n_pair),
        out_specs=VMEM,
        compiler_params=params(10),
        name="finish",
    )(modulation, temporal_proj, after, *parts)
    return out.reshape(1, rows, width)


def plain_modulate(values, modulation, which):
    normed = layer_norm(values.astype(F32))
    return (normed * (1.0 + modulation[which + 1]) + modulation[which]).astype(BF16)


def plain_shards(latents, merge_slot, modulation, spatial_qkv, spatial_proj, temporal_qkv, temporal_proj):
    row_count = latents.shape[1]
    slot_count = row_count // 2
    width = latents.shape[2]
    inner = spatial_proj.shape[0]
    root_size = math.sqrt(HD)
    own_rows = latents[0]
    normed = plain_modulate(own_rows, modulation, 0)
    local_slot = merge_slot[0] - lax.axis_index("space") * slot_count
    one_hot = (local_slot[:, None] == jnp.arange(slot_count, dtype=jnp.int32)[None, :]).astype(
        jnp.bfloat16
    )
    counts = jnp.sum(one_hot.astype(jnp.float32), 0)
    summed = lax.dot_general(
        one_hot, normed, (((0,), (0,)), ((), ())), preferred_element_type=jnp.float32
    )
    merged = (summed / counts[:, None]).astype(jnp.bfloat16)
    projected = jnp.dot(merged, spatial_qkv, preferred_element_type=jnp.float32).astype(
        jnp.bfloat16
    )
    query_rows = projected[:, :inner]
    key_rows = projected[:, inner : 2 * inner]
    value_rows = projected[:, 2 * inner :]
    head_query, head_key, head_value = (
        lax.all_to_all(query_rows, "space", split_axis=1, concat_axis=0, tiled=True),
        lax.all_to_all(key_rows, "space", split_axis=1, concat_axis=0, tiled=True),
        lax.all_to_all(value_rows, "space", split_axis=1, concat_axis=0, tiled=True),
    )
    local_heads = head_query.shape[1] // HD
    all_slots = head_query.shape[0]
    scores = (
        jnp.einsum(
            "qhd,khd->hqk",
            head_query.reshape(all_slots, local_heads, HD),
            head_key.reshape(all_slots, local_heads, HD),
            preferred_element_type=jnp.float32,
        )
        / root_size
    )
    weights = jnp.exp(scores - jnp.max(scores, -1, keepdims=True))
    row_total = jnp.sum(weights, -1)
    mixture = jnp.einsum(
        "hqk,khd->qhd",
        weights.astype(jnp.bfloat16),
        head_value.reshape(all_slots, local_heads, HD),
        preferred_element_type=jnp.float32,
    )
    head_result = (
        (mixture / row_total.T[..., None]).astype(jnp.bfloat16).reshape(all_slots, local_heads * HD)
    )
    attended = lax.all_to_all(head_result, "space", split_axis=0, concat_axis=1, tiled=True)
    spatial_out = jnp.dot(attended, spatial_proj, preferred_element_type=jnp.float32).astype(
        jnp.bfloat16
    )
    spread_back = jnp.dot(one_hot, spatial_out, preferred_element_type=jnp.float32)
    after_spatial = (own_rows.astype(jnp.float32) + modulation[2] * spread_back).astype(
        jnp.bfloat16
    )
    by_place = lax.all_to_all(
        after_spatial[None], "frames", split_axis=1, concat_axis=0, tiled=True
    )
    frame_count = by_place.shape[0]
    place_count = by_place.shape[1]
    flat = by_place.reshape(frame_count * place_count, width)
    normed_time = plain_modulate(flat, modulation, 3)
    projected_time = jnp.dot(normed_time, temporal_qkv, preferred_element_type=jnp.float32).astype(
        jnp.bfloat16
    )
    split = projected_time.reshape(frame_count, place_count, 3, inner // HD, HD)
    scores_time = (
        jnp.einsum(
            "flhd,glhd->lhfg", split[:, :, 0], split[:, :, 1], preferred_element_type=jnp.float32
        )
        / root_size
    )
    weights_time = jnp.exp(scores_time - jnp.max(scores_time, -1, keepdims=True))
    total_time = jnp.sum(weights_time, -1)
    mixture_time = (
        jnp.einsum(
            "lhfg,glhd->flhd",
            weights_time.astype(jnp.bfloat16),
            split[:, :, 2],
            preferred_element_type=jnp.float32,
        )
        / total_time.transpose(2, 0, 1)[..., None]
    )
    attended_time = mixture_time.astype(jnp.bfloat16).reshape(frame_count * place_count, inner)
    branch = jnp.dot(attended_time, temporal_proj, preferred_element_type=jnp.float32)
    finished = (
        (flat.astype(jnp.float32) + modulation[5] * branch)
        .astype(jnp.bfloat16)
        .reshape(frame_count, place_count, width)
    )
    return lax.all_to_all(finished, "frames", split_axis=0, concat_axis=1, tiled=True)


def solution(mesh):
    n_frames, n_space = mesh.shape["frames"], mesh.shape["space"]
    placed = (P("frames", "space", None), P("frames", "space"), P(), P(), P(), P(), P())

    def local(latents, *rest):
        fits = latents.shape[1] % (8 * n_frames) == 0 and n_frames & (n_frames - 1) == 0 and n_space & (n_space - 1) == 0
        body = functools.partial(shards, n_frames, n_space) if fits else plain_shards
        return body(latents, *rest)

    return jax.shard_map(local, mesh=mesh, in_specs=placed, out_specs=P("frames", "space", None), check_vma=False)
```

```python
import functools
import math

import jax
import jax.numpy as jnp
from jax import lax
from jax.experimental import pallas as pl
from jax.experimental.pallas import tpu as pltpu
from jax.sharding import PartitionSpec as P

HD = 72
LANES = 128
SUB = 16
F32 = jnp.float32
BF16 = jnp.bfloat16
VMEM = pl.BlockSpec(memory_space=pltpu.VMEM)
HBM = pl.BlockSpec(memory_space=pltpu.HBM)
MIB = 1 << 20
SCALE = math.log2(math.e) / math.sqrt(HD)


def struct(*shape):
    return jax.ShapeDtypeStruct(shape, BF16)


def params(mib):
    return pltpu.CompilerParams(vmem_limit_bytes=mib * MIB)


def layer_norm(values):
    center = values - jnp.mean(values, -1, keepdims=True)
    spread = jnp.mean(center * center, -1, keepdims=True)
    return center * lax.rsqrt(spread + 1e-06)


def dot(left, right):
    return jnp.dot(left, right, preferred_element_type=F32)


def dot_t(left, right):
    return lax.dot_general(left, right, (((1,), (1,)), ((), ())), preferred_element_type=F32)


def packing(rows, width):
    full, rest = divmod(width, LANES)
    free = LANES - rest
    parts = rest // free + 1 if rest and rest % free == 0 else 1
    high = -(-rows // (8 * parts)) * 8
    if rows - high * (parts - 1) <= 0 or parts == 1:
        parts, high = 1, rows
    return full, rest, parts, high


def packed_rows(rows, width):
    full, rest, parts, high = packing(rows, width)
    return -(-(full * rows + (max(parts - 1, 1) * high if rest else 0)) // SUB) * SUB


def pack(block):
    rows, width = block.shape
    full, rest, parts, high = packing(rows, width)
    pieces = [block[:, j * LANES : (j + 1) * LANES] for j in range(full)]
    if rest:
        tail, free = block[:, full * LANES :], LANES - rest
        if parts == 1:
            pieces.append(jnp.concatenate([tail, jnp.zeros((rows, free), block.dtype)], 1))
        else:
            last = tail[(parts - 1) * high :]
            if last.shape[0] < high:
                last = jnp.concatenate([last, jnp.zeros((high - last.shape[0], rest), block.dtype)], 0)
            for i in range(parts - 1):
                side = last[:, i * free : (i + 1) * free]
                pieces.append(jnp.concatenate([tail[i * high : (i + 1) * high], side], 1))
    here = sum(p.shape[0] for p in pieces)
    if here % SUB:
        pieces.append(jnp.zeros((-here % SUB, LANES), block.dtype))
    return jnp.concatenate(pieces, 0)


def unpack(packed, rows, width):
    full, rest, parts, high = packing(rows, width)
    pieces = [packed[j * rows : (j + 1) * rows] for j in range(full)]
    if rest:
        tail = packed[full * rows :]
        if parts == 1:
            pieces.append(tail[:rows, :rest])
        else:
            tiles = [tail[i * high : (i + 1) * high] for i in range(parts - 1)]
            last = jnp.concatenate([t[:, rest:] for t in tiles], 1)[: rows - (parts - 1) * high]
            pieces.append(jnp.concatenate([t[:, :rest] for t in tiles] + [last], 0))
    return jnp.concatenate(pieces, 1)


def merge_kernel(n_space, latents, slot, modulation, weights, out, merged, tokens, slots_in, mods, arrived, sems):
    me = lax.axis_index("space")
    inner = weights.shape[0] // 3
    wide = inner // n_space
    theirs = pl.multiple_of((me ^ (n_space - 1)) * wide, SUB)
    pairs = [(latents, tokens), (slot, slots_in), (modulation, mods)]
    pairs += [(weights.at[pl.ds(j * inner + theirs, wide)], arrived.at[pl.ds(j * wide, wide)]) for j in range(3)]
    copies = [pltpu.make_async_copy(there, here, sems.at[i]) for i, (there, here) in enumerate(pairs)]
    for copy in copies:
        copy.start()
    n_frames, places = latents.shape[:2]
    rows = n_frames * places
    slots = rows // 2
    for copy in copies[:3]:
        copy.wait()
    shift, scale = mods[0:1], 1.0 + mods[1:2]
    normed = jnp.concatenate(
        [layer_norm(tokens[f].astype(F32)) * scale + shift for f in range(n_frames)], 0
    ).astype(BF16)
    local = slots_in[...] - me * slots
    chosen = lax.broadcasted_iota(jnp.int32, (slots, rows), 0) == local
    counts = jnp.sum(chosen.astype(F32), 1, keepdims=True)
    held = (dot(chosen.astype(BF16), normed) / counts).astype(BF16)
    merged[...] = held
    for copy in copies[3:]:
        copy.wait()
    projected = dot_t(arrived[...], held)
    out[...] = pack(jnp.concatenate([projected[:wide] * SCALE, projected[wide:]], 0)).astype(BF16)


def spread_kernel(n_space, merged, weights, *refs):
    outs, (held, arrived, sem) = refs[: n_space - 1], refs[n_space - 1 :]
    copy = pltpu.make_async_copy(weights, arrived, sem)
    copy.start()
    me = lax.axis_index("space")
    inner = weights.shape[0] // 3
    wide = inner // n_space
    copy.wait()
    projected = dot_t(arrived[...], merged[...])
    for j in range(3):
        for d in range(n_space):
            part = projected[j * inner + d * wide : j * inner + (d + 1) * wide]
            held[d, j * wide : (j + 1) * wide] = part * SCALE if j == 0 else part
    for s in range(n_space - 1):
        outs[s][...] = pack(held[me ^ s]).astype(BF16)


def share_kernel(n_pair, latents, keep, give):
    frame = lax.axis_index("frames")
    for s in range(n_pair):
        keep[s] = latents[frame ^ (2 * s)]
        give[s] = latents[frame ^ (2 * s + 1)]


def prepare_kernel(wide, packed, slot, keys, others, chosen):
    slots, rows = keys.shape[0], slot.shape[1]
    local = slot[...] - lax.axis_index("space") * slots
    joined = (lax.broadcasted_iota(jnp.int32, (slots, rows), 0) == local).astype(F32)
    chosen[...] = joined.T.astype(BF16)
    block = unpack(packed[...].astype(F32), 3 * wide, slots)
    keys[...] = block[wide : 2 * wide].T.astype(BF16)
    others[...] = jnp.concatenate([block[:wide], block[2 * wide :]], 0).astype(BF16)


def attend(queries, keys, vals):
    ones = jnp.ones((8, vals.shape[1]), F32)
    results = []
    for h in range(vals.shape[0] // HD):
        at = slice(h * HD, (h + 1) * HD)
        scores = dot(keys[:, at], queries[at].astype(BF16))
        weights = jnp.exp2(scores - jnp.max(scores, 0, keepdims=True)).astype(BF16)
        mixed = dot(jnp.concatenate([vals[at], ones], 0).astype(BF16), weights)
        results.append(mixed[:HD] / mixed[HD : HD + 1])
    return jnp.concatenate(results, 0)


def others_kernel(n_space, slots, wide, far_keys, far_others, *refs):
    ins, outs, (own_queries, all_keys, all_vals) = refs[: n_space - 1], refs[n_space - 1 : -3], refs[-3:]
    blocks = [unpack(r[...].astype(F32), 3 * wide, slots) for r in reversed(ins)]
    others = far_others[...].astype(F32)
    queries = jnp.concatenate([b[:wide] for b in blocks[1:]] + [others[:wide]], 1)
    vals = jnp.concatenate([b[2 * wide :] for b in blocks] + [others[wide:]], 1)
    keys = jnp.concatenate([b[wide : 2 * wide].T.astype(BF16) for b in blocks] + [far_keys[...]], 0)
    own_queries[...] = blocks[0][:wide].astype(BF16)
    all_keys[...] = keys
    all_vals[...] = vals.astype(BF16)
    whole = attend(queries, keys, vals)
    for i, out in enumerate(outs):
        out[...] = pack(whole[:, i * slots : (i + 1) * slots]).astype(BF16)


def own_kernel(queries, keys, vals, out):
    out[...] = attend(queries[...].astype(F32), keys[...], vals[...].astype(F32)).astype(BF16)


def expand_kernel(n_space, n_pair, slots, wide, chosen, *refs):
    ins, (keep, give, attended, held, spread) = refs[:n_space], refs[n_space:]
    me, frame = lax.axis_index("space"), lax.axis_index("frames")
    held[me] = ins[n_space - 1][...].astype(F32)
    for s in range(1, n_space):
        held[me ^ s] = unpack(ins[n_space - 1 - s][...].astype(F32), wide, slots)
    whole = jnp.concatenate([held[d] for d in range(n_space)], 0).astype(BF16)
    attended[...] = whole
    wanted = dot_t(chosen[...], whole)
    places = wanted.shape[0] // (2 * n_pair)
    for f in range(2 * n_pair):
        spread[f] = pack(wanted[f * places : (f + 1) * places]).astype(BF16)
    for s in range(n_pair):
        keep[s] = spread[frame ^ (2 * s)]
        give[s] = spread[frame ^ (2 * s + 1)]


def cost(flops):
    return pl.CostEstimate(flops=flops, bytes_accessed=flops // 100, transcendentals=0)


def residual_kernel(attended, chosen, latents, modulation, proj, after):
    places = latents.shape[1]
    out = dot(attended[...].astype(F32).T.astype(BF16), proj[...]).astype(BF16)
    spread = modulation[2:3] * dot(chosen[...], out)
    for f in range(latents.shape[0]):
        after[f] = (latents[f].astype(F32) + spread[f * places : (f + 1) * places]).astype(BF16)


def pair_kernel(keep, got, *outs):
    for s, out in enumerate(outs):
        out[0] = keep[s]
        out[1] = got[s]


def project_blocks(places, modulation, proj, weights, tokens, results, normed):
    frames = [(s, t) for s in range(len(tokens)) for t in range(2)]
    inner = proj.shape[0]
    attended = [unpack(results[s][t].astype(F32), places, inner) for s, t in frames]
    attended = jnp.concatenate(attended, 0).astype(BF16)
    spatial = dot(attended, proj[...])
    gate, shift, scale = modulation[2:3], modulation[3:4], 1.0 + modulation[4:5]
    for f, (s, t) in enumerate(frames):
        at = slice(f * places, (f + 1) * places)
        normed[at] = layer_norm(tokens[s][t].astype(F32) + gate * spatial[at]) * scale + shift
    projected = dot_t(normed[...].astype(BF16), weights[...])
    space = jnp.zeros((-places % SUB, projected.shape[1]), F32)
    return [
        jnp.concatenate([projected[f * places : (f + 1) * places], space], 0).astype(BF16)
        for f in range(len(frames))
    ]


def project_kernel(places, n_parts, modulation, proj, weights, *refs):
    out, normed = refs[2 * n_parts :]
    blocks = project_blocks(places, modulation, proj, weights, refs[:n_parts], refs[n_parts : 2 * n_parts], normed)
    for f, block in enumerate(blocks):
        out[f] = block


def temporal_kernel(n_pair, places, n_parts, order, modulation, proj, weights, *refs):
    tokens, results, before = refs[:n_parts], refs[n_parts : 2 * n_parts], refs[2 * n_parts : n_pair + n_parts]
    keep, give, normed, held = refs[n_pair + n_parts :]
    n_frames = 2 * n_pair
    groups = -(-places // SUB)
    inner = proj.shape[0]
    heads = inner // HD
    by_frame = [ref[t] for ref in before for t in range(2)]
    by_frame += project_blocks(places, modulation, proj, weights, tokens, results, normed)
    size = n_frames * SUB
    row = lax.broadcasted_iota(jnp.int32, (size, size), 0)
    col = lax.broadcasted_iota(jnp.int32, (size, size), 1)
    same = jnp.concatenate([(row & (SUB - 1)) == (col & (SUB - 1))] * heads, 1)
    for g in range(groups):
        block = jnp.concatenate([b[g * SUB : (g + 1) * SUB] for b in by_frame], 0)

        def part(j, h):
            return block[:, j * inner + h * HD : j * inner + (h + 1) * HD]

        scores = jnp.concatenate([dot_t(part(1, h), part(0, h)) for h in range(heads)], 1)
        scores = jnp.where(same, scores, -jnp.inf)
        mix = jnp.exp2((scores - jnp.max(scores, 0, keepdims=True)) * SCALE)
        total = jnp.sum(mix, 0, keepdims=True)
        mix = mix.astype(BF16)
        vals = block[:, 2 * inner :].astype(F32).T
        mixed = [
            dot(vals[h * HD : (h + 1) * HD].astype(BF16), mix[:, h * size : (h + 1) * size])
            / total[:, h * size : (h + 1) * size]
            for h in range(heads)
        ]
        whole = jnp.concatenate(mixed, 0).T.astype(BF16)
        for f in range(n_frames):
            held[f, g * SUB : (g + 1) * SUB] = whole[f * SUB : (f + 1) * SUB]
    for i, s in enumerate(order):
        keep[s] = pack(held[2 * i].astype(F32)[:places]).astype(BF16)
        give[s] = pack(held[2 * i + 1].astype(F32)[:places]).astype(BF16)


def finish_kernel(taken, places, modulation, proj, after, *refs):
    parts, (out, held, sems) = refs[: len(taken)], refs[-3:]
    frame = lax.axis_index("frames")
    frames = [(s, t) for s in range(len(taken)) for t in range(2)]
    mixed = [unpack(parts[s][t].astype(F32), places, proj.shape[0]) for s, t in frames]
    mixed = jnp.concatenate(mixed, 0).astype(BF16)
    branch = dot(mixed, proj[...])
    gate = modulation[5:6]
    copies = []
    for k, (s, t) in enumerate(frames):
        at = frame ^ (2 * taken[s] + t)
        held[k] = (after[at].astype(F32) + gate * branch[k * places : (k + 1) * places]).astype(BF16)
        copies.append(pltpu.make_async_copy(held.at[k], out.at[at], sems.at[k]))
        copies[-1].start()
    for copy in copies:
        copy.wait()


def swap(block, axis, size, mask):
    return lax.ppermute(block, axis, [(i, i ^ mask) for i in range(size)])


def swaps(blocks, axis, size, step=1):
    moved = {s: swap(blocks[s], axis, size, s * step) for s in range(len(blocks) - 1, 0, -1)}
    return [blocks[0]] + [moved[s] for s in range(1, len(blocks))]


def exchange(keep, give, size):
    got = swap(give, "frames", size, 1)
    both = pl.pallas_call(
        pair_kernel,
        out_shape=[struct(2, *keep.shape[1:])] * (size // 2),
        in_specs=[VMEM] * 2,
        out_specs=[VMEM] * (size // 2),
        compiler_params=params(4),
        name="pair",
    )(keep, got)
    return swaps(both, "frames", size, 2)


def shards(n_frames, n_space, latents, merge_slot, modulation, spatial_qkv, spatial_proj, temporal_qkv, temporal_proj):
    rows, width = latents.shape[1:]
    slots, places = rows // 2, rows // n_frames
    inner = spatial_proj.shape[0]
    wide = inner // n_space
    n_pair = n_frames // 2
    spatial_qkv, temporal_qkv = spatial_qkv.T, temporal_qkv.T
    blocks = latents.reshape(n_frames, places, width)
    sent = packed_rows(3 * wide, slots)
    far, merged = pl.pallas_call(
        functools.partial(merge_kernel, n_space),
        out_shape=[struct(sent, LANES), struct(slots, width)],
        in_specs=[HBM] * 4,
        out_specs=[VMEM] * 2,
        scratch_shapes=[
            pltpu.VMEM(blocks.shape, BF16),
            pltpu.VMEM(merge_slot.shape, jnp.int32),
            pltpu.VMEM(modulation.shape, F32),
            pltpu.VMEM((3 * wide, width), BF16),
            pltpu.SemaphoreType.DMA((6,)),
        ],
        compiler_params=params(57),
        name="merge",
    )(blocks, merge_slot, modulation, spatial_qkv)
    queries = pl.pallas_call(
        functools.partial(spread_kernel, n_space),
        out_shape=[struct(sent, LANES)] * (n_space - 1),
        in_specs=[VMEM, HBM],
        out_specs=[VMEM] * (n_space - 1),
        scratch_shapes=[
            pltpu.VMEM((n_space, 3 * wide, slots), F32),
            pltpu.VMEM(spatial_qkv.shape, BF16),
            pltpu.SemaphoreType.DMA,
        ],
        compiler_params=params(20),
        cost_estimate=cost(2 * slots * 3 * inner * width),
        name="spread",
    )(merged, spatial_qkv)
    shared, merged = lax.optimization_barrier((blocks, merged))
    token_keep, token_give = pl.pallas_call(
        functools.partial(share_kernel, n_pair),
        out_shape=[struct(n_pair, places, width)] * 2,
        in_specs=[VMEM],
        out_specs=[VMEM] * 2,
        compiler_params=params(6),
        name="share",
    )(shared)
    queries = list(queries)
    queries.append(far)
    held = swaps(queries, "space", n_space)
    tokens = exchange(token_keep, token_give, n_frames)
    far_keys, far_others, chosen = pl.pallas_call(
        functools.partial(prepare_kernel, wide),
        out_shape=[struct(slots, wide), struct(2 * wide, slots), struct(rows, slots)],
        in_specs=[VMEM] * 2,
        out_specs=[VMEM] * 3,
        compiler_params=params(4),
        cost_estimate=cost(4 * slots * slots * n_space * n_space * wide),
        name="prepare",
    )(held[-1], merge_slot)
    held = lax.optimization_barrier([far_keys, far_others] + held[-2::-1])
    returned = packed_rows(wide, slots)
    moved = packed_rows(places, inner)
    *results, own_queries, all_keys, all_vals = pl.pallas_call(
        functools.partial(others_kernel, n_space, slots, wide),
        out_shape=[struct(returned, LANES)] * (n_space - 1)
        + [struct(wide, slots), struct(n_space * slots, wide), struct(wide, n_space * slots)],
        in_specs=[VMEM] * (n_space + 1),
        out_specs=[VMEM] * (n_space + 2),
        compiler_params=params(12),
        cost_estimate=cost(4 * slots * slots * n_space * (n_space - 1) * wide),
        name="attend_others",
    )(*held)
    own_queries, tokens = lax.optimization_barrier((own_queries, tokens))
    own = pl.pallas_call(
        own_kernel,
        out_shape=struct(wide, slots),
        in_specs=[VMEM] * 3,
        out_specs=VMEM,
        compiler_params=params(8),
        cost_estimate=cost(4 * slots * slots * n_space * wide),
        name="attend_own",
    )(own_queries, all_keys, all_vals)
    mine = swaps([own] + results, "space", n_space)
    keep, give, attended = pl.pallas_call(
        functools.partial(expand_kernel, n_space, n_pair, slots, wide),
        out_shape=[struct(n_pair, moved, LANES), struct(n_pair, moved, LANES), struct(inner, slots)],
        in_specs=[VMEM] * (n_space + 1),
        out_specs=[VMEM] * 3,
        scratch_shapes=[pltpu.VMEM((n_space, wide, slots), F32), pltpu.VMEM((n_frames, moved, LANES), BF16)],
        compiler_params=params(8),
        name="expand",
    )(chosen, *reversed(mine))
    attended_parts = exchange(keep, give, n_frames)
    after = pl.pallas_call(
        residual_kernel,
        out_shape=struct(n_frames, places, width),
        in_specs=[VMEM] * 5,
        out_specs=VMEM,
        compiler_params=params(10),
        cost_estimate=cost(4 * slots * inner * width),
        name="residual",
    )(attended, chosen, blocks, modulation, spatial_proj)
    pad = -(-places // SUB) * SUB
    order = [0] + list(range(n_pair - 1, 0, -1))
    steps = [order[:1], order[1:2]] if n_pair > 2 else [order[:1]]
    last = order[len(steps) :]
    before = []
    for i, step in enumerate(steps):
        before += [
            pl.pallas_call(
                functools.partial(project_kernel, places, len(step)),
                out_shape=struct(2 * len(step), pad, 3 * inner),
                in_specs=[VMEM] * (3 + 2 * len(step)),
                out_specs=VMEM,
                scratch_shapes=[pltpu.VMEM((2 * len(step) * places, width), F32)],
                compiler_params=params(10),
                cost_estimate=cost(2 * 2 * places * len(step) * 3 * inner * width),
                name="project_%d" % i,
            )(
                modulation,
                spatial_proj,
                temporal_qkv,
                *[tokens[s] for s in step],
                *[attended_parts[s] for s in step],
            )
        ]
    mixed = pl.pallas_call(
        functools.partial(temporal_kernel, n_pair, places, len(last), order),
        out_shape=[struct(n_pair, moved, LANES)] * 2,
        in_specs=[VMEM] * (3 + len(last) + n_pair),
        out_specs=[VMEM] * 2,
        scratch_shapes=[
            pltpu.VMEM((2 * len(last) * places, width), F32),
            pltpu.VMEM((n_frames, pad, inner), BF16),
        ],
        compiler_params=params(16),
        name="temporal",
    )(
        modulation,
        spatial_proj,
        temporal_qkv,
        *[tokens[s] for s in last],
        *[attended_parts[s] for s in last],
        *before,
    )
    mixed_keep, mixed_give = mixed
    parts = exchange(mixed_keep, mixed_give, n_frames)
    out = None
    for i, step in enumerate(([0, n_pair - 1], list(range(n_pair - 2, 0, -1)))):
        if step:
            out = pl.pallas_call(
                functools.partial(finish_kernel, step, places),
                out_shape=struct(n_frames, places, width),
                in_specs=[VMEM] * (3 + len(step)) + ([HBM] if i else []),
                out_specs=HBM,
                scratch_shapes=[
                    pltpu.VMEM((2 * len(step), places, width), BF16),
                    pltpu.SemaphoreType.DMA((2 * len(step),)),
                ],
                input_output_aliases={3 + len(step): 0} if i else {},
                compiler_params=params(10),
                cost_estimate=cost(2 * 2 * places * len(step) * inner * width),
                name="finish_%d" % i,
            )(modulation, temporal_proj, after, *[parts[s] for s in step], *([out] if i else []))
    return out.reshape(1, rows, width)


def plain_modulate(values, modulation, which):
    normed = layer_norm(values.astype(F32))
    return (normed * (1.0 + modulation[which + 1]) + modulation[which]).astype(BF16)


def plain_shards(latents, merge_slot, modulation, spatial_qkv, spatial_proj, temporal_qkv, temporal_proj):
    row_count = latents.shape[1]
    slot_count = row_count // 2
    width = latents.shape[2]
    inner = spatial_proj.shape[0]
    root_size = math.sqrt(HD)
    own_rows = latents[0]
    normed = plain_modulate(own_rows, modulation, 0)
    local_slot = merge_slot[0] - lax.axis_index("space") * slot_count
    one_hot = (local_slot[:, None] == jnp.arange(slot_count, dtype=jnp.int32)[None, :]).astype(
        jnp.bfloat16
    )
    counts = jnp.sum(one_hot.astype(jnp.float32), 0)
    summed = lax.dot_general(
        one_hot, normed, (((0,), (0,)), ((), ())), preferred_element_type=jnp.float32
    )
    merged = (summed / counts[:, None]).astype(jnp.bfloat16)
    projected = jnp.dot(merged, spatial_qkv, preferred_element_type=jnp.float32).astype(
        jnp.bfloat16
    )
    query_rows = projected[:, :inner]
    key_rows = projected[:, inner : 2 * inner]
    value_rows = projected[:, 2 * inner :]
    head_query, head_key, head_value = (
        lax.all_to_all(query_rows, "space", split_axis=1, concat_axis=0, tiled=True),
        lax.all_to_all(key_rows, "space", split_axis=1, concat_axis=0, tiled=True),
        lax.all_to_all(value_rows, "space", split_axis=1, concat_axis=0, tiled=True),
    )
    local_heads = head_query.shape[1] // HD
    all_slots = head_query.shape[0]
    scores = (
        jnp.einsum(
            "qhd,khd->hqk",
            head_query.reshape(all_slots, local_heads, HD),
            head_key.reshape(all_slots, local_heads, HD),
            preferred_element_type=jnp.float32,
        )
        / root_size
    )
    weights = jnp.exp(scores - jnp.max(scores, -1, keepdims=True))
    row_total = jnp.sum(weights, -1)
    mixture = jnp.einsum(
        "hqk,khd->qhd",
        weights.astype(jnp.bfloat16),
        head_value.reshape(all_slots, local_heads, HD),
        preferred_element_type=jnp.float32,
    )
    head_result = (
        (mixture / row_total.T[..., None]).astype(jnp.bfloat16).reshape(all_slots, local_heads * HD)
    )
    attended = lax.all_to_all(head_result, "space", split_axis=0, concat_axis=1, tiled=True)
    spatial_out = jnp.dot(attended, spatial_proj, preferred_element_type=jnp.float32).astype(
        jnp.bfloat16
    )
    spread_back = jnp.dot(one_hot, spatial_out, preferred_element_type=jnp.float32)
    after_spatial = (own_rows.astype(jnp.float32) + modulation[2] * spread_back).astype(
        jnp.bfloat16
    )
    by_place = lax.all_to_all(
        after_spatial[None], "frames", split_axis=1, concat_axis=0, tiled=True
    )
    frame_count = by_place.shape[0]
    place_count = by_place.shape[1]
    flat = by_place.reshape(frame_count * place_count, width)
    normed_time = plain_modulate(flat, modulation, 3)
    projected_time = jnp.dot(normed_time, temporal_qkv, preferred_element_type=jnp.float32).astype(
        jnp.bfloat16
    )
    split = projected_time.reshape(frame_count, place_count, 3, inner // HD, HD)
    scores_time = (
        jnp.einsum(
            "flhd,glhd->lhfg", split[:, :, 0], split[:, :, 1], preferred_element_type=jnp.float32
        )
        / root_size
    )
    weights_time = jnp.exp(scores_time - jnp.max(scores_time, -1, keepdims=True))
    total_time = jnp.sum(weights_time, -1)
    mixture_time = (
        jnp.einsum(
            "lhfg,glhd->flhd",
            weights_time.astype(jnp.bfloat16),
            split[:, :, 2],
            preferred_element_type=jnp.float32,
        )
        / total_time.transpose(2, 0, 1)[..., None]
    )
    attended_time = mixture_time.astype(jnp.bfloat16).reshape(frame_count * place_count, inner)
    branch = jnp.dot(attended_time, temporal_proj, preferred_element_type=jnp.float32)
    finished = (
        (flat.astype(jnp.float32) + modulation[5] * branch)
        .astype(jnp.bfloat16)
        .reshape(frame_count, place_count, width)
    )
    return lax.all_to_all(finished, "frames", split_axis=0, concat_axis=1, tiled=True)


def solution(mesh):
    n_frames, n_space = mesh.shape["frames"], mesh.shape["space"]
    placed = (P("frames", "space", None), P("frames", "space"), P(), P(), P(), P(), P())

    def local(latents, *rest):
        fits = latents.shape[1] % (8 * n_frames) == 0 and n_frames & (n_frames - 1) == 0 and n_space & (n_space - 1) == 0
        body = functools.partial(shards, n_frames, n_space) if fits else plain_shards
        return body(latents, *rest)

    return jax.shard_map(local, mesh=mesh, in_specs=placed, out_specs=P("frames", "space", None), check_vma=False)
```

```python
import functools
import math

import jax
import jax.numpy as jnp
from jax import lax
from jax.experimental import pallas as pl
from jax.experimental.pallas import tpu as pltpu
from jax.sharding import PartitionSpec as P

HD = 72
LANES = 128
SUB = 16
F32 = jnp.float32
BF16 = jnp.bfloat16
VMEM = pl.BlockSpec(memory_space=pltpu.VMEM)
HBM = pl.BlockSpec(memory_space=pltpu.HBM)
MIB = 1 << 20
SCALE = math.log2(math.e) / math.sqrt(HD)


def struct(*shape):
    return jax.ShapeDtypeStruct(shape, BF16)


def params(mib):
    return pltpu.CompilerParams(vmem_limit_bytes=mib * MIB)


def layer_norm(values):
    center = values - jnp.mean(values, -1, keepdims=True)
    spread = jnp.mean(center * center, -1, keepdims=True)
    return center * lax.rsqrt(spread + 1e-06)


def dot(left, right):
    return jnp.dot(left, right, preferred_element_type=F32)


def dot_t(left, right):
    return lax.dot_general(left, right, (((1,), (1,)), ((), ())), preferred_element_type=F32)


def packing(rows, width):
    full, rest = divmod(width, LANES)
    free = LANES - rest
    parts = rest // free + 1 if rest and rest % free == 0 else 1
    high = -(-rows // (8 * parts)) * 8
    if rows - high * (parts - 1) <= 0 or parts == 1:
        parts, high = 1, rows
    return full, rest, parts, high


def packed_rows(rows, width):
    full, rest, parts, high = packing(rows, width)
    return -(-(full * rows + (max(parts - 1, 1) * high if rest else 0)) // 8) * 8


def pack(block):
    rows, width = block.shape
    full, rest, parts, high = packing(rows, width)
    pieces = [block[:, j * LANES : (j + 1) * LANES] for j in range(full)]
    if rest:
        tail, free = block[:, full * LANES :], LANES - rest
        if parts == 1:
            pieces.append(jnp.concatenate([tail, jnp.zeros((rows, free), block.dtype)], 1))
        else:
            last = tail[(parts - 1) * high :]
            if last.shape[0] < high:
                last = jnp.concatenate([last, jnp.zeros((high - last.shape[0], rest), block.dtype)], 0)
            for i in range(parts - 1):
                side = last[:, i * free : (i + 1) * free]
                pieces.append(jnp.concatenate([tail[i * high : (i + 1) * high], side], 1))
    here = sum(p.shape[0] for p in pieces)
    if here % 8:
        pieces.append(jnp.zeros((-here % 8, LANES), block.dtype))
    return jnp.concatenate(pieces, 0)


def unpack(packed, rows, width):
    full, rest, parts, high = packing(rows, width)
    pieces = [packed[j * rows : (j + 1) * rows] for j in range(full)]
    if rest:
        tail = packed[full * rows :]
        if parts == 1:
            pieces.append(tail[:rows, :rest])
        else:
            tiles = [tail[i * high : (i + 1) * high] for i in range(parts - 1)]
            last = jnp.concatenate([t[:, rest:] for t in tiles], 1)[: rows - (parts - 1) * high]
            pieces.append(jnp.concatenate([t[:, :rest] for t in tiles] + [last], 0))
    return jnp.concatenate(pieces, 1)


def merge_kernel(n_space, latents, slot, modulation, weights, out, merged, tokens, slots_in, mods, arrived, sems):
    me = lax.axis_index("space")
    inner = weights.shape[0] // 3
    wide = inner // n_space
    theirs = pl.multiple_of((me ^ (n_space - 1)) * wide, SUB)
    pairs = [(latents, tokens), (slot, slots_in), (modulation, mods)]
    pairs += [(weights.at[pl.ds(j * inner + theirs, wide)], arrived.at[pl.ds(j * wide, wide)]) for j in range(3)]
    copies = [pltpu.make_async_copy(there, here, sems.at[i]) for i, (there, here) in enumerate(pairs)]
    for copy in copies:
        copy.start()
    n_frames, places = latents.shape[:2]
    rows = n_frames * places
    slots = rows // 2
    for copy in copies[:3]:
        copy.wait()
    shift, scale = mods[0:1], 1.0 + mods[1:2]
    normed = jnp.concatenate(
        [layer_norm(tokens[f].astype(F32)) * scale + shift for f in range(n_frames)], 0
    ).astype(BF16)
    local = slots_in[...] - me * slots
    chosen = lax.broadcasted_iota(jnp.int32, (slots, rows), 0) == local
    counts = jnp.sum(chosen.astype(F32), 1, keepdims=True)
    held = (dot(chosen.astype(BF16), normed) / counts).astype(BF16)
    merged[...] = held
    for copy in copies[3:]:
        copy.wait()
    projected = dot_t(arrived[...], held)
    out[...] = pack(jnp.concatenate([projected[:wide] * SCALE, projected[wide:]], 0)).astype(BF16)


def spread_kernel(n_space, merged, weights, *refs):
    outs, (held, arrived, sem) = refs[: n_space - 1], refs[n_space - 1 :]
    copy = pltpu.make_async_copy(weights, arrived, sem)
    copy.start()
    me = lax.axis_index("space")
    inner = weights.shape[0] // 3
    wide = inner // n_space
    copy.wait()
    projected = dot_t(arrived[...], merged[...])
    for j in range(3):
        for d in range(n_space):
            part = projected[j * inner + d * wide : j * inner + (d + 1) * wide]
            held[d, j * wide : (j + 1) * wide] = part * SCALE if j == 0 else part
    for s in range(n_space - 1):
        outs[s][...] = pack(held[me ^ s]).astype(BF16)


def share_kernel(n_pair, latents, keep, give):
    frame = lax.axis_index("frames")
    for s in range(n_pair):
        keep[s] = latents[frame ^ (2 * s)]
        give[s] = latents[frame ^ (2 * s + 1)]


def prepare_kernel(wide, packed, slot, keys, others, chosen):
    slots, rows = keys.shape[0], slot.shape[1]
    local = slot[...] - lax.axis_index("space") * slots
    joined = (lax.broadcasted_iota(jnp.int32, (slots, rows), 0) == local).astype(F32)
    chosen[...] = joined.T.astype(BF16)
    block = unpack(packed[...].astype(F32), 3 * wide, slots)
    keys[...] = block[wide : 2 * wide].T.astype(BF16)
    others[...] = jnp.concatenate([block[:wide], block[2 * wide :]], 0).astype(BF16)


def attend(queries, keys, vals):
    ones = jnp.ones((8, vals.shape[1]), F32)
    results = []
    for h in range(vals.shape[0] // HD):
        at = slice(h * HD, (h + 1) * HD)
        scores = dot(keys[:, at], queries[at].astype(BF16))
        weights = jnp.exp2(scores - jnp.max(scores, 0, keepdims=True)).astype(BF16)
        mixed = dot(jnp.concatenate([vals[at], ones], 0).astype(BF16), weights)
        results.append(mixed[:HD] / mixed[HD : HD + 1])
    return jnp.concatenate(results, 0)


def others_kernel(n_space, slots, wide, far_keys, far_others, *refs):
    ins, outs, (own_queries, all_keys, all_vals) = refs[: n_space - 1], refs[n_space - 1 : -3], refs[-3:]
    blocks = [unpack(r[...].astype(F32), 3 * wide, slots) for r in reversed(ins)]
    others = far_others[...].astype(F32)
    queries = jnp.concatenate([b[:wide] for b in blocks[1:]] + [others[:wide]], 1)
    vals = jnp.concatenate([b[2 * wide :] for b in blocks] + [others[wide:]], 1)
    keys = jnp.concatenate([b[wide : 2 * wide].T.astype(BF16) for b in blocks] + [far_keys[...]], 0)
    own_queries[...] = blocks[0][:wide].astype(BF16)
    all_keys[...] = keys
    all_vals[...] = vals.astype(BF16)
    whole = attend(queries, keys, vals)
    for i, out in enumerate(outs):
        out[...] = pack(whole[:, i * slots : (i + 1) * slots]).astype(BF16)


def own_kernel(queries, keys, vals, out):
    out[...] = attend(queries[...].astype(F32), keys[...], vals[...].astype(F32)).astype(BF16)


def expand_kernel(n_space, n_pair, slots, wide, chosen, *refs):
    ins, (keep, give, attended, held, spread) = refs[:n_space], refs[n_space:]
    me, frame = lax.axis_index("space"), lax.axis_index("frames")
    held[me] = ins[n_space - 1][...].astype(F32)
    for s in range(1, n_space):
        held[me ^ s] = unpack(ins[n_space - 1 - s][...].astype(F32), wide, slots)
    whole = jnp.concatenate([held[d] for d in range(n_space)], 0).astype(BF16)
    attended[...] = whole
    wanted = dot_t(chosen[...], whole)
    places = wanted.shape[0] // (2 * n_pair)
    for f in range(2 * n_pair):
        spread[f] = pack(wanted[f * places : (f + 1) * places]).astype(BF16)
    for s in range(n_pair):
        keep[s] = spread[frame ^ (2 * s)]
        give[s] = spread[frame ^ (2 * s + 1)]


def cost(flops):
    return pl.CostEstimate(flops=flops, bytes_accessed=flops // 100, transcendentals=0)


def residual_kernel(attended, chosen, latents, modulation, proj, after):
    places = latents.shape[1]
    out = dot(attended[...].astype(F32).T.astype(BF16), proj[...]).astype(BF16)
    spread = modulation[2:3] * dot(chosen[...], out)
    for f in range(latents.shape[0]):
        after[f] = (latents[f].astype(F32) + spread[f * places : (f + 1) * places]).astype(BF16)


def pair_kernel(keep, got, *outs):
    for s, out in enumerate(outs):
        out[0] = keep[s]
        out[1] = got[s]


def project_blocks(places, modulation, proj, weights, tokens, results, normed):
    frames = [(s, t) for s in range(len(tokens)) for t in range(2)]
    inner = proj.shape[0]
    attended = [unpack(results[s][t].astype(F32), places, inner) for s, t in frames]
    attended = jnp.concatenate(attended, 0).astype(BF16)
    spatial = dot(attended, proj[...])
    gate, shift, scale = modulation[2:3], modulation[3:4], 1.0 + modulation[4:5]
    for f, (s, t) in enumerate(frames):
        at = slice(f * places, (f + 1) * places)
        normed[at] = layer_norm(tokens[s][t].astype(F32) + gate * spatial[at]) * scale + shift
    projected = dot_t(normed[...].astype(BF16), weights[...])
    space = jnp.zeros((-places % SUB, projected.shape[1]), F32)
    return [
        jnp.concatenate([projected[f * places : (f + 1) * places], space], 0).astype(BF16)
        for f in range(len(frames))
    ]


def project_kernel(places, n_parts, modulation, proj, weights, *refs):
    out, normed = refs[2 * n_parts :]
    blocks = project_blocks(places, modulation, proj, weights, refs[:n_parts], refs[n_parts : 2 * n_parts], normed)
    for f, block in enumerate(blocks):
        out[f] = block


def temporal_kernel(n_pair, places, n_parts, order, modulation, proj, weights, *refs):
    tokens, results, before = refs[:n_parts], refs[n_parts : 2 * n_parts], refs[2 * n_parts : n_pair + n_parts]
    keep, give, normed, held = refs[n_pair + n_parts :]
    n_frames = 2 * n_pair
    groups = -(-places // SUB)
    inner = proj.shape[0]
    heads = inner // HD
    by_frame = [ref[t] for ref in before for t in range(2)]
    by_frame += project_blocks(places, modulation, proj, weights, tokens, results, normed)
    size = n_frames * SUB
    row = lax.broadcasted_iota(jnp.int32, (size, size), 0)
    col = lax.broadcasted_iota(jnp.int32, (size, size), 1)
    same = jnp.concatenate([(row & (SUB - 1)) == (col & (SUB - 1))] * (heads * groups), 1)
    blocks = [jnp.concatenate([b[g * SUB : (g + 1) * SUB] for b in by_frame], 0) for g in range(groups)]
    scores = [
        dot_t(block[:, inner + h * HD : inner + (h + 1) * HD], block[:, h * HD : (h + 1) * HD])
        for block in blocks
        for h in range(heads)
    ]
    scores = jnp.where(same, jnp.concatenate(scores, 1), -jnp.inf)
    mix = jnp.exp2((scores - jnp.max(scores, 0, keepdims=True)) * SCALE)
    total = jnp.sum(mix, 0, keepdims=True)
    mix = mix.astype(BF16)
    mixed = []
    for g, block in enumerate(blocks):
        vals = block[:, 2 * inner :].astype(F32).T
        parts = []
        for h in range(heads):
            at = slice((g * heads + h) * size, (g * heads + h + 1) * size)
            parts.append(dot(vals[h * HD : (h + 1) * HD].astype(BF16), mix[:, at]) / total[:, at])
        mixed.append(jnp.concatenate(parts, 0))
    whole = jnp.concatenate(mixed, 1).T.astype(BF16)
    for g in range(groups):
        for f in range(n_frames):
            at = g * size + f * SUB
            held[f, g * SUB : (g + 1) * SUB] = whole[at : at + SUB]
    for i, s in enumerate(order):
        keep[s] = pack(held[2 * i].astype(F32)[:places]).astype(BF16)
        give[s] = pack(held[2 * i + 1].astype(F32)[:places]).astype(BF16)


def finish_kernel(taken, places, modulation, proj, after, *refs):
    parts, (out, held, sems) = refs[: len(taken)], refs[-3:]
    frame = lax.axis_index("frames")
    frames = [(s, t) for s in range(len(taken)) for t in range(2)]
    mixed = [unpack(parts[s][t].astype(F32), places, proj.shape[0]) for s, t in frames]
    mixed = jnp.concatenate(mixed, 0).astype(BF16)
    branch = dot(mixed, proj[...])
    gate = modulation[5:6]
    copies = []
    for k, (s, t) in enumerate(frames):
        at = frame ^ (2 * taken[s] + t)
        held[k] = (after[at].astype(F32) + gate * branch[k * places : (k + 1) * places]).astype(BF16)
        copies.append(pltpu.make_async_copy(held.at[k], out.at[at], sems.at[k]))
        copies[-1].start()
    for copy in copies:
        copy.wait()


def swap(block, axis, size, mask):
    return lax.ppermute(block, axis, [(i, i ^ mask) for i in range(size)])


def swaps(blocks, axis, size, step=1):
    moved = {s: swap(blocks[s], axis, size, s * step) for s in range(len(blocks) - 1, 0, -1)}
    return [blocks[0]] + [moved[s] for s in range(1, len(blocks))]


def exchange(keep, give, size):
    got = swap(give, "frames", size, 1)
    both = pl.pallas_call(
        pair_kernel,
        out_shape=[struct(2, *keep.shape[1:])] * (size // 2),
        in_specs=[VMEM] * 2,
        out_specs=[VMEM] * (size // 2),
        compiler_params=params(4),
        name="pair",
    )(keep, got)
    return swaps(both, "frames", size, 2)


def shards(n_frames, n_space, latents, merge_slot, modulation, spatial_qkv, spatial_proj, temporal_qkv, temporal_proj):
    rows, width = latents.shape[1:]
    slots, places = rows // 2, rows // n_frames
    inner = spatial_proj.shape[0]
    wide = inner // n_space
    n_pair = n_frames // 2
    spatial_qkv, temporal_qkv = spatial_qkv.T, temporal_qkv.T
    blocks = latents.reshape(n_frames, places, width)
    sent = packed_rows(3 * wide, slots)
    far, merged = pl.pallas_call(
        functools.partial(merge_kernel, n_space),
        out_shape=[struct(sent, LANES), struct(slots, width)],
        in_specs=[HBM] * 4,
        out_specs=[VMEM] * 2,
        scratch_shapes=[
            pltpu.VMEM(blocks.shape, BF16),
            pltpu.VMEM(merge_slot.shape, jnp.int32),
            pltpu.VMEM(modulation.shape, F32),
            pltpu.VMEM((3 * wide, width), BF16),
            pltpu.SemaphoreType.DMA((6,)),
        ],
        compiler_params=params(57),
        name="merge",
    )(blocks, merge_slot, modulation, spatial_qkv)
    queries = pl.pallas_call(
        functools.partial(spread_kernel, n_space),
        out_shape=[struct(sent, LANES)] * (n_space - 1),
        in_specs=[VMEM, HBM],
        out_specs=[VMEM] * (n_space - 1),
        scratch_shapes=[
            pltpu.VMEM((n_space, 3 * wide, slots), F32),
            pltpu.VMEM(spatial_qkv.shape, BF16),
            pltpu.SemaphoreType.DMA,
        ],
        compiler_params=params(20),
        cost_estimate=cost(2 * slots * 3 * inner * width),
        name="spread",
    )(merged, spatial_qkv)
    shared, merged = lax.optimization_barrier((blocks, merged))
    token_keep, token_give = pl.pallas_call(
        functools.partial(share_kernel, n_pair),
        out_shape=[struct(n_pair, places, width)] * 2,
        in_specs=[VMEM],
        out_specs=[VMEM] * 2,
        compiler_params=params(6),
        name="share",
    )(shared)
    queries = list(queries)
    queries.append(far)
    held = swaps(queries, "space", n_space)
    tokens = exchange(token_keep, token_give, n_frames)
    far_keys, far_others, chosen = pl.pallas_call(
        functools.partial(prepare_kernel, wide),
        out_shape=[struct(slots, wide), struct(2 * wide, slots), struct(rows, slots)],
        in_specs=[VMEM] * 2,
        out_specs=[VMEM] * 3,
        compiler_params=params(4),
        cost_estimate=cost(4 * slots * slots * n_space * n_space * wide),
        name="prepare",
    )(held[-1], merge_slot)
    held = lax.optimization_barrier([far_keys, far_others] + held[-2::-1])
    returned = packed_rows(wide, slots)
    moved = packed_rows(places, inner)
    *results, own_queries, all_keys, all_vals = pl.pallas_call(
        functools.partial(others_kernel, n_space, slots, wide),
        out_shape=[struct(returned, LANES)] * (n_space - 1)
        + [struct(wide, slots), struct(n_space * slots, wide), struct(wide, n_space * slots)],
        in_specs=[VMEM] * (n_space + 1),
        out_specs=[VMEM] * (n_space + 2),
        compiler_params=params(12),
        cost_estimate=cost(4 * slots * slots * n_space * (n_space - 1) * wide),
        name="attend_others",
    )(*held)
    own_queries, tokens = lax.optimization_barrier((own_queries, tokens))
    own = pl.pallas_call(
        own_kernel,
        out_shape=struct(wide, slots),
        in_specs=[VMEM] * 3,
        out_specs=VMEM,
        compiler_params=params(8),
        cost_estimate=cost(4 * slots * slots * n_space * wide),
        name="attend_own",
    )(own_queries, all_keys, all_vals)
    mine = swaps([own] + results, "space", n_space)
    keep, give, attended = pl.pallas_call(
        functools.partial(expand_kernel, n_space, n_pair, slots, wide),
        out_shape=[struct(n_pair, moved, LANES), struct(n_pair, moved, LANES), struct(inner, slots)],
        in_specs=[VMEM] * (n_space + 1),
        out_specs=[VMEM] * 3,
        scratch_shapes=[pltpu.VMEM((n_space, wide, slots), F32), pltpu.VMEM((n_frames, moved, LANES), BF16)],
        compiler_params=params(8),
        name="expand",
    )(chosen, *reversed(mine))
    attended_parts = exchange(keep, give, n_frames)
    after = pl.pallas_call(
        residual_kernel,
        out_shape=struct(n_frames, places, width),
        in_specs=[VMEM] * 5,
        out_specs=VMEM,
        compiler_params=params(10),
        cost_estimate=cost(4 * slots * inner * width),
        name="residual",
    )(attended, chosen, blocks, modulation, spatial_proj)
    pad = -(-places // SUB) * SUB
    order = [0] + list(range(n_pair - 1, 0, -1))
    steps = [order[:1], order[1:2]] if n_pair > 2 else [order[:1]]
    last = order[len(steps) :]
    before = []
    for i, step in enumerate(steps):
        before += [
            pl.pallas_call(
                functools.partial(project_kernel, places, len(step)),
                out_shape=struct(2 * len(step), pad, 3 * inner),
                in_specs=[VMEM] * (3 + 2 * len(step)),
                out_specs=VMEM,
                scratch_shapes=[pltpu.VMEM((2 * len(step) * places, width), F32)],
                compiler_params=params(10),
                cost_estimate=cost(2 * 2 * places * len(step) * 3 * inner * width),
                name="project_%d" % i,
            )(
                modulation,
                spatial_proj,
                temporal_qkv,
                *[tokens[s] for s in step],
                *[attended_parts[s] for s in step],
            )
        ]
    mixed = pl.pallas_call(
        functools.partial(temporal_kernel, n_pair, places, len(last), order),
        out_shape=[struct(n_pair, moved, LANES)] * 2,
        in_specs=[VMEM] * (3 + len(last) + n_pair),
        out_specs=[VMEM] * 2,
        scratch_shapes=[
            pltpu.VMEM((2 * len(last) * places, width), F32),
            pltpu.VMEM((n_frames, pad, inner), BF16),
        ],
        compiler_params=params(16),
        name="temporal",
    )(
        modulation,
        spatial_proj,
        temporal_qkv,
        *[tokens[s] for s in last],
        *[attended_parts[s] for s in last],
        *before,
    )
    mixed_keep, mixed_give = mixed
    parts = exchange(mixed_keep, mixed_give, n_frames)
    out = None
    for i, step in enumerate(([0, n_pair - 1], list(range(n_pair - 2, 0, -1)))):
        if step:
            out = pl.pallas_call(
                functools.partial(finish_kernel, step, places),
                out_shape=struct(n_frames, places, width),
                in_specs=[VMEM] * (3 + len(step)) + ([HBM] if i else []),
                out_specs=HBM,
                scratch_shapes=[
                    pltpu.VMEM((2 * len(step), places, width), BF16),
                    pltpu.SemaphoreType.DMA((2 * len(step),)),
                ],
                input_output_aliases={3 + len(step): 0} if i else {},
                compiler_params=params(10),
                cost_estimate=cost(2 * 2 * places * len(step) * inner * width),
                name="finish_%d" % i,
            )(modulation, temporal_proj, after, *[parts[s] for s in step], *([out] if i else []))
    return out.reshape(1, rows, width)


def plain_modulate(values, modulation, which):
    normed = layer_norm(values.astype(F32))
    return (normed * (1.0 + modulation[which + 1]) + modulation[which]).astype(BF16)


def plain_shards(latents, merge_slot, modulation, spatial_qkv, spatial_proj, temporal_qkv, temporal_proj):
    row_count = latents.shape[1]
    slot_count = row_count // 2
    width = latents.shape[2]
    inner = spatial_proj.shape[0]
    root_size = math.sqrt(HD)
    own_rows = latents[0]
    normed = plain_modulate(own_rows, modulation, 0)
    local_slot = merge_slot[0] - lax.axis_index("space") * slot_count
    one_hot = (local_slot[:, None] == jnp.arange(slot_count, dtype=jnp.int32)[None, :]).astype(
        jnp.bfloat16
    )
    counts = jnp.sum(one_hot.astype(jnp.float32), 0)
    summed = lax.dot_general(
        one_hot, normed, (((0,), (0,)), ((), ())), preferred_element_type=jnp.float32
    )
    merged = (summed / counts[:, None]).astype(jnp.bfloat16)
    projected = jnp.dot(merged, spatial_qkv, preferred_element_type=jnp.float32).astype(
        jnp.bfloat16
    )
    query_rows = projected[:, :inner]
    key_rows = projected[:, inner : 2 * inner]
    value_rows = projected[:, 2 * inner :]
    head_query, head_key, head_value = (
        lax.all_to_all(query_rows, "space", split_axis=1, concat_axis=0, tiled=True),
        lax.all_to_all(key_rows, "space", split_axis=1, concat_axis=0, tiled=True),
        lax.all_to_all(value_rows, "space", split_axis=1, concat_axis=0, tiled=True),
    )
    local_heads = head_query.shape[1] // HD
    all_slots = head_query.shape[0]
    scores = (
        jnp.einsum(
            "qhd,khd->hqk",
            head_query.reshape(all_slots, local_heads, HD),
            head_key.reshape(all_slots, local_heads, HD),
            preferred_element_type=jnp.float32,
        )
        / root_size
    )
    weights = jnp.exp(scores - jnp.max(scores, -1, keepdims=True))
    row_total = jnp.sum(weights, -1)
    mixture = jnp.einsum(
        "hqk,khd->qhd",
        weights.astype(jnp.bfloat16),
        head_value.reshape(all_slots, local_heads, HD),
        preferred_element_type=jnp.float32,
    )
    head_result = (
        (mixture / row_total.T[..., None]).astype(jnp.bfloat16).reshape(all_slots, local_heads * HD)
    )
    attended = lax.all_to_all(head_result, "space", split_axis=0, concat_axis=1, tiled=True)
    spatial_out = jnp.dot(attended, spatial_proj, preferred_element_type=jnp.float32).astype(
        jnp.bfloat16
    )
    spread_back = jnp.dot(one_hot, spatial_out, preferred_element_type=jnp.float32)
    after_spatial = (own_rows.astype(jnp.float32) + modulation[2] * spread_back).astype(
        jnp.bfloat16
    )
    by_place = lax.all_to_all(
        after_spatial[None], "frames", split_axis=1, concat_axis=0, tiled=True
    )
    frame_count = by_place.shape[0]
    place_count = by_place.shape[1]
    flat = by_place.reshape(frame_count * place_count, width)
    normed_time = plain_modulate(flat, modulation, 3)
    projected_time = jnp.dot(normed_time, temporal_qkv, preferred_element_type=jnp.float32).astype(
        jnp.bfloat16
    )
    split = projected_time.reshape(frame_count, place_count, 3, inner // HD, HD)
    scores_time = (
        jnp.einsum(
            "flhd,glhd->lhfg", split[:, :, 0], split[:, :, 1], preferred_element_type=jnp.float32
        )
        / root_size
    )
    weights_time = jnp.exp(scores_time - jnp.max(scores_time, -1, keepdims=True))
    total_time = jnp.sum(weights_time, -1)
    mixture_time = (
        jnp.einsum(
            "lhfg,glhd->flhd",
            weights_time.astype(jnp.bfloat16),
            split[:, :, 2],
            preferred_element_type=jnp.float32,
        )
        / total_time.transpose(2, 0, 1)[..., None]
    )
    attended_time = mixture_time.astype(jnp.bfloat16).reshape(frame_count * place_count, inner)
    branch = jnp.dot(attended_time, temporal_proj, preferred_element_type=jnp.float32)
    finished = (
        (flat.astype(jnp.float32) + modulation[5] * branch)
        .astype(jnp.bfloat16)
        .reshape(frame_count, place_count, width)
    )
    return lax.all_to_all(finished, "frames", split_axis=0, concat_axis=1, tiled=True)


def solution(mesh):
    n_frames, n_space = mesh.shape["frames"], mesh.shape["space"]
    placed = (P("frames", "space", None), P("frames", "space"), P(), P(), P(), P(), P())

    def local(latents, *rest):
        fits = latents.shape[1] % (8 * n_frames) == 0 and n_frames & (n_frames - 1) == 0 and n_space & (n_space - 1) == 0
        body = functools.partial(shards, n_frames, n_space) if fits else plain_shards
        return body(latents, *rest)

    return jax.shard_map(local, mesh=mesh, in_specs=placed, out_specs=P("frames", "space", None), check_vma=False)
```

```python
import functools
import math

import jax
import jax.numpy as jnp
from jax import lax
from jax.experimental import pallas as pl
from jax.experimental.pallas import tpu as pltpu
from jax.sharding import PartitionSpec as P

HD = 72
LANES = 128
SUB = 16
F32 = jnp.float32
BF16 = jnp.bfloat16
VMEM = pl.BlockSpec(memory_space=pltpu.VMEM)
HBM = pl.BlockSpec(memory_space=pltpu.HBM)
MIB = 1 << 20
SCALE = math.log2(math.e) / math.sqrt(HD)


def struct(*shape):
    return jax.ShapeDtypeStruct(shape, BF16)


def params(mib):
    return pltpu.CompilerParams(vmem_limit_bytes=mib * MIB)


def layer_norm(values):
    center = values - jnp.mean(values, -1, keepdims=True)
    spread = jnp.mean(center * center, -1, keepdims=True)
    return center * lax.rsqrt(spread + 1e-06)


def dot(left, right):
    return jnp.dot(left, right, preferred_element_type=F32)


def dot_t(left, right):
    return lax.dot_general(left, right, (((1,), (1,)), ((), ())), preferred_element_type=F32)


def packing(rows, width):
    full, rest = divmod(width, LANES)
    free = LANES - rest
    parts = rest // free + 1 if rest and rest % free == 0 else 1
    high = -(-rows // (8 * parts)) * 8
    if rows - high * (parts - 1) <= 0 or parts == 1:
        parts, high = 1, rows
    return full, rest, parts, high


def packed_rows(rows, width):
    full, rest, parts, high = packing(rows, width)
    return -(-(full * rows + (max(parts - 1, 1) * high if rest else 0)) // 8) * 8


def pack(block):
    rows, width = block.shape
    full, rest, parts, high = packing(rows, width)
    pieces = [block[:, j * LANES : (j + 1) * LANES] for j in range(full)]
    if rest:
        tail, free = block[:, full * LANES :], LANES - rest
        if parts == 1:
            pieces.append(jnp.concatenate([tail, jnp.zeros((rows, free), block.dtype)], 1))
        else:
            last = tail[(parts - 1) * high :]
            if last.shape[0] < high:
                last = jnp.concatenate([last, jnp.zeros((high - last.shape[0], rest), block.dtype)], 0)
            for i in range(parts - 1):
                side = last[:, i * free : (i + 1) * free]
                pieces.append(jnp.concatenate([tail[i * high : (i + 1) * high], side], 1))
    here = sum(p.shape[0] for p in pieces)
    if here % 8:
        pieces.append(jnp.zeros((-here % 8, LANES), block.dtype))
    return jnp.concatenate(pieces, 0)


def unpack(packed, rows, width):
    full, rest, parts, high = packing(rows, width)
    pieces = [packed[j * rows : (j + 1) * rows] for j in range(full)]
    if rest:
        tail = packed[full * rows :]
        if parts == 1:
            pieces.append(tail[:rows, :rest])
        else:
            tiles = [tail[i * high : (i + 1) * high] for i in range(parts - 1)]
            last = jnp.concatenate([t[:, rest:] for t in tiles], 1)[: rows - (parts - 1) * high]
            pieces.append(jnp.concatenate([t[:, :rest] for t in tiles] + [last], 0))
    return jnp.concatenate(pieces, 1)


def merge_kernel(n_space, latents, slot, modulation, weights, out, merged, tokens, slots_in, mods, arrived, sems):
    me = lax.axis_index("space")
    inner = weights.shape[0] // 3
    wide = inner // n_space
    theirs = pl.multiple_of((me ^ (n_space - 1)) * wide, SUB)
    pairs = [(latents, tokens), (slot, slots_in), (modulation, mods)]
    pairs += [(weights.at[pl.ds(j * inner + theirs, wide)], arrived.at[pl.ds(j * wide, wide)]) for j in range(3)]
    copies = [pltpu.make_async_copy(there, here, sems.at[i]) for i, (there, here) in enumerate(pairs)]
    for copy in copies:
        copy.start()
    n_frames, places = latents.shape[:2]
    rows = n_frames * places
    slots = rows // 2
    for copy in copies[:3]:
        copy.wait()
    shift, scale = mods[0:1], 1.0 + mods[1:2]
    normed = jnp.concatenate(
        [layer_norm(tokens[f].astype(F32)) * scale + shift for f in range(n_frames)], 0
    ).astype(BF16)
    local = slots_in[...] - me * slots
    chosen = lax.broadcasted_iota(jnp.int32, (slots, rows), 0) == local
    counts = jnp.sum(chosen.astype(F32), 1, keepdims=True)
    held = (dot(chosen.astype(BF16), normed) / counts).astype(BF16)
    merged[...] = held
    for copy in copies[3:]:
        copy.wait()
    projected = dot_t(arrived[...], held)
    out[...] = pack(jnp.concatenate([projected[:wide] * SCALE, projected[wide:]], 0)).astype(BF16)


def spread_kernel(n_space, merged, weights, *refs):
    outs, (held, arrived, sem) = refs[: n_space - 1], refs[n_space - 1 :]
    copy = pltpu.make_async_copy(weights, arrived, sem)
    copy.start()
    me = lax.axis_index("space")
    inner = weights.shape[0] // 3
    wide = inner // n_space
    copy.wait()
    projected = dot_t(arrived[...], merged[...])
    for j in range(3):
        for d in range(n_space):
            part = projected[j * inner + d * wide : j * inner + (d + 1) * wide]
            held[d, j * wide : (j + 1) * wide] = part * SCALE if j == 0 else part
    for s in range(n_space - 1):
        outs[s][...] = pack(held[me ^ s]).astype(BF16)


def share_kernel(n_pair, latents, keep, give):
    frame = lax.axis_index("frames")
    for s in range(n_pair):
        keep[s] = latents[frame ^ (2 * s)]
        give[s] = latents[frame ^ (2 * s + 1)]


def prepare_kernel(wide, packed, slot, keys, others, chosen):
    slots, rows = keys.shape[0], slot.shape[1]
    local = slot[...] - lax.axis_index("space") * slots
    joined = (lax.broadcasted_iota(jnp.int32, (slots, rows), 0) == local).astype(F32).T
    n_frames, places = chosen.shape[:2]
    for f in range(n_frames):
        chosen[lax.axis_index("frames") ^ f] = joined[f * places : (f + 1) * places]
    block = unpack(packed[...].astype(F32), 3 * wide, slots)
    keys[...] = block[wide : 2 * wide].T.astype(BF16)
    others[...] = jnp.concatenate([block[:wide], block[2 * wide :]], 0).astype(BF16)


def attend(queries, keys, vals):
    ones = jnp.ones((8, vals.shape[1]), F32)
    results = []
    for h in range(vals.shape[0] // HD):
        at = slice(h * HD, (h + 1) * HD)
        scores = dot(keys[:, at], queries[at].astype(BF16))
        weights = jnp.exp2(scores - jnp.max(scores, 0, keepdims=True)).astype(BF16)
        mixed = dot(jnp.concatenate([vals[at], ones], 0).astype(BF16), weights)
        results.append(mixed[:HD] / mixed[HD : HD + 1])
    return jnp.concatenate(results, 0)


def others_kernel(n_space, slots, wide, far_keys, far_others, *refs):
    ins, outs, (own_queries, all_keys, all_vals) = refs[: n_space - 1], refs[n_space - 1 : -3], refs[-3:]
    blocks = [unpack(r[...].astype(F32), 3 * wide, slots) for r in reversed(ins)]
    others = far_others[...].astype(F32)
    queries = jnp.concatenate([b[:wide] for b in blocks[1:]] + [others[:wide]], 1)
    vals = jnp.concatenate([b[2 * wide :] for b in blocks] + [others[wide:]], 1)
    keys = jnp.concatenate([b[wide : 2 * wide].T.astype(BF16) for b in blocks] + [far_keys[...]], 0)
    own_queries[...] = blocks[0][:wide].astype(BF16)
    all_keys[...] = keys
    all_vals[...] = vals.astype(BF16)
    whole = attend(queries, keys, vals)
    for i, out in enumerate(outs):
        out[...] = pack(whole[:, i * slots : (i + 1) * slots]).astype(BF16)


def own_kernel(queries, keys, vals, out):
    out[...] = attend(queries[...].astype(F32), keys[...], vals[...].astype(F32)).astype(BF16)


def expand_kernel(n_space, n_pair, slots, wide, chosen, *refs):
    ins, (keep, give, attended, held) = refs[:n_space], refs[n_space:]
    me = lax.axis_index("space")
    held[me] = ins[n_space - 1][...].astype(F32)
    for s in range(1, n_space):
        held[me ^ s] = unpack(ins[n_space - 1 - s][...].astype(F32), wide, slots)
    whole = jnp.concatenate([held[d] for d in range(n_space)], 0).astype(BF16)
    attended[...] = whole
    places = chosen.shape[1]
    wanted = dot_t(jnp.concatenate([chosen[r] for r in range(2 * n_pair)], 0).astype(BF16), whole)
    for s in range(n_pair):
        for t, out in enumerate((keep, give)):
            at = (2 * s + t) * places
            out[s] = pack(wanted[at : at + places]).astype(BF16)


def cost(flops):
    return pl.CostEstimate(flops=flops, bytes_accessed=flops // 100, transcendentals=0)


def residual_kernel(attended, chosen, latents, modulation, proj, after):
    places = latents.shape[1]
    out = dot(attended[...].astype(F32).T.astype(BF16), proj[...]).astype(BF16)
    n_frames = latents.shape[0]
    picked = jnp.concatenate([chosen[r] for r in range(n_frames)], 0).astype(BF16)
    spread = modulation[2:3] * dot(picked, out)
    for r in range(n_frames):
        f = lax.axis_index("frames") ^ r
        after[f] = (latents[f].astype(F32) + spread[r * places : (r + 1) * places]).astype(BF16)


def pair_kernel(keep, got, *outs):
    for s, out in enumerate(outs):
        out[0] = keep[s]
        out[1] = got[s]


def project_blocks(places, modulation, proj, weights, tokens, results, normed):
    frames = [(s, t) for s in range(len(tokens)) for t in range(2)]
    inner = proj.shape[0]
    attended = [unpack(results[s][t].astype(F32), places, inner) for s, t in frames]
    attended = jnp.concatenate(attended, 0).astype(BF16)
    spatial = dot(attended, proj[...])
    gate, shift, scale = modulation[2:3], modulation[3:4], 1.0 + modulation[4:5]
    for f, (s, t) in enumerate(frames):
        at = slice(f * places, (f + 1) * places)
        normed[at] = layer_norm(tokens[s][t].astype(F32) + gate * spatial[at]) * scale + shift
    projected = dot_t(normed[...].astype(BF16), weights[...])
    space = jnp.zeros((-places % SUB, projected.shape[1]), F32)
    return [
        jnp.concatenate([projected[f * places : (f + 1) * places], space], 0).astype(BF16)
        for f in range(len(frames))
    ]


def project_kernel(places, n_parts, modulation, proj, weights, *refs):
    out, normed = refs[2 * n_parts :]
    blocks = project_blocks(places, modulation, proj, weights, refs[:n_parts], refs[n_parts : 2 * n_parts], normed)
    for f, block in enumerate(blocks):
        out[f] = block


def temporal_kernel(n_pair, places, n_parts, order, modulation, proj, weights, *refs):
    tokens, results, before = refs[:n_parts], refs[n_parts : 2 * n_parts], refs[2 * n_parts : n_pair + n_parts]
    keep, give, normed = refs[n_pair + n_parts :]
    n_frames = 2 * n_pair
    groups = -(-places // SUB)
    inner = proj.shape[0]
    heads = inner // HD
    by_frame = [ref[t] for ref in before for t in range(2)]
    by_frame += project_blocks(places, modulation, proj, weights, tokens, results, normed)
    size = n_frames * SUB
    row = lax.broadcasted_iota(jnp.int32, (size, size), 0)
    col = lax.broadcasted_iota(jnp.int32, (size, size), 1)
    same = jnp.concatenate([(row & (SUB - 1)) == (col & (SUB - 1))] * (heads * groups), 1)
    blocks = [jnp.concatenate([b[g * SUB : (g + 1) * SUB] for b in by_frame], 0) for g in range(groups)]
    scores = [
        dot_t(block[:, inner + h * HD : inner + (h + 1) * HD], block[:, h * HD : (h + 1) * HD])
        for block in blocks
        for h in range(heads)
    ]
    scores = jnp.where(same, jnp.concatenate(scores, 1), -jnp.inf)
    mix = jnp.exp2((scores - jnp.max(scores, 0, keepdims=True)) * SCALE)
    total = jnp.sum(mix, 0, keepdims=True)
    mix = mix.astype(BF16)
    mixed = []
    for g, block in enumerate(blocks):
        vals = block[:, 2 * inner :].astype(F32).T
        parts = []
        for h in range(heads):
            at = slice((g * heads + h) * size, (g * heads + h + 1) * size)
            parts.append(dot(vals[h * HD : (h + 1) * HD].astype(BF16), mix[:, at]) / total[:, at])
        mixed.append(jnp.concatenate(parts, 0))
    whole = jnp.concatenate(mixed, 1).T
    for i, s in enumerate(order):
        for out, f in ((keep, 2 * i), (give, 2 * i + 1)):
            rows = [whole[g * size + f * SUB : g * size + (f + 1) * SUB] for g in range(groups)]
            out[s] = pack(jnp.concatenate(rows, 0)[:places]).astype(BF16)


def finish_kernel(taken, places, modulation, proj, after, *refs):
    parts, (out, held, sems) = refs[: len(taken)], refs[-3:]
    frame = lax.axis_index("frames")
    frames = [(s, t) for s in range(len(taken)) for t in range(2)]
    mixed = [unpack(parts[s][t].astype(F32), places, proj.shape[0]) for s, t in frames]
    mixed = jnp.concatenate(mixed, 0).astype(BF16)
    branch = dot(mixed, proj[...])
    gate = modulation[5:6]
    copies = []
    for k, (s, t) in enumerate(frames):
        at = frame ^ (2 * taken[s] + t)
        held[k] = (after[at].astype(F32) + gate * branch[k * places : (k + 1) * places]).astype(BF16)
        copies.append(pltpu.make_async_copy(held.at[k], out.at[at], sems.at[k]))
        copies[-1].start()
    for copy in copies:
        copy.wait()


def swap(block, axis, size, mask):
    return lax.ppermute(block, axis, [(i, i ^ mask) for i in range(size)])


def swaps(blocks, axis, size, step=1):
    moved = {s: swap(blocks[s], axis, size, s * step) for s in range(len(blocks) - 1, 0, -1)}
    return [blocks[0]] + [moved[s] for s in range(1, len(blocks))]


def exchange(keep, give, size):
    got = swap(give, "frames", size, 1)
    both = pl.pallas_call(
        pair_kernel,
        out_shape=[struct(2, *keep.shape[1:])] * (size // 2),
        in_specs=[VMEM] * 2,
        out_specs=[VMEM] * (size // 2),
        compiler_params=params(4),
        name="pair",
    )(keep, got)
    return swaps(both, "frames", size, 2)


def shards(n_frames, n_space, latents, merge_slot, modulation, spatial_qkv, spatial_proj, temporal_qkv, temporal_proj):
    rows, width = latents.shape[1:]
    slots, places = rows // 2, rows // n_frames
    inner = spatial_proj.shape[0]
    wide = inner // n_space
    n_pair = n_frames // 2
    spatial_qkv, temporal_qkv = spatial_qkv.T, temporal_qkv.T
    blocks = latents.reshape(n_frames, places, width)
    sent = packed_rows(3 * wide, slots)
    far, merged = pl.pallas_call(
        functools.partial(merge_kernel, n_space),
        out_shape=[struct(sent, LANES), struct(slots, width)],
        in_specs=[HBM] * 4,
        out_specs=[VMEM] * 2,
        scratch_shapes=[
            pltpu.VMEM(blocks.shape, BF16),
            pltpu.VMEM(merge_slot.shape, jnp.int32),
            pltpu.VMEM(modulation.shape, F32),
            pltpu.VMEM((3 * wide, width), BF16),
            pltpu.SemaphoreType.DMA((6,)),
        ],
        compiler_params=params(57),
        name="merge",
    )(blocks, merge_slot, modulation, spatial_qkv)
    queries = pl.pallas_call(
        functools.partial(spread_kernel, n_space),
        out_shape=[struct(sent, LANES)] * (n_space - 1),
        in_specs=[VMEM, HBM],
        out_specs=[VMEM] * (n_space - 1),
        scratch_shapes=[
            pltpu.VMEM((n_space, 3 * wide, slots), F32),
            pltpu.VMEM(spatial_qkv.shape, BF16),
            pltpu.SemaphoreType.DMA,
        ],
        compiler_params=params(20),
        cost_estimate=cost(2 * slots * 3 * inner * width),
        name="spread",
    )(merged, spatial_qkv)
    shared, merged = lax.optimization_barrier((blocks, merged))
    token_keep, token_give = pl.pallas_call(
        functools.partial(share_kernel, n_pair),
        out_shape=[struct(n_pair, places, width)] * 2,
        in_specs=[VMEM],
        out_specs=[VMEM] * 2,
        compiler_params=params(6),
        name="share",
    )(shared)
    queries = list(queries)
    queries.append(far)
    held = swaps(queries, "space", n_space)
    tokens = exchange(token_keep, token_give, n_frames)
    far_keys, far_others, chosen = pl.pallas_call(
        functools.partial(prepare_kernel, wide),
        out_shape=[struct(slots, wide), struct(2 * wide, slots), jax.ShapeDtypeStruct((n_frames, places, slots), F32)],
        in_specs=[VMEM] * 2,
        out_specs=[VMEM] * 3,
        compiler_params=params(4),
        cost_estimate=cost(4 * slots * slots * n_space * n_space * wide),
        name="prepare",
    )(held[-1], merge_slot)
    held = lax.optimization_barrier([far_keys, far_others] + held[-2::-1])
    returned = packed_rows(wide, slots)
    moved = packed_rows(places, inner)
    *results, own_queries, all_keys, all_vals = pl.pallas_call(
        functools.partial(others_kernel, n_space, slots, wide),
        out_shape=[struct(returned, LANES)] * (n_space - 1)
        + [struct(wide, slots), struct(n_space * slots, wide), struct(wide, n_space * slots)],
        in_specs=[VMEM] * (n_space + 1),
        out_specs=[VMEM] * (n_space + 2),
        compiler_params=params(12),
        cost_estimate=cost(4 * slots * slots * n_space * (n_space - 1) * wide),
        name="attend_others",
    )(*held)
    own_queries, tokens = lax.optimization_barrier((own_queries, tokens))
    own = pl.pallas_call(
        own_kernel,
        out_shape=struct(wide, slots),
        in_specs=[VMEM] * 3,
        out_specs=VMEM,
        compiler_params=params(8),
        cost_estimate=cost(4 * slots * slots * n_space * wide),
        name="attend_own",
    )(own_queries, all_keys, all_vals)
    mine = swaps([own] + results, "space", n_space)
    keep, give, attended = pl.pallas_call(
        functools.partial(expand_kernel, n_space, n_pair, slots, wide),
        out_shape=[struct(n_pair, moved, LANES), struct(n_pair, moved, LANES), struct(inner, slots)],
        in_specs=[VMEM] * (n_space + 1),
        out_specs=[VMEM] * 3,
        scratch_shapes=[pltpu.VMEM((n_space, wide, slots), F32)],
        compiler_params=params(8),
        name="expand",
    )(chosen, *reversed(mine))
    attended_parts = exchange(keep, give, n_frames)
    after = pl.pallas_call(
        residual_kernel,
        out_shape=struct(n_frames, places, width),
        in_specs=[VMEM] * 5,
        out_specs=VMEM,
        compiler_params=params(10),
        cost_estimate=cost(4 * slots * inner * width),
        name="residual",
    )(attended, chosen, blocks, modulation, spatial_proj)
    pad = -(-places // SUB) * SUB
    order = [0] + list(range(n_pair - 1, 0, -1))
    steps = [order[:1], order[1:2]] if n_pair > 2 else [order[:1]]
    last = order[len(steps) :]
    before = []
    for i, step in enumerate(steps):
        before += [
            pl.pallas_call(
                functools.partial(project_kernel, places, len(step)),
                out_shape=struct(2 * len(step), pad, 3 * inner),
                in_specs=[VMEM] * (3 + 2 * len(step)),
                out_specs=VMEM,
                scratch_shapes=[pltpu.VMEM((2 * len(step) * places, width), F32)],
                compiler_params=params(10),
                cost_estimate=cost(2 * 2 * places * len(step) * 3 * inner * width),
                name="project_%d" % i,
            )(
                modulation,
                spatial_proj,
                temporal_qkv,
                *[tokens[s] for s in step],
                *[attended_parts[s] for s in step],
            )
        ]
    mixed = pl.pallas_call(
        functools.partial(temporal_kernel, n_pair, places, len(last), order),
        out_shape=[struct(n_pair, moved, LANES)] * 2,
        in_specs=[VMEM] * (3 + len(last) + n_pair),
        out_specs=[VMEM] * 2,
        scratch_shapes=[pltpu.VMEM((2 * len(last) * places, width), F32)],
        compiler_params=params(16),
        name="temporal",
    )(
        modulation,
        spatial_proj,
        temporal_qkv,
        *[tokens[s] for s in last],
        *[attended_parts[s] for s in last],
        *before,
    )
    mixed_keep, mixed_give = mixed
    parts = exchange(mixed_keep, mixed_give, n_frames)
    out = None
    for i, step in enumerate(([0, n_pair - 1], list(range(n_pair - 2, 0, -1)))):
        if step:
            out = pl.pallas_call(
                functools.partial(finish_kernel, step, places),
                out_shape=struct(n_frames, places, width),
                in_specs=[VMEM] * (3 + len(step)) + ([HBM] if i else []),
                out_specs=HBM,
                scratch_shapes=[
                    pltpu.VMEM((2 * len(step), places, width), BF16),
                    pltpu.SemaphoreType.DMA((2 * len(step),)),
                ],
                input_output_aliases={3 + len(step): 0} if i else {},
                compiler_params=params(10),
                cost_estimate=cost(2 * 2 * places * len(step) * inner * width),
                name="finish_%d" % i,
            )(modulation, temporal_proj, after, *[parts[s] for s in step], *([out] if i else []))
    return out.reshape(1, rows, width)


def plain_modulate(values, modulation, which):
    normed = layer_norm(values.astype(F32))
    return (normed * (1.0 + modulation[which + 1]) + modulation[which]).astype(BF16)


def plain_shards(latents, merge_slot, modulation, spatial_qkv, spatial_proj, temporal_qkv, temporal_proj):
    row_count = latents.shape[1]
    slot_count = row_count // 2
    width = latents.shape[2]
    inner = spatial_proj.shape[0]
    root_size = math.sqrt(HD)
    own_rows = latents[0]
    normed = plain_modulate(own_rows, modulation, 0)
    local_slot = merge_slot[0] - lax.axis_index("space") * slot_count
    one_hot = (local_slot[:, None] == jnp.arange(slot_count, dtype=jnp.int32)[None, :]).astype(
        jnp.bfloat16
    )
    counts = jnp.sum(one_hot.astype(jnp.float32), 0)
    summed = lax.dot_general(
        one_hot, normed, (((0,), (0,)), ((), ())), preferred_element_type=jnp.float32
    )
    merged = (summed / counts[:, None]).astype(jnp.bfloat16)
    projected = jnp.dot(merged, spatial_qkv, preferred_element_type=jnp.float32).astype(
        jnp.bfloat16
    )
    query_rows = projected[:, :inner]
    key_rows = projected[:, inner : 2 * inner]
    value_rows = projected[:, 2 * inner :]
    head_query, head_key, head_value = (
        lax.all_to_all(query_rows, "space", split_axis=1, concat_axis=0, tiled=True),
        lax.all_to_all(key_rows, "space", split_axis=1, concat_axis=0, tiled=True),
        lax.all_to_all(value_rows, "space", split_axis=1, concat_axis=0, tiled=True),
    )
    local_heads = head_query.shape[1] // HD
    all_slots = head_query.shape[0]
    scores = (
        jnp.einsum(
            "qhd,khd->hqk",
            head_query.reshape(all_slots, local_heads, HD),
            head_key.reshape(all_slots, local_heads, HD),
            preferred_element_type=jnp.float32,
        )
        / root_size
    )
    weights = jnp.exp(scores - jnp.max(scores, -1, keepdims=True))
    row_total = jnp.sum(weights, -1)
    mixture = jnp.einsum(
        "hqk,khd->qhd",
        weights.astype(jnp.bfloat16),
        head_value.reshape(all_slots, local_heads, HD),
        preferred_element_type=jnp.float32,
    )
    head_result = (
        (mixture / row_total.T[..., None]).astype(jnp.bfloat16).reshape(all_slots, local_heads * HD)
    )
    attended = lax.all_to_all(head_result, "space", split_axis=0, concat_axis=1, tiled=True)
    spatial_out = jnp.dot(attended, spatial_proj, preferred_element_type=jnp.float32).astype(
        jnp.bfloat16
    )
    spread_back = jnp.dot(one_hot, spatial_out, preferred_element_type=jnp.float32)
    after_spatial = (own_rows.astype(jnp.float32) + modulation[2] * spread_back).astype(
        jnp.bfloat16
    )
    by_place = lax.all_to_all(
        after_spatial[None], "frames", split_axis=1, concat_axis=0, tiled=True
    )
    frame_count = by_place.shape[0]
    place_count = by_place.shape[1]
    flat = by_place.reshape(frame_count * place_count, width)
    normed_time = plain_modulate(flat, modulation, 3)
    projected_time = jnp.dot(normed_time, temporal_qkv, preferred_element_type=jnp.float32).astype(
        jnp.bfloat16
    )
    split = projected_time.reshape(frame_count, place_count, 3, inner // HD, HD)
    scores_time = (
        jnp.einsum(
            "flhd,glhd->lhfg", split[:, :, 0], split[:, :, 1], preferred_element_type=jnp.float32
        )
        / root_size
    )
    weights_time = jnp.exp(scores_time - jnp.max(scores_time, -1, keepdims=True))
    total_time = jnp.sum(weights_time, -1)
    mixture_time = (
        jnp.einsum(
            "lhfg,glhd->flhd",
            weights_time.astype(jnp.bfloat16),
            split[:, :, 2],
            preferred_element_type=jnp.float32,
        )
        / total_time.transpose(2, 0, 1)[..., None]
    )
    attended_time = mixture_time.astype(jnp.bfloat16).reshape(frame_count * place_count, inner)
    branch = jnp.dot(attended_time, temporal_proj, preferred_element_type=jnp.float32)
    finished = (
        (flat.astype(jnp.float32) + modulation[5] * branch)
        .astype(jnp.bfloat16)
        .reshape(frame_count, place_count, width)
    )
    return lax.all_to_all(finished, "frames", split_axis=0, concat_axis=1, tiled=True)


def solution(mesh):
    n_frames, n_space = mesh.shape["frames"], mesh.shape["space"]
    placed = (P("frames", "space", None), P("frames", "space"), P(), P(), P(), P(), P())

    def local(latents, *rest):
        fits = latents.shape[1] % (8 * n_frames) == 0 and n_frames & (n_frames - 1) == 0 and n_space & (n_space - 1) == 0
        body = functools.partial(shards, n_frames, n_space) if fits else plain_shards
        return body(latents, *rest)

    return jax.shard_map(local, mesh=mesh, in_specs=placed, out_specs=P("frames", "space", None), check_vma=False)
```

```python
import functools
import math

import jax
import jax.numpy as jnp
from jax import lax
from jax.experimental import pallas as pl
from jax.experimental.pallas import tpu as pltpu
from jax.sharding import PartitionSpec as P

HD = 72
LANES = 128
SUB = 16
F32 = jnp.float32
BF16 = jnp.bfloat16
VMEM = pl.BlockSpec(memory_space=pltpu.VMEM)
HBM = pl.BlockSpec(memory_space=pltpu.HBM)
MIB = 1 << 20
SCALE = math.log2(math.e) / math.sqrt(HD)


def struct(*shape):
    return jax.ShapeDtypeStruct(shape, BF16)


def params(mib):
    return pltpu.CompilerParams(vmem_limit_bytes=mib * MIB)


def layer_norm(values):
    center = values - jnp.mean(values, -1, keepdims=True)
    spread = jnp.mean(center * center, -1, keepdims=True)
    return center * lax.rsqrt(spread + 1e-06)


def dot(left, right):
    return jnp.dot(left, right, preferred_element_type=F32)


def dot_t(left, right):
    return lax.dot_general(left, right, (((1,), (1,)), ((), ())), preferred_element_type=F32)


def packing(rows, width):
    full, rest = divmod(width, LANES)
    free = LANES - rest
    if not rest:
        return full, rest, []
    count = rest // free if rest % free == 0 else 0
    if count:
        units = -(-rows * count // ((count + 1) * 8))
        heights = [8 * (units // count + (i < units % count)) for i in range(count)]
        if 0 < rows - sum(heights) <= min(heights):
            return full, rest, heights
    return full, rest, [rows]


def packed_rows(rows, width):
    full, _, heights = packing(rows, width)
    return -(-(full * rows + sum(heights)) // 8) * 8


def pack(block):
    rows, width = block.shape
    full, rest, heights = packing(rows, width)
    pieces = [block[:, j * LANES : (j + 1) * LANES] for j in range(full)]
    if rest:
        tail, free, top = block[:, full * LANES :], LANES - rest, 0
        last = tail[sum(heights) :]
        for i, high in enumerate(heights):
            side = [last[:, i * free : (i + 1) * free]] if last.shape[0] else []
            if high > last.shape[0]:
                side.append(jnp.zeros((high - last.shape[0], free), block.dtype))
            side = jnp.concatenate(side, 0) if len(side) > 1 else side[0]
            pieces.append(jnp.concatenate([tail[top : top + high], side], 1))
            top += high
    here = sum(p.shape[0] for p in pieces)
    if here % 8:
        pieces.append(jnp.zeros((-here % 8, LANES), block.dtype))
    return jnp.concatenate(pieces, 0)


def unpack(packed, rows, width):
    full, rest, heights = packing(rows, width)
    pieces = [packed[j * rows : (j + 1) * rows] for j in range(full)]
    if rest:
        tiles, top = [], full * rows
        for high in heights:
            tiles.append(packed[top : top + high])
            top += high
        over = rows - sum(heights)
        parts = [t[:, :rest] for t in tiles]
        if over:
            parts.append(jnp.concatenate([t[:over, rest:] for t in tiles], 1))
        pieces.append(jnp.concatenate(parts, 0) if len(parts) > 1 else parts[0])
    return jnp.concatenate(pieces, 1) if len(pieces) > 1 else pieces[0]


def merge_kernel(n_space, latents, slot, modulation, weights, out, merged, tokens, slots_in, mods, arrived, sems):
    me = lax.axis_index("space")
    inner = weights.shape[0] // 3
    wide = inner // n_space
    theirs = pl.multiple_of((me ^ (n_space - 1)) * wide, SUB)
    pairs = [(latents, tokens), (slot, slots_in), (modulation, mods)]
    pairs += [(weights.at[pl.ds(j * inner + theirs, wide)], arrived.at[pl.ds(j * wide, wide)]) for j in range(3)]
    copies = [pltpu.make_async_copy(there, here, sems.at[i]) for i, (there, here) in enumerate(pairs)]
    for copy in copies:
        copy.start()
    n_frames, places = latents.shape[:2]
    rows = n_frames * places
    slots = rows // 2
    for copy in copies[:3]:
        copy.wait()
    shift, scale = mods[0:1], 1.0 + mods[1:2]
    normed = jnp.concatenate(
        [layer_norm(tokens[f].astype(F32)) * scale + shift for f in range(n_frames)], 0
    ).astype(BF16)
    local = slots_in[...] - me * slots
    chosen = lax.broadcasted_iota(jnp.int32, (slots, rows), 0) == local
    counts = jnp.sum(chosen.astype(F32), 1, keepdims=True)
    held = (dot(chosen.astype(BF16), normed) / counts).astype(BF16)
    merged[...] = held
    for copy in copies[3:]:
        copy.wait()
    projected = dot_t(arrived[...], held)
    out[...] = pack(jnp.concatenate([projected[:wide] * SCALE, projected[wide:]], 0)).astype(BF16)


def spread_kernel(n_space, merged, weights, *refs):
    outs, (held, arrived, sem) = refs[: n_space - 1], refs[n_space - 1 :]
    copy = pltpu.make_async_copy(weights, arrived, sem)
    copy.start()
    me = lax.axis_index("space")
    inner = weights.shape[0] // 3
    wide = inner // n_space
    copy.wait()
    projected = dot_t(arrived[...], merged[...])
    for j in range(3):
        for d in range(n_space):
            part = projected[j * inner + d * wide : j * inner + (d + 1) * wide]
            held[d, j * wide : (j + 1) * wide] = part * SCALE if j == 0 else part
    for s in range(n_space - 1):
        outs[s][...] = pack(held[me ^ s]).astype(BF16)


def share_kernel(n_pair, latents, keep, give):
    frame = lax.axis_index("frames")
    for s in range(n_pair):
        keep[s] = latents[frame ^ (2 * s)]
        give[s] = latents[frame ^ (2 * s + 1)]


def prepare_kernel(wide, packed, slot, keys, others, chosen):
    slots, rows = keys.shape[0], slot.shape[1]
    local = slot[...] - lax.axis_index("space") * slots
    joined = (lax.broadcasted_iota(jnp.int32, (slots, rows), 0) == local).astype(F32).T
    n_frames, places = chosen.shape[:2]
    for f in range(n_frames):
        chosen[lax.axis_index("frames") ^ f] = joined[f * places : (f + 1) * places]
    block = unpack(packed[...].astype(F32), 3 * wide, slots)
    keys[...] = block[wide : 2 * wide].T.astype(BF16)
    others[...] = jnp.concatenate([block[:wide], block[2 * wide :]], 0).astype(BF16)


def attend(queries, keys, vals):
    ones = jnp.ones((8, vals.shape[1]), F32)
    results = []
    for h in range(vals.shape[0] // HD):
        at = slice(h * HD, (h + 1) * HD)
        scores = dot(keys[:, at], queries[at].astype(BF16))
        weights = jnp.exp2(scores - jnp.max(scores, 0, keepdims=True)).astype(BF16)
        mixed = dot(jnp.concatenate([vals[at], ones], 0).astype(BF16), weights)
        results.append(mixed[:HD] / mixed[HD : HD + 1])
    return jnp.concatenate(results, 0)


def others_kernel(n_space, slots, wide, far_keys, far_others, *refs):
    ins, outs, (own_queries, all_keys, all_vals) = refs[: n_space - 1], refs[n_space - 1 : -3], refs[-3:]
    blocks = [unpack(r[...].astype(F32), 3 * wide, slots) for r in reversed(ins)]
    others = far_others[...].astype(F32)
    queries = jnp.concatenate([b[:wide] for b in blocks[1:]] + [others[:wide]], 1)
    vals = jnp.concatenate([b[2 * wide :] for b in blocks] + [others[wide:]], 1)
    keys = jnp.concatenate([b[wide : 2 * wide].T.astype(BF16) for b in blocks] + [far_keys[...]], 0)
    own_queries[...] = blocks[0][:wide].astype(BF16)
    all_keys[...] = keys
    all_vals[...] = vals.astype(BF16)
    whole = attend(queries, keys, vals)
    for i, out in enumerate(outs):
        out[...] = pack(whole[:, i * slots : (i + 1) * slots]).astype(BF16)


def own_kernel(queries, keys, vals, out):
    out[...] = attend(queries[...].astype(F32), keys[...], vals[...].astype(F32)).astype(BF16)


def expand_kernel(n_space, n_pair, slots, wide, chosen, *refs):
    ins, (keep, give, attended, held) = refs[:n_space], refs[n_space:]
    me = lax.axis_index("space")
    held[me] = ins[n_space - 1][...].astype(F32)
    for s in range(1, n_space):
        held[me ^ s] = unpack(ins[n_space - 1 - s][...].astype(F32), wide, slots)
    whole = jnp.concatenate([held[d] for d in range(n_space)], 0).astype(BF16)
    attended[...] = whole
    places = chosen.shape[1]
    wanted = dot_t(jnp.concatenate([chosen[r] for r in range(2 * n_pair)], 0).astype(BF16), whole)
    for s in range(n_pair):
        for t, out in enumerate((keep, give)):
            at = (2 * s + t) * places
            out[s] = pack(wanted[at : at + places]).astype(BF16)


def cost(flops):
    return pl.CostEstimate(flops=flops, bytes_accessed=flops // 100, transcendentals=0)


def residual_kernel(attended, chosen, latents, modulation, proj, after):
    places = latents.shape[1]
    out = dot(attended[...].astype(F32).T.astype(BF16), proj[...]).astype(BF16)
    n_frames = latents.shape[0]
    picked = jnp.concatenate([chosen[r] for r in range(n_frames)], 0).astype(BF16)
    spread = modulation[2:3] * dot(picked, out)
    for r in range(n_frames):
        f = lax.axis_index("frames") ^ r
        after[f] = (latents[f].astype(F32) + spread[r * places : (r + 1) * places]).astype(BF16)


def pair_kernel(keep, got, *outs):
    for s, out in enumerate(outs):
        out[0] = keep[s]
        out[1] = got[s]


def project_blocks(places, modulation, proj, weights, tokens, results, normed):
    frames = [(s, t) for s in range(len(tokens)) for t in range(2)]
    inner = proj.shape[0]
    attended = [unpack(results[s][t].astype(F32), places, inner) for s, t in frames]
    attended = jnp.concatenate(attended, 0).astype(BF16)
    spatial = dot(attended, proj[...])
    gate, shift, scale = modulation[2:3], modulation[3:4], 1.0 + modulation[4:5]
    for f, (s, t) in enumerate(frames):
        at = slice(f * places, (f + 1) * places)
        normed[at] = layer_norm(tokens[s][t].astype(F32) + gate * spatial[at]) * scale + shift
    projected = dot_t(normed[...].astype(BF16), weights[...])
    space = jnp.zeros((-places % SUB, projected.shape[1]), F32)
    return [
        jnp.concatenate([projected[f * places : (f + 1) * places], space], 0).astype(BF16)
        for f in range(len(frames))
    ]


def project_kernel(places, n_parts, modulation, proj, weights, *refs):
    out, normed = refs[2 * n_parts :]
    blocks = project_blocks(places, modulation, proj, weights, refs[:n_parts], refs[n_parts : 2 * n_parts], normed)
    for f, block in enumerate(blocks):
        out[f] = block


def temporal_kernel(n_pair, places, n_parts, order, modulation, proj, weights, *refs):
    tokens, results, before = refs[:n_parts], refs[n_parts : 2 * n_parts], refs[2 * n_parts : n_pair + n_parts]
    keep, give, normed = refs[n_pair + n_parts :]
    n_frames = 2 * n_pair
    groups = -(-places // SUB)
    inner = proj.shape[0]
    heads = inner // HD
    by_frame = [ref[t] for ref in before for t in range(2)]
    by_frame += project_blocks(places, modulation, proj, weights, tokens, results, normed)
    size = n_frames * SUB
    row = lax.broadcasted_iota(jnp.int32, (size, size), 0)
    col = lax.broadcasted_iota(jnp.int32, (size, size), 1)
    same = jnp.concatenate([(row & (SUB - 1)) == (col & (SUB - 1))] * (heads * groups), 1)
    blocks = [jnp.concatenate([b[g * SUB : (g + 1) * SUB] for b in by_frame], 0) for g in range(groups)]
    scores = [
        dot_t(block[:, inner + h * HD : inner + (h + 1) * HD], block[:, h * HD : (h + 1) * HD])
        for block in blocks
        for h in range(heads)
    ]
    scores = jnp.where(same, jnp.concatenate(scores, 1), -jnp.inf)
    mix = jnp.exp2((scores - jnp.max(scores, 0, keepdims=True)) * SCALE)
    total = jnp.sum(mix, 0, keepdims=True)
    mix = mix.astype(BF16)
    mixed = []
    for g, block in enumerate(blocks):
        vals = block[:, 2 * inner :].astype(F32).T
        parts = []
        for h in range(heads):
            at = slice((g * heads + h) * size, (g * heads + h + 1) * size)
            parts.append(dot(vals[h * HD : (h + 1) * HD].astype(BF16), mix[:, at]) / total[:, at])
        mixed.append(jnp.concatenate(parts, 0))
    whole = jnp.concatenate(mixed, 1).T
    for i, s in enumerate(order):
        for out, f in ((keep, 2 * i), (give, 2 * i + 1)):
            rows = [whole[g * size + f * SUB : g * size + (f + 1) * SUB] for g in range(groups)]
            out[s] = pack(jnp.concatenate(rows, 0)[:places]).astype(BF16)


def finish_kernel(taken, places, modulation, proj, after, *refs):
    parts, (out, held, sems) = refs[: len(taken)], refs[-3:]
    frame = lax.axis_index("frames")
    frames = [(s, t) for s in range(len(taken)) for t in range(2)]
    mixed = [unpack(parts[s][t].astype(F32), places, proj.shape[0]) for s, t in frames]
    mixed = jnp.concatenate(mixed, 0).astype(BF16)
    branch = dot(mixed, proj[...])
    gate = modulation[5:6]
    copies = []
    for k, (s, t) in enumerate(frames):
        at = frame ^ (2 * taken[s] + t)
        held[k] = (after[at].astype(F32) + gate * branch[k * places : (k + 1) * places]).astype(BF16)
        copies.append(pltpu.make_async_copy(held.at[k], out.at[at], sems.at[k]))
        copies[-1].start()
    for copy in copies:
        copy.wait()


def swap(block, axis, size, mask):
    return lax.ppermute(block, axis, [(i, i ^ mask) for i in range(size)])


def swaps(blocks, axis, size, step=1):
    moved = {s: swap(blocks[s], axis, size, s * step) for s in range(len(blocks) - 1, 0, -1)}
    return [blocks[0]] + [moved[s] for s in range(1, len(blocks))]


def exchange(keep, give, size):
    got = swap(give, "frames", size, 1)
    both = pl.pallas_call(
        pair_kernel,
        out_shape=[struct(2, *keep.shape[1:])] * (size // 2),
        in_specs=[VMEM] * 2,
        out_specs=[VMEM] * (size // 2),
        compiler_params=params(4),
        name="pair",
    )(keep, got)
    return swaps(both, "frames", size, 2)


def shards(n_frames, n_space, latents, merge_slot, modulation, spatial_qkv, spatial_proj, temporal_qkv, temporal_proj):
    rows, width = latents.shape[1:]
    slots, places = rows // 2, rows // n_frames
    inner = spatial_proj.shape[0]
    wide = inner // n_space
    n_pair = n_frames // 2
    spatial_qkv, temporal_qkv = spatial_qkv.T, temporal_qkv.T
    blocks = latents.reshape(n_frames, places, width)
    sent = packed_rows(3 * wide, slots)
    far, merged = pl.pallas_call(
        functools.partial(merge_kernel, n_space),
        out_shape=[struct(sent, LANES), struct(slots, width)],
        in_specs=[HBM] * 4,
        out_specs=[VMEM] * 2,
        scratch_shapes=[
            pltpu.VMEM(blocks.shape, BF16),
            pltpu.VMEM(merge_slot.shape, jnp.int32),
            pltpu.VMEM(modulation.shape, F32),
            pltpu.VMEM((3 * wide, width), BF16),
            pltpu.SemaphoreType.DMA((6,)),
        ],
        compiler_params=params(57),
        name="merge",
    )(blocks, merge_slot, modulation, spatial_qkv)
    queries = pl.pallas_call(
        functools.partial(spread_kernel, n_space),
        out_shape=[struct(sent, LANES)] * (n_space - 1),
        in_specs=[VMEM, HBM],
        out_specs=[VMEM] * (n_space - 1),
        scratch_shapes=[
            pltpu.VMEM((n_space, 3 * wide, slots), F32),
            pltpu.VMEM(spatial_qkv.shape, BF16),
            pltpu.SemaphoreType.DMA,
        ],
        compiler_params=params(20),
        cost_estimate=cost(2 * slots * 3 * inner * width),
        name="spread",
    )(merged, spatial_qkv)
    shared, merged = lax.optimization_barrier((blocks, merged))
    token_keep, token_give = pl.pallas_call(
        functools.partial(share_kernel, n_pair),
        out_shape=[struct(n_pair, places, width)] * 2,
        in_specs=[VMEM],
        out_specs=[VMEM] * 2,
        compiler_params=params(6),
        name="share",
    )(shared)
    queries = list(queries)
    queries.append(far)
    held = swaps(queries, "space", n_space)
    tokens = exchange(token_keep, token_give, n_frames)
    far_keys, far_others, chosen = pl.pallas_call(
        functools.partial(prepare_kernel, wide),
        out_shape=[struct(slots, wide), struct(2 * wide, slots), jax.ShapeDtypeStruct((n_frames, places, slots), F32)],
        in_specs=[VMEM] * 2,
        out_specs=[VMEM] * 3,
        compiler_params=params(4),
        cost_estimate=cost(4 * slots * slots * n_space * n_space * wide),
        name="prepare",
    )(held[-1], merge_slot)
    held = lax.optimization_barrier([far_keys, far_others] + held[-2::-1])
    returned = packed_rows(wide, slots)
    moved = packed_rows(places, inner)
    *results, own_queries, all_keys, all_vals = pl.pallas_call(
        functools.partial(others_kernel, n_space, slots, wide),
        out_shape=[struct(returned, LANES)] * (n_space - 1)
        + [struct(wide, slots), struct(n_space * slots, wide), struct(wide, n_space * slots)],
        in_specs=[VMEM] * (n_space + 1),
        out_specs=[VMEM] * (n_space + 2),
        compiler_params=params(12),
        cost_estimate=cost(4 * slots * slots * n_space * (n_space - 1) * wide),
        name="attend_others",
    )(*held)
    own_queries, tokens = lax.optimization_barrier((own_queries, tokens))
    own = pl.pallas_call(
        own_kernel,
        out_shape=struct(wide, slots),
        in_specs=[VMEM] * 3,
        out_specs=VMEM,
        compiler_params=params(8),
        cost_estimate=cost(4 * slots * slots * n_space * wide),
        name="attend_own",
    )(own_queries, all_keys, all_vals)
    mine = swaps([own] + results, "space", n_space)
    keep, give, attended = pl.pallas_call(
        functools.partial(expand_kernel, n_space, n_pair, slots, wide),
        out_shape=[struct(n_pair, moved, LANES), struct(n_pair, moved, LANES), struct(inner, slots)],
        in_specs=[VMEM] * (n_space + 1),
        out_specs=[VMEM] * 3,
        scratch_shapes=[pltpu.VMEM((n_space, wide, slots), F32)],
        compiler_params=params(8),
        name="expand",
    )(chosen, *reversed(mine))
    attended_parts = exchange(keep, give, n_frames)
    after = pl.pallas_call(
        residual_kernel,
        out_shape=struct(n_frames, places, width),
        in_specs=[VMEM] * 5,
        out_specs=VMEM,
        compiler_params=params(10),
        cost_estimate=cost(4 * slots * inner * width),
        name="residual",
    )(attended, chosen, blocks, modulation, spatial_proj)
    pad = -(-places // SUB) * SUB
    order = [0] + list(range(n_pair - 1, 0, -1))
    steps = [order[:1], order[1:2]] if n_pair > 2 else [order[:1]]
    last = order[len(steps) :]
    before = []
    for i, step in enumerate(steps):
        before += [
            pl.pallas_call(
                functools.partial(project_kernel, places, len(step)),
                out_shape=struct(2 * len(step), pad, 3 * inner),
                in_specs=[VMEM] * (3 + 2 * len(step)),
                out_specs=VMEM,
                scratch_shapes=[pltpu.VMEM((2 * len(step) * places, width), F32)],
                compiler_params=params(10),
                cost_estimate=cost(2 * 2 * places * len(step) * 3 * inner * width),
                name="project_%d" % i,
            )(
                modulation,
                spatial_proj,
                temporal_qkv,
                *[tokens[s] for s in step],
                *[attended_parts[s] for s in step],
            )
        ]
    mixed = pl.pallas_call(
        functools.partial(temporal_kernel, n_pair, places, len(last), order),
        out_shape=[struct(n_pair, moved, LANES)] * 2,
        in_specs=[VMEM] * (3 + len(last) + n_pair),
        out_specs=[VMEM] * 2,
        scratch_shapes=[pltpu.VMEM((2 * len(last) * places, width), F32)],
        compiler_params=params(16),
        name="temporal",
    )(
        modulation,
        spatial_proj,
        temporal_qkv,
        *[tokens[s] for s in last],
        *[attended_parts[s] for s in last],
        *before,
    )
    mixed_keep, mixed_give = mixed
    parts = exchange(mixed_keep, mixed_give, n_frames)
    out = None
    for i, step in enumerate(([0, n_pair - 1], list(range(n_pair - 2, 0, -1)))):
        if step:
            out = pl.pallas_call(
                functools.partial(finish_kernel, step, places),
                out_shape=struct(n_frames, places, width),
                in_specs=[VMEM] * (3 + len(step)) + ([HBM] if i else []),
                out_specs=HBM,
                scratch_shapes=[
                    pltpu.VMEM((2 * len(step), places, width), BF16),
                    pltpu.SemaphoreType.DMA((2 * len(step),)),
                ],
                input_output_aliases={3 + len(step): 0} if i else {},
                compiler_params=params(10),
                cost_estimate=cost(2 * 2 * places * len(step) * inner * width),
                name="finish_%d" % i,
            )(modulation, temporal_proj, after, *[parts[s] for s in step], *([out] if i else []))
    return out.reshape(1, rows, width)


def plain_modulate(values, modulation, which):
    normed = layer_norm(values.astype(F32))
    return (normed * (1.0 + modulation[which + 1]) + modulation[which]).astype(BF16)


def plain_shards(latents, merge_slot, modulation, spatial_qkv, spatial_proj, temporal_qkv, temporal_proj):
    row_count = latents.shape[1]
    slot_count = row_count // 2
    width = latents.shape[2]
    inner = spatial_proj.shape[0]
    root_size = math.sqrt(HD)
    own_rows = latents[0]
    normed = plain_modulate(own_rows, modulation, 0)
    local_slot = merge_slot[0] - lax.axis_index("space") * slot_count
    one_hot = (local_slot[:, None] == jnp.arange(slot_count, dtype=jnp.int32)[None, :]).astype(
        jnp.bfloat16
    )
    counts = jnp.sum(one_hot.astype(jnp.float32), 0)
    summed = lax.dot_general(
        one_hot, normed, (((0,), (0,)), ((), ())), preferred_element_type=jnp.float32
    )
    merged = (summed / counts[:, None]).astype(jnp.bfloat16)
    projected = jnp.dot(merged, spatial_qkv, preferred_element_type=jnp.float32).astype(
        jnp.bfloat16
    )
    query_rows = projected[:, :inner]
    key_rows = projected[:, inner : 2 * inner]
    value_rows = projected[:, 2 * inner :]
    head_query, head_key, head_value = (
        lax.all_to_all(query_rows, "space", split_axis=1, concat_axis=0, tiled=True),
        lax.all_to_all(key_rows, "space", split_axis=1, concat_axis=0, tiled=True),
        lax.all_to_all(value_rows, "space", split_axis=1, concat_axis=0, tiled=True),
    )
    local_heads = head_query.shape[1] // HD
    all_slots = head_query.shape[0]
    scores = (
        jnp.einsum(
            "qhd,khd->hqk",
            head_query.reshape(all_slots, local_heads, HD),
            head_key.reshape(all_slots, local_heads, HD),
            preferred_element_type=jnp.float32,
        )
        / root_size
    )
    weights = jnp.exp(scores - jnp.max(scores, -1, keepdims=True))
    row_total = jnp.sum(weights, -1)
    mixture = jnp.einsum(
        "hqk,khd->qhd",
        weights.astype(jnp.bfloat16),
        head_value.reshape(all_slots, local_heads, HD),
        preferred_element_type=jnp.float32,
    )
    head_result = (
        (mixture / row_total.T[..., None]).astype(jnp.bfloat16).reshape(all_slots, local_heads * HD)
    )
    attended = lax.all_to_all(head_result, "space", split_axis=0, concat_axis=1, tiled=True)
    spatial_out = jnp.dot(attended, spatial_proj, preferred_element_type=jnp.float32).astype(
        jnp.bfloat16
    )
    spread_back = jnp.dot(one_hot, spatial_out, preferred_element_type=jnp.float32)
    after_spatial = (own_rows.astype(jnp.float32) + modulation[2] * spread_back).astype(
        jnp.bfloat16
    )
    by_place = lax.all_to_all(
        after_spatial[None], "frames", split_axis=1, concat_axis=0, tiled=True
    )
    frame_count = by_place.shape[0]
    place_count = by_place.shape[1]
    flat = by_place.reshape(frame_count * place_count, width)
    normed_time = plain_modulate(flat, modulation, 3)
    projected_time = jnp.dot(normed_time, temporal_qkv, preferred_element_type=jnp.float32).astype(
        jnp.bfloat16
    )
    split = projected_time.reshape(frame_count, place_count, 3, inner // HD, HD)
    scores_time = (
        jnp.einsum(
            "flhd,glhd->lhfg", split[:, :, 0], split[:, :, 1], preferred_element_type=jnp.float32
        )
        / root_size
    )
    weights_time = jnp.exp(scores_time - jnp.max(scores_time, -1, keepdims=True))
    total_time = jnp.sum(weights_time, -1)
    mixture_time = (
        jnp.einsum(
            "lhfg,glhd->flhd",
            weights_time.astype(jnp.bfloat16),
            split[:, :, 2],
            preferred_element_type=jnp.float32,
        )
        / total_time.transpose(2, 0, 1)[..., None]
    )
    attended_time = mixture_time.astype(jnp.bfloat16).reshape(frame_count * place_count, inner)
    branch = jnp.dot(attended_time, temporal_proj, preferred_element_type=jnp.float32)
    finished = (
        (flat.astype(jnp.float32) + modulation[5] * branch)
        .astype(jnp.bfloat16)
        .reshape(frame_count, place_count, width)
    )
    return lax.all_to_all(finished, "frames", split_axis=0, concat_axis=1, tiled=True)


def solution(mesh):
    n_frames, n_space = mesh.shape["frames"], mesh.shape["space"]
    placed = (P("frames", "space", None), P("frames", "space"), P(), P(), P(), P(), P())

    def local(latents, *rest):
        fits = latents.shape[1] % (8 * n_frames) == 0 and n_frames & (n_frames - 1) == 0 and n_space & (n_space - 1) == 0
        body = functools.partial(shards, n_frames, n_space) if fits else plain_shards
        return body(latents, *rest)

    return jax.shard_map(local, mesh=mesh, in_specs=placed, out_specs=P("frames", "space", None), check_vma=False)
```

```python
import functools
import math

import jax
import jax.numpy as jnp
from jax import lax
from jax.experimental import pallas as pl
from jax.experimental.pallas import tpu as pltpu
from jax.sharding import PartitionSpec as P

HD = 72
LANES = 128
SUB = 16
F32 = jnp.float32
BF16 = jnp.bfloat16
VMEM = pl.BlockSpec(memory_space=pltpu.VMEM)
HBM = pl.BlockSpec(memory_space=pltpu.HBM)
MIB = 1 << 20
SCALE = math.log2(math.e) / math.sqrt(HD)


def struct(*shape):
    return jax.ShapeDtypeStruct(shape, BF16)


def params(mib):
    return pltpu.CompilerParams(vmem_limit_bytes=mib * MIB)


def layer_norm(values):
    center = values - jnp.mean(values, -1, keepdims=True)
    spread = jnp.mean(center * center, -1, keepdims=True)
    return center * lax.rsqrt(spread + 1e-06)


def dot(left, right):
    return jnp.dot(left, right, preferred_element_type=F32)


def dot_t(left, right):
    return lax.dot_general(left, right, (((1,), (1,)), ((), ())), preferred_element_type=F32)


def packing(rows, width):
    full, rest = divmod(width, LANES)
    free = LANES - rest
    if not rest:
        return full, rest, []
    count = rest // free if rest % free == 0 else 0
    if count:
        units = -(-rows * count // ((count + 1) * 8))
        heights = [8 * (units // count + (i < units % count)) for i in range(count)]
        if 0 < rows - sum(heights) <= min(heights):
            return full, rest, heights
    return full, rest, [rows]


def packed_rows(rows, width):
    full, _, heights = packing(rows, width)
    return -(-(full * rows + sum(heights)) // 8) * 8


def pack(block):
    rows, width = block.shape
    full, rest, heights = packing(rows, width)
    pieces = [block[:, j * LANES : (j + 1) * LANES] for j in range(full)]
    if rest:
        tail, free, top = block[:, full * LANES :], LANES - rest, 0
        last = tail[sum(heights) :]
        for i, high in enumerate(heights):
            side = [last[:, i * free : (i + 1) * free]] if last.shape[0] else []
            if high > last.shape[0]:
                side.append(jnp.zeros((high - last.shape[0], free), block.dtype))
            side = jnp.concatenate(side, 0) if len(side) > 1 else side[0]
            pieces.append(jnp.concatenate([tail[top : top + high], side], 1))
            top += high
    here = sum(p.shape[0] for p in pieces)
    if here % 8:
        pieces.append(jnp.zeros((-here % 8, LANES), block.dtype))
    return jnp.concatenate(pieces, 0)


def unpack(packed, rows, width):
    full, rest, heights = packing(rows, width)
    pieces = [packed[j * rows : (j + 1) * rows] for j in range(full)]
    if rest:
        tiles, top = [], full * rows
        for high in heights:
            tiles.append(packed[top : top + high])
            top += high
        over = rows - sum(heights)
        parts = [t[:, :rest] for t in tiles]
        if over:
            parts.append(jnp.concatenate([t[:over, rest:] for t in tiles], 1))
        pieces.append(jnp.concatenate(parts, 0) if len(parts) > 1 else parts[0])
    return jnp.concatenate(pieces, 1) if len(pieces) > 1 else pieces[0]


def merge_kernel(n_space, latents, slot, modulation, weights, out, merged, tokens, slots_in, mods, arrived, sems):
    me = lax.axis_index("space")
    inner = weights.shape[0] // 3
    wide = inner // n_space
    theirs = pl.multiple_of((me ^ (n_space - 1)) * wide, SUB)
    pairs = [(latents, tokens), (slot, slots_in), (modulation, mods)]
    pairs += [(weights.at[pl.ds(j * inner + theirs, wide)], arrived.at[pl.ds(j * wide, wide)]) for j in range(3)]
    copies = [pltpu.make_async_copy(there, here, sems.at[i]) for i, (there, here) in enumerate(pairs)]
    for copy in copies:
        copy.start()
    n_frames, places = latents.shape[:2]
    rows = n_frames * places
    slots = rows // 2
    for copy in copies[:3]:
        copy.wait()
    shift, scale = mods[0:1], 1.0 + mods[1:2]
    normed = jnp.concatenate(
        [layer_norm(tokens[f].astype(F32)) * scale + shift for f in range(n_frames)], 0
    ).astype(BF16)
    local = slots_in[...] - me * slots
    chosen = lax.broadcasted_iota(jnp.int32, (slots, rows), 0) == local
    counts = jnp.sum(chosen.astype(F32), 1, keepdims=True)
    held = (dot(chosen.astype(BF16), normed) / counts).astype(BF16)
    merged[...] = held
    for copy in copies[3:]:
        copy.wait()
    projected = dot_t(arrived[...], held)
    out[...] = pack(jnp.concatenate([projected[:wide] * SCALE, projected[wide:]], 0)).astype(BF16)


def spread_kernel(n_space, merged, weights, *refs):
    outs, (held, arrived, sem) = refs[: n_space - 1], refs[n_space - 1 :]
    copy = pltpu.make_async_copy(weights, arrived, sem)
    copy.start()
    me = lax.axis_index("space")
    inner = weights.shape[0] // 3
    wide = inner // n_space
    copy.wait()
    projected = dot_t(arrived[...], merged[...])
    for j in range(3):
        for d in range(n_space):
            part = projected[j * inner + d * wide : j * inner + (d + 1) * wide]
            held[d, j * wide : (j + 1) * wide] = part * SCALE if j == 0 else part
    for s in range(n_space - 1):
        outs[s][...] = pack(held[me ^ s]).astype(BF16)


def share_kernel(n_pair, latents, keep, give):
    frame = lax.axis_index("frames")
    for s in range(n_pair):
        keep[s] = latents[frame ^ (2 * s)]
        give[s] = latents[frame ^ (2 * s + 1)]


def prepare_kernel(wide, packed, slot, keys, others, chosen):
    slots, rows = keys.shape[0], slot.shape[1]
    local = slot[...] - lax.axis_index("space") * slots
    joined = (lax.broadcasted_iota(jnp.int32, (slots, rows), 0) == local).astype(F32).T
    n_frames, places = chosen.shape[:2]
    for f in range(n_frames):
        chosen[lax.axis_index("frames") ^ f] = joined[f * places : (f + 1) * places]
    block = unpack(packed[...].astype(F32), 3 * wide, slots)
    keys[...] = block[wide : 2 * wide].T.astype(BF16)
    others[...] = jnp.concatenate([block[:wide], block[2 * wide :]], 0).astype(BF16)


def attend(queries, keys, vals):
    ones = jnp.ones((8, vals.shape[1]), F32)
    results = []
    for h in range(vals.shape[0] // HD):
        at = slice(h * HD, (h + 1) * HD)
        scores = dot(keys[:, at], queries[at].astype(BF16))
        weights = jnp.exp2(scores - jnp.max(scores, 0, keepdims=True)).astype(BF16)
        mixed = dot(jnp.concatenate([vals[at], ones], 0).astype(BF16), weights)
        results.append(mixed[:HD] / mixed[HD : HD + 1])
    return jnp.concatenate(results, 0)


def others_kernel(n_space, slots, wide, far_keys, far_others, *refs):
    ins, outs, (own_queries, all_keys, all_vals) = refs[: n_space - 1], refs[n_space - 1 : -3], refs[-3:]
    blocks = [unpack(r[...].astype(F32), 3 * wide, slots) for r in reversed(ins)]
    others = far_others[...].astype(F32)
    queries = jnp.concatenate([b[:wide] for b in blocks[1:]] + [others[:wide]], 1)
    vals = jnp.concatenate([b[2 * wide :] for b in blocks] + [others[wide:]], 1)
    keys = jnp.concatenate([b[wide : 2 * wide].T.astype(BF16) for b in blocks] + [far_keys[...]], 0)
    own_queries[...] = blocks[0][:wide].astype(BF16)
    all_keys[...] = keys
    all_vals[...] = vals.astype(BF16)
    whole = attend(queries, keys, vals)
    for i, out in enumerate(outs):
        out[...] = pack(whole[:, i * slots : (i + 1) * slots]).astype(BF16)


def own_kernel(queries, keys, vals, out):
    out[...] = attend(queries[...].astype(F32), keys[...], vals[...].astype(F32)).astype(BF16)


def expand_kernel(n_space, n_pair, slots, wide, chosen, *refs):
    ins, (keep, give, same, other, attended, held) = refs[:n_space], refs[n_space:]
    me = lax.axis_index("space")
    held[me] = ins[n_space - 1][...].astype(F32)
    for s in range(1, n_space):
        held[me ^ s] = unpack(ins[n_space - 1 - s][...].astype(F32), wide, slots)
    whole = jnp.concatenate([held[d] for d in range(n_space)], 0).astype(BF16)
    attended[...] = whole
    places = chosen.shape[1]
    wanted = dot_t(jnp.concatenate([chosen[r] for r in range(2 * n_pair)], 0).astype(BF16), whole)
    for s in range(n_pair):
        for t, out in enumerate((keep, give)):
            at = (2 * s + t) * places
            block = pack(wanted[at : at + places]).astype(BF16)
            if s < n_pair - 1:
                out[s] = block
            else:
                (same, other)[t][...] = block


def cost(flops):
    return pl.CostEstimate(flops=flops, bytes_accessed=flops // 100, transcendentals=0)


def residual_kernel(attended, chosen, latents, modulation, proj, after):
    places = latents.shape[1]
    out = dot(attended[...].astype(F32).T.astype(BF16), proj[...]).astype(BF16)
    n_frames = latents.shape[0]
    picked = jnp.concatenate([chosen[r] for r in range(n_frames)], 0).astype(BF16)
    spread = modulation[2:3] * dot(picked, out)
    for r in range(n_frames):
        f = lax.axis_index("frames") ^ r
        after[f] = (latents[f].astype(F32) + spread[r * places : (r + 1) * places]).astype(BF16)


def pair_kernel(keep, got, *outs):
    for s, out in enumerate(outs):
        out[0] = keep[s]
        out[1] = got[s]


def project_blocks(places, modulation, proj, weights, tokens, results, normed):
    frames = [(s, t) for s in range(len(tokens)) for t in range(2)]
    inner = proj.shape[0]
    attended = [unpack(results[s][t][...].astype(F32), places, inner) for s, t in frames]
    attended = jnp.concatenate(attended, 0).astype(BF16)
    spatial = dot(attended, proj[...])
    gate, shift, scale = modulation[2:3], modulation[3:4], 1.0 + modulation[4:5]
    for f, (s, t) in enumerate(frames):
        at = slice(f * places, (f + 1) * places)
        normed[at] = layer_norm(tokens[s][t].astype(F32) + gate * spatial[at]) * scale + shift
    projected = dot_t(normed[...].astype(BF16), weights[...])
    space = jnp.zeros((-places % SUB, projected.shape[1]), F32)
    return [
        jnp.concatenate([projected[f * places : (f + 1) * places], space], 0).astype(BF16)
        for f in range(len(frames))
    ]


def project_kernel(places, n_parts, modulation, proj, weights, *refs):
    out, normed = refs[-2:]
    results = regroup(refs[n_parts:-2], n_parts)
    blocks = project_blocks(places, modulation, proj, weights, refs[:n_parts], results, normed)
    for f, block in enumerate(blocks):
        out[f] = block


def temporal_kernel(n_pair, places, n_parts, order, modulation, proj, weights, *refs):
    tokens, results, before = refs[:n_parts], refs[n_parts : 2 * n_parts], refs[2 * n_parts : n_pair + n_parts]
    keep, give, normed = refs[n_pair + n_parts :]
    n_frames = 2 * n_pair
    groups = -(-places // SUB)
    inner = proj.shape[0]
    heads = inner // HD
    by_frame = [ref[t] for ref in before for t in range(2)]
    by_frame += project_blocks(places, modulation, proj, weights, tokens, results, normed)
    size = n_frames * SUB
    row = lax.broadcasted_iota(jnp.int32, (size, size), 0)
    col = lax.broadcasted_iota(jnp.int32, (size, size), 1)
    same = jnp.concatenate([(row & (SUB - 1)) == (col & (SUB - 1))] * (heads * groups), 1)
    blocks = [jnp.concatenate([b[g * SUB : (g + 1) * SUB] for b in by_frame], 0) for g in range(groups)]
    scores = [
        dot_t(block[:, inner + h * HD : inner + (h + 1) * HD], block[:, h * HD : (h + 1) * HD])
        for block in blocks
        for h in range(heads)
    ]
    scores = jnp.where(same, jnp.concatenate(scores, 1), -jnp.inf)
    mix = jnp.exp2((scores - jnp.max(scores, 0, keepdims=True)) * SCALE)
    total = jnp.sum(mix, 0, keepdims=True)
    mix = mix.astype(BF16)
    mixed = []
    for g, block in enumerate(blocks):
        vals = block[:, 2 * inner :].astype(F32).T
        parts = []
        for h in range(heads):
            at = slice((g * heads + h) * size, (g * heads + h + 1) * size)
            parts.append(dot(vals[h * HD : (h + 1) * HD].astype(BF16), mix[:, at]) / total[:, at])
        mixed.append(jnp.concatenate(parts, 0))
    whole = jnp.concatenate(mixed, 1).T
    for i, s in enumerate(order):
        for out, f in ((keep, 2 * i), (give, 2 * i + 1)):
            rows = [whole[g * size + f * SUB : g * size + (f + 1) * SUB] for g in range(groups)]
            out[s] = pack(jnp.concatenate(rows, 0)[:places]).astype(BF16)


def finish_kernel(taken, places, n_refs, modulation, proj, after, *refs):
    out, held, sems = refs[-3:]
    parts = regroup(refs[:n_refs], len(taken))
    frame = lax.axis_index("frames")
    frames = [(s, t) for s in range(len(taken)) for t in range(2)]
    mixed = [unpack(parts[s][t][...].astype(F32), places, proj.shape[0]) for s, t in frames]
    mixed = jnp.concatenate(mixed, 0).astype(BF16)
    branch = dot(mixed, proj[...])
    gate = modulation[5:6]
    copies = []
    for k, (s, t) in enumerate(frames):
        at = frame ^ (2 * taken[s] + t)
        held[k] = (after[at].astype(F32) + gate * branch[k * places : (k + 1) * places]).astype(BF16)
        copies.append(pltpu.make_async_copy(held.at[k], out.at[at], sems.at[k]))
        copies[-1].start()
    for copy in copies:
        copy.wait()


def swap(block, axis, size, mask):
    return lax.ppermute(block, axis, [(i, i ^ mask) for i in range(size)])


def swaps(blocks, axis, size, step=1):
    moved = {s: swap(blocks[s], axis, size, s * step) for s in range(len(blocks) - 1, 0, -1)}
    return [blocks[0]] + [moved[s] for s in range(1, len(blocks))]


def exchange(keep, give, size):
    got = swap(give, "frames", size, 1)
    both = pl.pallas_call(
        pair_kernel,
        out_shape=[struct(2, *keep.shape[1:])] * keep.shape[0],
        in_specs=[VMEM] * 2,
        out_specs=[VMEM] * keep.shape[0],
        compiler_params=params(4),
        name="pair",
    )(keep, got)
    return swaps(both, "frames", size, 2)


def exchange_apart(keep, give, same, other, size):
    far = size - 2
    straight = [swap(same, "frames", size, far), swap(other, "frames", size, far + 1)]
    return [[both] for both in exchange(keep, give, size)] + [straight]


def regroup(refs, count):
    return list(refs) if len(refs) == count else list(refs[: count - 1]) + [refs[count - 1 :]]


def shards(n_frames, n_space, latents, merge_slot, modulation, spatial_qkv, spatial_proj, temporal_qkv, temporal_proj):
    rows, width = latents.shape[1:]
    slots, places = rows // 2, rows // n_frames
    inner = spatial_proj.shape[0]
    wide = inner // n_space
    n_pair = n_frames // 2
    spatial_qkv, temporal_qkv = spatial_qkv.T, temporal_qkv.T
    blocks = latents.reshape(n_frames, places, width)
    sent = packed_rows(3 * wide, slots)
    far, merged = pl.pallas_call(
        functools.partial(merge_kernel, n_space),
        out_shape=[struct(sent, LANES), struct(slots, width)],
        in_specs=[HBM] * 4,
        out_specs=[VMEM] * 2,
        scratch_shapes=[
            pltpu.VMEM(blocks.shape, BF16),
            pltpu.VMEM(merge_slot.shape, jnp.int32),
            pltpu.VMEM(modulation.shape, F32),
            pltpu.VMEM((3 * wide, width), BF16),
            pltpu.SemaphoreType.DMA((6,)),
        ],
        compiler_params=params(57),
        name="merge",
    )(blocks, merge_slot, modulation, spatial_qkv)
    queries = pl.pallas_call(
        functools.partial(spread_kernel, n_space),
        out_shape=[struct(sent, LANES)] * (n_space - 1),
        in_specs=[VMEM, HBM],
        out_specs=[VMEM] * (n_space - 1),
        scratch_shapes=[
            pltpu.VMEM((n_space, 3 * wide, slots), F32),
            pltpu.VMEM(spatial_qkv.shape, BF16),
            pltpu.SemaphoreType.DMA,
        ],
        compiler_params=params(20),
        cost_estimate=cost(2 * slots * 3 * inner * width),
        name="spread",
    )(merged, spatial_qkv)
    shared, merged = lax.optimization_barrier((blocks, merged))
    token_keep, token_give = pl.pallas_call(
        functools.partial(share_kernel, n_pair),
        out_shape=[struct(n_pair, places, width)] * 2,
        in_specs=[VMEM],
        out_specs=[VMEM] * 2,
        compiler_params=params(6),
        name="share",
    )(shared)
    queries = list(queries)
    queries.append(far)
    held = swaps(queries, "space", n_space)
    tokens = exchange(token_keep, token_give, n_frames)
    far_keys, far_others, chosen = pl.pallas_call(
        functools.partial(prepare_kernel, wide),
        out_shape=[struct(slots, wide), struct(2 * wide, slots), jax.ShapeDtypeStruct((n_frames, places, slots), F32)],
        in_specs=[VMEM] * 2,
        out_specs=[VMEM] * 3,
        compiler_params=params(4),
        cost_estimate=cost(4 * slots * slots * n_space * n_space * wide),
        name="prepare",
    )(held[-1], merge_slot)
    held = lax.optimization_barrier([far_keys, far_others] + held[-2::-1])
    returned = packed_rows(wide, slots)
    moved = packed_rows(places, inner)
    *results, own_queries, all_keys, all_vals = pl.pallas_call(
        functools.partial(others_kernel, n_space, slots, wide),
        out_shape=[struct(returned, LANES)] * (n_space - 1)
        + [struct(wide, slots), struct(n_space * slots, wide), struct(wide, n_space * slots)],
        in_specs=[VMEM] * (n_space + 1),
        out_specs=[VMEM] * (n_space + 2),
        compiler_params=params(12),
        cost_estimate=cost(4 * slots * slots * n_space * (n_space - 1) * wide),
        name="attend_others",
    )(*held)
    own_queries, tokens = lax.optimization_barrier((own_queries, tokens))
    own = pl.pallas_call(
        own_kernel,
        out_shape=struct(wide, slots),
        in_specs=[VMEM] * 3,
        out_specs=VMEM,
        compiler_params=params(8),
        cost_estimate=cost(4 * slots * slots * n_space * wide),
        name="attend_own",
    )(own_queries, all_keys, all_vals)
    mine = swaps([own] + results, "space", n_space)
    apart = [struct(n_pair - 1, moved, LANES)] * 2 + [struct(moved, LANES)] * 2
    *blocks_apart, attended = pl.pallas_call(
        functools.partial(expand_kernel, n_space, n_pair, slots, wide),
        out_shape=apart + [struct(inner, slots)],
        in_specs=[VMEM] * (n_space + 1),
        out_specs=[VMEM] * 5,
        scratch_shapes=[pltpu.VMEM((n_space, wide, slots), F32)],
        compiler_params=params(8),
        name="expand",
    )(chosen, *reversed(mine))
    attended_parts = exchange_apart(*blocks_apart, n_frames)
    after = pl.pallas_call(
        residual_kernel,
        out_shape=struct(n_frames, places, width),
        in_specs=[VMEM] * 5,
        out_specs=VMEM,
        compiler_params=params(10),
        cost_estimate=cost(4 * slots * inner * width),
        name="residual",
    )(attended, chosen, blocks, modulation, spatial_proj)
    pad = -(-places // SUB) * SUB
    order = [0] + list(range(n_pair - 1, 0, -1))
    steps = [order[:1], order[1:2]] if n_pair > 2 else [order[:1]]
    last = order[len(steps) :]
    before = []
    for i, step in enumerate(steps):
        if before:
            s = step[-1]
            attended_parts[s], before = lax.optimization_barrier((attended_parts[s], before))
        before += [
            pl.pallas_call(
                functools.partial(project_kernel, places, len(step)),
                out_shape=struct(2 * len(step), pad, 3 * inner),
                in_specs=[VMEM] * (3 + len(step) + sum(len(attended_parts[s]) for s in step)),
                out_specs=VMEM,
                scratch_shapes=[pltpu.VMEM((2 * len(step) * places, width), F32)],
                compiler_params=params(10),
                cost_estimate=cost((1 + 9 * i) * 2 * 2 * places * len(step) * 3 * inner * width),
                name="project_%d" % i,
            )(
                modulation,
                spatial_proj,
                temporal_qkv,
                *[tokens[s] for s in step],
                *[part for s in step for part in attended_parts[s]],
            )
        ]
    mixed = pl.pallas_call(
        functools.partial(temporal_kernel, n_pair, places, len(last), order),
        out_shape=[struct(n_pair, moved, LANES)] * 2,
        in_specs=[VMEM] * (3 + len(last) + n_pair),
        out_specs=[VMEM] * 2,
        scratch_shapes=[pltpu.VMEM((2 * len(last) * places, width), F32)],
        compiler_params=params(16),
        name="temporal",
    )(
        modulation,
        spatial_proj,
        temporal_qkv,
        *[tokens[s] for s in last],
        *[part for s in last for part in attended_parts[s]],
        *before,
    )
    parts = [[both] for both in exchange(*mixed, n_frames)]
    out = None
    for i, step in enumerate(([0, n_pair - 1], list(range(n_pair - 2, 0, -1)))):
        if step:
            given = [part for s in step for part in parts[s]]
            out = pl.pallas_call(
                functools.partial(finish_kernel, step, places, len(given)),
                out_shape=struct(n_frames, places, width),
                in_specs=[VMEM] * (3 + len(given)) + ([HBM] if i else []),
                out_specs=HBM,
                scratch_shapes=[
                    pltpu.VMEM((2 * len(step), places, width), BF16),
                    pltpu.SemaphoreType.DMA((2 * len(step),)),
                ],
                input_output_aliases={3 + len(given): 0} if i else {},
                compiler_params=params(10),
                cost_estimate=cost(2 * 2 * places * len(step) * inner * width),
                name="finish_%d" % i,
            )(modulation, temporal_proj, after, *given, *([out] if i else []))
    return out.reshape(1, rows, width)


def plain_modulate(values, modulation, which):
    normed = layer_norm(values.astype(F32))
    return (normed * (1.0 + modulation[which + 1]) + modulation[which]).astype(BF16)


def plain_shards(latents, merge_slot, modulation, spatial_qkv, spatial_proj, temporal_qkv, temporal_proj):
    row_count = latents.shape[1]
    slot_count = row_count // 2
    width = latents.shape[2]
    inner = spatial_proj.shape[0]
    root_size = math.sqrt(HD)
    own_rows = latents[0]
    normed = plain_modulate(own_rows, modulation, 0)
    local_slot = merge_slot[0] - lax.axis_index("space") * slot_count
    one_hot = (local_slot[:, None] == jnp.arange(slot_count, dtype=jnp.int32)[None, :]).astype(
        jnp.bfloat16
    )
    counts = jnp.sum(one_hot.astype(jnp.float32), 0)
    summed = lax.dot_general(
        one_hot, normed, (((0,), (0,)), ((), ())), preferred_element_type=jnp.float32
    )
    merged = (summed / counts[:, None]).astype(jnp.bfloat16)
    projected = jnp.dot(merged, spatial_qkv, preferred_element_type=jnp.float32).astype(
        jnp.bfloat16
    )
    query_rows = projected[:, :inner]
    key_rows = projected[:, inner : 2 * inner]
    value_rows = projected[:, 2 * inner :]
    head_query, head_key, head_value = (
        lax.all_to_all(query_rows, "space", split_axis=1, concat_axis=0, tiled=True),
        lax.all_to_all(key_rows, "space", split_axis=1, concat_axis=0, tiled=True),
        lax.all_to_all(value_rows, "space", split_axis=1, concat_axis=0, tiled=True),
    )
    local_heads = head_query.shape[1] // HD
    all_slots = head_query.shape[0]
    scores = (
        jnp.einsum(
            "qhd,khd->hqk",
            head_query.reshape(all_slots, local_heads, HD),
            head_key.reshape(all_slots, local_heads, HD),
            preferred_element_type=jnp.float32,
        )
        / root_size
    )
    weights = jnp.exp(scores - jnp.max(scores, -1, keepdims=True))
    row_total = jnp.sum(weights, -1)
    mixture = jnp.einsum(
        "hqk,khd->qhd",
        weights.astype(jnp.bfloat16),
        head_value.reshape(all_slots, local_heads, HD),
        preferred_element_type=jnp.float32,
    )
    head_result = (
        (mixture / row_total.T[..., None]).astype(jnp.bfloat16).reshape(all_slots, local_heads * HD)
    )
    attended = lax.all_to_all(head_result, "space", split_axis=0, concat_axis=1, tiled=True)
    spatial_out = jnp.dot(attended, spatial_proj, preferred_element_type=jnp.float32).astype(
        jnp.bfloat16
    )
    spread_back = jnp.dot(one_hot, spatial_out, preferred_element_type=jnp.float32)
    after_spatial = (own_rows.astype(jnp.float32) + modulation[2] * spread_back).astype(
        jnp.bfloat16
    )
    by_place = lax.all_to_all(
        after_spatial[None], "frames", split_axis=1, concat_axis=0, tiled=True
    )
    frame_count = by_place.shape[0]
    place_count = by_place.shape[1]
    flat = by_place.reshape(frame_count * place_count, width)
    normed_time = plain_modulate(flat, modulation, 3)
    projected_time = jnp.dot(normed_time, temporal_qkv, preferred_element_type=jnp.float32).astype(
        jnp.bfloat16
    )
    split = projected_time.reshape(frame_count, place_count, 3, inner // HD, HD)
    scores_time = (
        jnp.einsum(
            "flhd,glhd->lhfg", split[:, :, 0], split[:, :, 1], preferred_element_type=jnp.float32
        )
        / root_size
    )
    weights_time = jnp.exp(scores_time - jnp.max(scores_time, -1, keepdims=True))
    total_time = jnp.sum(weights_time, -1)
    mixture_time = (
        jnp.einsum(
            "lhfg,glhd->flhd",
            weights_time.astype(jnp.bfloat16),
            split[:, :, 2],
            preferred_element_type=jnp.float32,
        )
        / total_time.transpose(2, 0, 1)[..., None]
    )
    attended_time = mixture_time.astype(jnp.bfloat16).reshape(frame_count * place_count, inner)
    branch = jnp.dot(attended_time, temporal_proj, preferred_element_type=jnp.float32)
    finished = (
        (flat.astype(jnp.float32) + modulation[5] * branch)
        .astype(jnp.bfloat16)
        .reshape(frame_count, place_count, width)
    )
    return lax.all_to_all(finished, "frames", split_axis=0, concat_axis=1, tiled=True)


def solution(mesh):
    n_frames, n_space = mesh.shape["frames"], mesh.shape["space"]
    placed = (P("frames", "space", None), P("frames", "space"), P(), P(), P(), P(), P())

    def local(latents, *rest):
        fits = n_frames >= 8 and latents.shape[1] % (8 * n_frames) == 0 and n_frames & (n_frames - 1) == 0 and n_space & (n_space - 1) == 0
        body = functools.partial(shards, n_frames, n_space) if fits else plain_shards
        return body(latents, *rest)

    return jax.shard_map(local, mesh=mesh, in_specs=placed, out_specs=P("frames", "space", None), check_vma=False)
```

```python
import functools
import math

import jax
import jax.numpy as jnp
from jax import lax
from jax.experimental import pallas as pl
from jax.experimental.pallas import tpu as pltpu
from jax.sharding import PartitionSpec as P

HD = 72
LANES = 128
SUB = 16
F32 = jnp.float32
BF16 = jnp.bfloat16
VMEM = pl.BlockSpec(memory_space=pltpu.VMEM)
HBM = pl.BlockSpec(memory_space=pltpu.HBM)
MIB = 1 << 20
SCALE = math.log2(math.e) / math.sqrt(HD)


def struct(*shape):
    return jax.ShapeDtypeStruct(shape, BF16)


def params(mib):
    return pltpu.CompilerParams(vmem_limit_bytes=mib * MIB)


def layer_norm(values):
    center = values - jnp.mean(values, -1, keepdims=True)
    spread = jnp.mean(center * center, -1, keepdims=True)
    return center * lax.rsqrt(spread + 1e-06)


def dot(left, right):
    return jnp.dot(left, right, preferred_element_type=F32)


def dot_t(left, right):
    return lax.dot_general(left, right, (((1,), (1,)), ((), ())), preferred_element_type=F32)


def packing(rows, width):
    full, rest = divmod(width, LANES)
    free = LANES - rest
    if not rest:
        return full, rest, []
    count = rest // free if rest % free == 0 else 0
    if count:
        units = -(-rows * count // ((count + 1) * 8))
        heights = [8 * (units // count + (i < units % count)) for i in range(count)]
        if 0 < rows - sum(heights) <= min(heights):
            return full, rest, heights
    return full, rest, [rows]


def packed_rows(rows, width):
    full, _, heights = packing(rows, width)
    return -(-(full * rows + sum(heights)) // 8) * 8


def pack(block):
    rows, width = block.shape
    full, rest, heights = packing(rows, width)
    pieces = [block[:, j * LANES : (j + 1) * LANES] for j in range(full)]
    if rest:
        tail, free, top = block[:, full * LANES :], LANES - rest, 0
        last = tail[sum(heights) :]
        for i, high in enumerate(heights):
            side = [last[:, i * free : (i + 1) * free]] if last.shape[0] else []
            if high > last.shape[0]:
                side.append(jnp.zeros((high - last.shape[0], free), block.dtype))
            side = jnp.concatenate(side, 0) if len(side) > 1 else side[0]
            pieces.append(jnp.concatenate([tail[top : top + high], side], 1))
            top += high
    here = sum(p.shape[0] for p in pieces)
    if here % 8:
        pieces.append(jnp.zeros((-here % 8, LANES), block.dtype))
    return jnp.concatenate(pieces, 0)


def unpack(packed, rows, width):
    full, rest, heights = packing(rows, width)
    pieces = [packed[j * rows : (j + 1) * rows] for j in range(full)]
    if rest:
        tiles, top = [], full * rows
        for high in heights:
            tiles.append(packed[top : top + high])
            top += high
        over = rows - sum(heights)
        parts = [t[:, :rest] for t in tiles]
        if over:
            parts.append(jnp.concatenate([t[:over, rest:] for t in tiles], 1))
        pieces.append(jnp.concatenate(parts, 0) if len(parts) > 1 else parts[0])
    return jnp.concatenate(pieces, 1) if len(pieces) > 1 else pieces[0]


def merge_kernel(n_space, latents, slot, modulation, weights, out, merged, tokens, slots_in, mods, arrived, sems):
    me = lax.axis_index("space")
    inner = weights.shape[0] // 3
    wide = inner // n_space
    theirs = pl.multiple_of((me ^ (n_space - 1)) * wide, SUB)
    pairs = [(latents, tokens), (slot, slots_in), (modulation, mods)]
    pairs += [(weights.at[pl.ds(j * inner + theirs, wide)], arrived.at[pl.ds(j * wide, wide)]) for j in range(3)]
    copies = [pltpu.make_async_copy(there, here, sems.at[i]) for i, (there, here) in enumerate(pairs)]
    for copy in copies:
        copy.start()
    n_frames, places = latents.shape[:2]
    rows = n_frames * places
    slots = rows // 2
    for copy in copies[:3]:
        copy.wait()
    shift, scale = mods[0:1], 1.0 + mods[1:2]
    normed = jnp.concatenate(
        [layer_norm(tokens[f].astype(F32)) * scale + shift for f in range(n_frames)], 0
    ).astype(BF16)
    local = slots_in[...] - me * slots
    chosen = lax.broadcasted_iota(jnp.int32, (slots, rows), 0) == local
    counts = jnp.sum(chosen.astype(F32), 1, keepdims=True)
    held = (dot(chosen.astype(BF16), normed) / counts).astype(BF16)
    merged[...] = held
    for copy in copies[3:]:
        copy.wait()
    projected = dot_t(arrived[...], held)
    out[...] = pack(jnp.concatenate([projected[:wide] * SCALE, projected[wide:]], 0)).astype(BF16)


def spread_kernel(n_space, merged, weights, *refs):
    outs, (held, arrived, sem) = refs[: n_space - 1], refs[n_space - 1 :]
    copy = pltpu.make_async_copy(weights, arrived, sem)
    copy.start()
    me = lax.axis_index("space")
    inner = weights.shape[0] // 3
    wide = inner // n_space
    copy.wait()
    projected = dot_t(arrived[...], merged[...])
    for j in range(3):
        for d in range(n_space):
            part = projected[j * inner + d * wide : j * inner + (d + 1) * wide]
            held[d, j * wide : (j + 1) * wide] = part * SCALE if j == 0 else part
    for s in range(n_space - 1):
        outs[s][...] = pack(held[me ^ s]).astype(BF16)


def share_kernel(n_pair, latents, keep, give):
    frame = lax.axis_index("frames")
    for s in range(n_pair):
        keep[s] = latents[frame ^ (2 * s)]
        give[s] = latents[frame ^ (2 * s + 1)]


def prepare_kernel(wide, packed, slot, keys, others, chosen):
    slots, rows = keys.shape[0], slot.shape[1]
    local = slot[...] - lax.axis_index("space") * slots
    joined = (lax.broadcasted_iota(jnp.int32, (slots, rows), 0) == local).astype(F32).T
    n_frames, places = chosen.shape[:2]
    for f in range(n_frames):
        chosen[lax.axis_index("frames") ^ f] = joined[f * places : (f + 1) * places]
    block = unpack(packed[...].astype(F32), 3 * wide, slots)
    keys[...] = block[wide : 2 * wide].T.astype(BF16)
    others[...] = jnp.concatenate([block[:wide], block[2 * wide :]], 0).astype(BF16)


def attend(queries, keys, vals):
    ones = jnp.ones((8, vals.shape[1]), F32)
    results = []
    for h in range(vals.shape[0] // HD):
        at = slice(h * HD, (h + 1) * HD)
        scores = dot(keys[:, at], queries[at].astype(BF16))
        weights = jnp.exp2(scores - jnp.max(scores, 0, keepdims=True)).astype(BF16)
        mixed = dot(jnp.concatenate([vals[at], ones], 0).astype(BF16), weights)
        results.append(mixed[:HD] / mixed[HD : HD + 1])
    return jnp.concatenate(results, 0)


def others_kernel(n_space, slots, wide, far_keys, far_others, *refs):
    ins, outs, (own_queries, all_keys, all_vals) = refs[: n_space - 1], refs[n_space - 1 : -3], refs[-3:]
    blocks = [unpack(r[...].astype(F32), 3 * wide, slots) for r in reversed(ins)]
    others = far_others[...].astype(F32)
    queries = jnp.concatenate([b[:wide] for b in blocks[1:]] + [others[:wide]], 1)
    vals = jnp.concatenate([b[2 * wide :] for b in blocks] + [others[wide:]], 1)
    keys = jnp.concatenate([b[wide : 2 * wide].T.astype(BF16) for b in blocks] + [far_keys[...]], 0)
    own_queries[...] = blocks[0][:wide].astype(BF16)
    all_keys[...] = keys
    all_vals[...] = vals.astype(BF16)
    whole = attend(queries, keys, vals)
    for i, out in enumerate(outs):
        out[...] = pack(whole[:, i * slots : (i + 1) * slots]).astype(BF16)


def own_kernel(queries, keys, vals, out):
    out[...] = attend(queries[...].astype(F32), keys[...], vals[...].astype(F32)).astype(BF16)


def expand_kernel(n_space, n_pair, slots, wide, chosen, *refs):
    ins, (keep, give, same, other, attended, held) = refs[:n_space], refs[n_space:]
    me = lax.axis_index("space")
    held[me] = ins[n_space - 1][...].astype(F32)
    for s in range(1, n_space):
        held[me ^ s] = unpack(ins[n_space - 1 - s][...].astype(F32), wide, slots)
    whole = jnp.concatenate([held[d] for d in range(n_space)], 0).astype(BF16)
    attended[...] = whole
    places = chosen.shape[1]
    wanted = dot_t(jnp.concatenate([chosen[r] for r in range(2 * n_pair)], 0).astype(BF16), whole)
    for s in range(n_pair):
        for t, out in enumerate((keep, give)):
            at = (2 * s + t) * places
            block = pack(wanted[at : at + places]).astype(BF16)
            if s < n_pair - 1:
                out[s] = block
            else:
                (same, other)[t][...] = block


def cost(flops):
    return pl.CostEstimate(flops=flops, bytes_accessed=flops // 100, transcendentals=0)


def residual_kernel(attended, chosen, latents, modulation, proj, after):
    places = latents.shape[1]
    out = dot(attended[...].astype(F32).T.astype(BF16), proj[...]).astype(BF16)
    n_frames = latents.shape[0]
    picked = jnp.concatenate([chosen[r] for r in range(n_frames)], 0).astype(BF16)
    spread = modulation[2:3] * dot(picked, out)
    for r in range(n_frames):
        f = lax.axis_index("frames") ^ r
        after[f] = (latents[f].astype(F32) + spread[r * places : (r + 1) * places]).astype(BF16)


def pair_kernel(keep, got, *outs):
    for s, out in enumerate(outs):
        out[0] = keep[s]
        out[1] = got[s]


def project_blocks(places, modulation, proj, weights, tokens, results, normed):
    frames = [(s, t) for s in range(len(tokens)) for t in range(2)]
    inner = proj.shape[0]
    attended = [unpack(results[s][t][...].astype(F32), places, inner) for s, t in frames]
    attended = jnp.concatenate(attended, 0).astype(BF16)
    spatial = dot(attended, proj[...])
    gate, shift, scale = modulation[2:3], modulation[3:4], 1.0 + modulation[4:5]
    for f, (s, t) in enumerate(frames):
        at = slice(f * places, (f + 1) * places)
        normed[at] = layer_norm(tokens[s][t].astype(F32) + gate * spatial[at]) * scale + shift
    projected = dot_t(normed[...].astype(BF16), weights[...])
    space = jnp.zeros((-places % SUB, projected.shape[1]), F32)
    return [
        jnp.concatenate([projected[f * places : (f + 1) * places], space], 0).astype(BF16)
        for f in range(len(frames))
    ]


def project_kernel(places, n_parts, modulation, proj, weights, *refs):
    out, normed = refs[-2:]
    results = regroup(refs[n_parts:-2], n_parts)
    blocks = project_blocks(places, modulation, proj, weights, refs[:n_parts], results, normed)
    for f, block in enumerate(blocks):
        out[f] = block


def temporal_kernel(n_pair, places, n_parts, order, modulation, proj, weights, *refs):
    tokens, results, before = refs[:n_parts], refs[n_parts : 2 * n_parts], refs[2 * n_parts : n_pair + n_parts]
    keep, give, alike, other, normed = refs[n_pair + n_parts :]
    n_frames = 2 * n_pair
    groups = -(-places // SUB)
    inner = proj.shape[0]
    heads = inner // HD
    by_frame = [ref[t] for ref in before for t in range(2)]
    by_frame += project_blocks(places, modulation, proj, weights, tokens, results, normed)
    size = n_frames * SUB
    row = lax.broadcasted_iota(jnp.int32, (size, size), 0)
    col = lax.broadcasted_iota(jnp.int32, (size, size), 1)
    same = jnp.concatenate([(row & (SUB - 1)) == (col & (SUB - 1))] * (heads * groups), 1)
    blocks = [jnp.concatenate([b[g * SUB : (g + 1) * SUB] for b in by_frame], 0) for g in range(groups)]
    scores = [
        dot_t(block[:, inner + h * HD : inner + (h + 1) * HD], block[:, h * HD : (h + 1) * HD])
        for block in blocks
        for h in range(heads)
    ]
    scores = jnp.where(same, jnp.concatenate(scores, 1), -jnp.inf)
    mix = jnp.exp2((scores - jnp.max(scores, 0, keepdims=True)) * SCALE)
    total = jnp.sum(mix, 0, keepdims=True)
    mix = mix.astype(BF16)
    mixed = []
    for g, block in enumerate(blocks):
        vals = block[:, 2 * inner :].astype(F32).T
        parts = []
        for h in range(heads):
            at = slice((g * heads + h) * size, (g * heads + h + 1) * size)
            parts.append(dot(vals[h * HD : (h + 1) * HD].astype(BF16), mix[:, at]) / total[:, at])
        mixed.append(jnp.concatenate(parts, 0))
    whole = jnp.concatenate(mixed, 1).T
    for i, s in enumerate(order):
        for out, f in ((keep, 2 * i), (give, 2 * i + 1)):
            rows = [whole[g * size + f * SUB : g * size + (f + 1) * SUB] for g in range(groups)]
            block = pack(jnp.concatenate(rows, 0)[:places]).astype(BF16)
            if s < n_pair - 1:
                out[s] = block
            else:
                (alike if out is keep else other)[...] = block


def finish_kernel(taken, places, n_refs, modulation, proj, after, *refs):
    out, held, sems = refs[-3:]
    parts = regroup(refs[:n_refs], len(taken))
    frame = lax.axis_index("frames")
    frames = [(s, t) for s in range(len(taken)) for t in range(2)]
    mixed = [unpack(parts[s][t][...].astype(F32), places, proj.shape[0]) for s, t in frames]
    mixed = jnp.concatenate(mixed, 0).astype(BF16)
    branch = dot(mixed, proj[...])
    gate = modulation[5:6]
    copies = []
    for k, (s, t) in enumerate(frames):
        at = frame ^ (2 * taken[s] + t)
        held[k] = (after[at].astype(F32) + gate * branch[k * places : (k + 1) * places]).astype(BF16)
        copies.append(pltpu.make_async_copy(held.at[k], out.at[at], sems.at[k]))
        copies[-1].start()
    for copy in copies:
        copy.wait()


def swap(block, axis, size, mask):
    return lax.ppermute(block, axis, [(i, i ^ mask) for i in range(size)])


def swaps(blocks, axis, size, step=1):
    moved = {s: swap(blocks[s], axis, size, s * step) for s in range(len(blocks) - 1, 0, -1)}
    return [blocks[0]] + [moved[s] for s in range(1, len(blocks))]


def exchange(keep, give, size):
    got = swap(give, "frames", size, 1)
    both = pl.pallas_call(
        pair_kernel,
        out_shape=[struct(2, *keep.shape[1:])] * keep.shape[0],
        in_specs=[VMEM] * 2,
        out_specs=[VMEM] * keep.shape[0],
        compiler_params=params(4),
        name="pair",
    )(keep, got)
    return swaps(both, "frames", size, 2)


def exchange_apart(keep, give, same, other, size):
    far = size - 2
    straight = [swap(same, "frames", size, far), swap(other, "frames", size, far + 1)]
    return [[both] for both in exchange(keep, give, size)] + [straight]


def regroup(refs, count):
    return list(refs) if len(refs) == count else list(refs[: count - 1]) + [refs[count - 1 :]]


def shards(n_frames, n_space, latents, merge_slot, modulation, spatial_qkv, spatial_proj, temporal_qkv, temporal_proj):
    rows, width = latents.shape[1:]
    slots, places = rows // 2, rows // n_frames
    inner = spatial_proj.shape[0]
    wide = inner // n_space
    n_pair = n_frames // 2
    spatial_qkv, temporal_qkv = spatial_qkv.T, temporal_qkv.T
    blocks = latents.reshape(n_frames, places, width)
    sent = packed_rows(3 * wide, slots)
    far, merged = pl.pallas_call(
        functools.partial(merge_kernel, n_space),
        out_shape=[struct(sent, LANES), struct(slots, width)],
        in_specs=[HBM] * 4,
        out_specs=[VMEM] * 2,
        scratch_shapes=[
            pltpu.VMEM(blocks.shape, BF16),
            pltpu.VMEM(merge_slot.shape, jnp.int32),
            pltpu.VMEM(modulation.shape, F32),
            pltpu.VMEM((3 * wide, width), BF16),
            pltpu.SemaphoreType.DMA((6,)),
        ],
        compiler_params=params(57),
        name="merge",
    )(blocks, merge_slot, modulation, spatial_qkv)
    queries = pl.pallas_call(
        functools.partial(spread_kernel, n_space),
        out_shape=[struct(sent, LANES)] * (n_space - 1),
        in_specs=[VMEM, HBM],
        out_specs=[VMEM] * (n_space - 1),
        scratch_shapes=[
            pltpu.VMEM((n_space, 3 * wide, slots), F32),
            pltpu.VMEM(spatial_qkv.shape, BF16),
            pltpu.SemaphoreType.DMA,
        ],
        compiler_params=params(20),
        cost_estimate=cost(2 * slots * 3 * inner * width),
        name="spread",
    )(merged, spatial_qkv)
    shared, merged = lax.optimization_barrier((blocks, merged))
    token_keep, token_give = pl.pallas_call(
        functools.partial(share_kernel, n_pair),
        out_shape=[struct(n_pair, places, width)] * 2,
        in_specs=[VMEM],
        out_specs=[VMEM] * 2,
        compiler_params=params(6),
        name="share",
    )(shared)
    queries = list(queries)
    queries.append(far)
    held = swaps(queries, "space", n_space)
    tokens = exchange(token_keep, token_give, n_frames)
    far_keys, far_others, chosen = pl.pallas_call(
        functools.partial(prepare_kernel, wide),
        out_shape=[struct(slots, wide), struct(2 * wide, slots), jax.ShapeDtypeStruct((n_frames, places, slots), F32)],
        in_specs=[VMEM] * 2,
        out_specs=[VMEM] * 3,
        compiler_params=params(4),
        cost_estimate=cost(4 * slots * slots * n_space * n_space * wide),
        name="prepare",
    )(held[-1], merge_slot)
    held = lax.optimization_barrier([far_keys, far_others] + held[-2::-1])
    returned = packed_rows(wide, slots)
    moved = packed_rows(places, inner)
    *results, own_queries, all_keys, all_vals = pl.pallas_call(
        functools.partial(others_kernel, n_space, slots, wide),
        out_shape=[struct(returned, LANES)] * (n_space - 1)
        + [struct(wide, slots), struct(n_space * slots, wide), struct(wide, n_space * slots)],
        in_specs=[VMEM] * (n_space + 1),
        out_specs=[VMEM] * (n_space + 2),
        compiler_params=params(12),
        cost_estimate=cost(4 * slots * slots * n_space * (n_space - 1) * wide),
        name="attend_others",
    )(*held)
    own_queries, tokens = lax.optimization_barrier((own_queries, tokens))
    own = pl.pallas_call(
        own_kernel,
        out_shape=struct(wide, slots),
        in_specs=[VMEM] * 3,
        out_specs=VMEM,
        compiler_params=params(8),
        cost_estimate=cost(4 * slots * slots * n_space * wide),
        name="attend_own",
    )(own_queries, all_keys, all_vals)
    mine = swaps([own] + results, "space", n_space)
    apart = [struct(n_pair - 1, moved, LANES)] * 2 + [struct(moved, LANES)] * 2
    *blocks_apart, attended = pl.pallas_call(
        functools.partial(expand_kernel, n_space, n_pair, slots, wide),
        out_shape=apart + [struct(inner, slots)],
        in_specs=[VMEM] * (n_space + 1),
        out_specs=[VMEM] * 5,
        scratch_shapes=[pltpu.VMEM((n_space, wide, slots), F32)],
        compiler_params=params(8),
        name="expand",
    )(chosen, *reversed(mine))
    attended_parts = exchange_apart(*blocks_apart, n_frames)
    after = pl.pallas_call(
        residual_kernel,
        out_shape=struct(n_frames, places, width),
        in_specs=[VMEM] * 5,
        out_specs=VMEM,
        compiler_params=params(10),
        cost_estimate=cost(4 * slots * inner * width),
        name="residual",
    )(attended, chosen, blocks, modulation, spatial_proj)
    pad = -(-places // SUB) * SUB
    order = [0] + list(range(n_pair - 1, 0, -1))
    steps = [order[:1], order[1:2]] if n_pair > 2 else [order[:1]]
    last = order[len(steps) :]
    before = []
    for i, step in enumerate(steps):
        if before:
            s = step[-1]
            attended_parts[s], before = lax.optimization_barrier((attended_parts[s], before))
        before += [
            pl.pallas_call(
                functools.partial(project_kernel, places, len(step)),
                out_shape=struct(2 * len(step), pad, 3 * inner),
                in_specs=[VMEM] * (3 + len(step) + sum(len(attended_parts[s]) for s in step)),
                out_specs=VMEM,
                scratch_shapes=[pltpu.VMEM((2 * len(step) * places, width), F32)],
                compiler_params=params(10),
                cost_estimate=cost((1 + 9 * i) * 2 * 2 * places * len(step) * 3 * inner * width),
                name="project_%d" % i,
            )(
                modulation,
                spatial_proj,
                temporal_qkv,
                *[tokens[s] for s in step],
                *[part for s in step for part in attended_parts[s]],
            )
        ]
    mixed = pl.pallas_call(
        functools.partial(temporal_kernel, n_pair, places, len(last), order),
        out_shape=apart,
        in_specs=[VMEM] * (3 + len(last) + n_pair),
        out_specs=[VMEM] * 4,
        scratch_shapes=[pltpu.VMEM((2 * len(last) * places, width), F32)],
        compiler_params=params(16),
        name="temporal",
    )(
        modulation,
        spatial_proj,
        temporal_qkv,
        *[tokens[s] for s in last],
        *[part for s in last for part in attended_parts[s]],
        *before,
    )
    parts = exchange_apart(*mixed, n_frames)
    out = None
    for i, step in enumerate(([0, n_pair - 1], list(range(n_pair - 2, 0, -1)))):
        if step:
            given = [part for s in step for part in parts[s]]
            out = pl.pallas_call(
                functools.partial(finish_kernel, step, places, len(given)),
                out_shape=struct(n_frames, places, width),
                in_specs=[VMEM] * (3 + len(given)) + ([HBM] if i else []),
                out_specs=HBM,
                scratch_shapes=[
                    pltpu.VMEM((2 * len(step), places, width), BF16),
                    pltpu.SemaphoreType.DMA((2 * len(step),)),
                ],
                input_output_aliases={3 + len(given): 0} if i else {},
                compiler_params=params(10),
                cost_estimate=cost((1 + 29 * (1 - i)) * 2 * 2 * places * len(step) * inner * width),
                name="finish_%d" % i,
            )(modulation, temporal_proj, after, *given, *([out] if i else []))
    return out.reshape(1, rows, width)


def plain_modulate(values, modulation, which):
    normed = layer_norm(values.astype(F32))
    return (normed * (1.0 + modulation[which + 1]) + modulation[which]).astype(BF16)


def plain_shards(latents, merge_slot, modulation, spatial_qkv, spatial_proj, temporal_qkv, temporal_proj):
    row_count = latents.shape[1]
    slot_count = row_count // 2
    width = latents.shape[2]
    inner = spatial_proj.shape[0]
    root_size = math.sqrt(HD)
    own_rows = latents[0]
    normed = plain_modulate(own_rows, modulation, 0)
    local_slot = merge_slot[0] - lax.axis_index("space") * slot_count
    one_hot = (local_slot[:, None] == jnp.arange(slot_count, dtype=jnp.int32)[None, :]).astype(
        jnp.bfloat16
    )
    counts = jnp.sum(one_hot.astype(jnp.float32), 0)
    summed = lax.dot_general(
        one_hot, normed, (((0,), (0,)), ((), ())), preferred_element_type=jnp.float32
    )
    merged = (summed / counts[:, None]).astype(jnp.bfloat16)
    projected = jnp.dot(merged, spatial_qkv, preferred_element_type=jnp.float32).astype(
        jnp.bfloat16
    )
    query_rows = projected[:, :inner]
    key_rows = projected[:, inner : 2 * inner]
    value_rows = projected[:, 2 * inner :]
    head_query, head_key, head_value = (
        lax.all_to_all(query_rows, "space", split_axis=1, concat_axis=0, tiled=True),
        lax.all_to_all(key_rows, "space", split_axis=1, concat_axis=0, tiled=True),
        lax.all_to_all(value_rows, "space", split_axis=1, concat_axis=0, tiled=True),
    )
    local_heads = head_query.shape[1] // HD
    all_slots = head_query.shape[0]
    scores = (
        jnp.einsum(
            "qhd,khd->hqk",
            head_query.reshape(all_slots, local_heads, HD),
            head_key.reshape(all_slots, local_heads, HD),
            preferred_element_type=jnp.float32,
        )
        / root_size
    )
    weights = jnp.exp(scores - jnp.max(scores, -1, keepdims=True))
    row_total = jnp.sum(weights, -1)
    mixture = jnp.einsum(
        "hqk,khd->qhd",
        weights.astype(jnp.bfloat16),
        head_value.reshape(all_slots, local_heads, HD),
        preferred_element_type=jnp.float32,
    )
    head_result = (
        (mixture / row_total.T[..., None]).astype(jnp.bfloat16).reshape(all_slots, local_heads * HD)
    )
    attended = lax.all_to_all(head_result, "space", split_axis=0, concat_axis=1, tiled=True)
    spatial_out = jnp.dot(attended, spatial_proj, preferred_element_type=jnp.float32).astype(
        jnp.bfloat16
    )
    spread_back = jnp.dot(one_hot, spatial_out, preferred_element_type=jnp.float32)
    after_spatial = (own_rows.astype(jnp.float32) + modulation[2] * spread_back).astype(
        jnp.bfloat16
    )
    by_place = lax.all_to_all(
        after_spatial[None], "frames", split_axis=1, concat_axis=0, tiled=True
    )
    frame_count = by_place.shape[0]
    place_count = by_place.shape[1]
    flat = by_place.reshape(frame_count * place_count, width)
    normed_time = plain_modulate(flat, modulation, 3)
    projected_time = jnp.dot(normed_time, temporal_qkv, preferred_element_type=jnp.float32).astype(
        jnp.bfloat16
    )
    split = projected_time.reshape(frame_count, place_count, 3, inner // HD, HD)
    scores_time = (
        jnp.einsum(
            "flhd,glhd->lhfg", split[:, :, 0], split[:, :, 1], preferred_element_type=jnp.float32
        )
        / root_size
    )
    weights_time = jnp.exp(scores_time - jnp.max(scores_time, -1, keepdims=True))
    total_time = jnp.sum(weights_time, -1)
    mixture_time = (
        jnp.einsum(
            "lhfg,glhd->flhd",
            weights_time.astype(jnp.bfloat16),
            split[:, :, 2],
            preferred_element_type=jnp.float32,
        )
        / total_time.transpose(2, 0, 1)[..., None]
    )
    attended_time = mixture_time.astype(jnp.bfloat16).reshape(frame_count * place_count, inner)
    branch = jnp.dot(attended_time, temporal_proj, preferred_element_type=jnp.float32)
    finished = (
        (flat.astype(jnp.float32) + modulation[5] * branch)
        .astype(jnp.bfloat16)
        .reshape(frame_count, place_count, width)
    )
    return lax.all_to_all(finished, "frames", split_axis=0, concat_axis=1, tiled=True)


def solution(mesh):
    n_frames, n_space = mesh.shape["frames"], mesh.shape["space"]
    placed = (P("frames", "space", None), P("frames", "space"), P(), P(), P(), P(), P())

    def local(latents, *rest):
        fits = n_frames >= 8 and latents.shape[1] % (8 * n_frames) == 0 and n_frames & (n_frames - 1) == 0 and n_space & (n_space - 1) == 0
        body = functools.partial(shards, n_frames, n_space) if fits else plain_shards
        return body(latents, *rest)

    return jax.shard_map(local, mesh=mesh, in_specs=placed, out_specs=P("frames", "space", None), check_vma=False)
```
